32 devices in a mesh: dp: 2 (over x), ctx: 4 (over z), head: 4 (over y, core).
Axes of the slice: x: 2, y: 2, z: 4, core: 2. Of those that a mesh axis runs over, the one named last changes fastest.
Arguments:
- hidden_in: bfloat16 [4096, 512], P(('dp', 'ctx', 'head')), may hold values from -8 to 8, as said below
- lengths: int32 [2, 4], P('dp'), may hold values from 1 to 1537, 2048 in all within a row
- attn_gain: float32 [2, 512], replicated, may hold values from 0.5 to 1.5
- attn_shift: float32 [2, 512], replicated, may hold values from -3 to 3
- mlp_gain: float32 [2, 512], replicated, may hold values from 0.5 to 1.5
- mlp_shift: float32 [2, 512], replicated, may hold values from -3 to 3
- qkv_weight: bfloat16 [2, 512, 1536], replicated, may hold values from -0.25 to 0.25
- qkv_bias: float32 [2, 1536], replicated, may hold values from -3 to 3
- out_weight: bfloat16 [2, 512, 512], replicated, may hold values from -1.5 to 1.5
- out_bias: float32 [2, 512], replicated, may hold values from -3 to 3
- up_weight: bfloat16 [2, 512, 2048], replicated, may hold values from -0.25 to 0.25
- up_bias: float32 [2, 2048], replicated, may hold values from -3 to 3
- down_weight: bfloat16 [2, 2048, 512], replicated, may hold values from -0.1875 to 0.1875
- down_bias: float32 [2, 512], replicated, may hold values from -3 to 3
- cotangent: bfloat16 [4096, 512], P(('dp', 'ctx', 'head')), may hold values from -6 to 6
Outputs:
- output_rows: bfloat16 [4096, 512], P(('dp', 'ctx', 'head'))
- input_grad: float32 [4096, 512], P(('dp', 'ctx', 'head'))
- attn_gain_grad: float32 [2, 512], P(None, 'head')
- attn_shift_grad: float32 [2, 512], P(None, 'head')
- mlp_gain_grad: float32 [2, 512], P(None, 'head')
- mlp_shift_grad: float32 [2, 512], P(None, 'head')
- qkv_weight_grad: float32 [2, 512, 1536], P(None, None, 'head')
- qkv_bias_grad: float32 [2, 1536], P(None, 'head')
- out_weight_grad: float32 [2, 512, 512], P(None, None, 'head')
- out_bias_grad: float32 [2, 512], P(None, 'head')
- up_weight_grad: float32 [2, 512, 2048], P(None, None, 'head')
- up_bias_grad: float32 [2, 2048], P(None, 'head')
- down_weight_grad: float32 [2, 2048, 512], P(None, None, 'head')
- down_bias_grad: float32 [2, 512], P(None, 'head')
- layer_stats: float32 [2, 3], replicated
The draws below stay inside these ranges and needn't reach their ends.
Inputs may be any that keep to these rules, and one draw needn't show every extreme that they name: Each row lists the lengths of one group's sequences in order; they add up to 2048. `hidden_in`: activations of order one.
All inputs are finite; a program needn't handle non-finite values.
Results may differ from the reference program's by a relative error of at most 0.013.
Values may be sent and summed in bfloat16 or wider, within the bound.
No kernel may reach another device: no remote copies, remote signals or barrier semaphores. Data moves between devices by JAX's collectives and lax.ppermute only.
A program may use at most 128 MiB of HBM per device.

```python
import math
import jax
import jax.numpy as jnp
import numpy as np
from jax import lax

D = 512
FF = 2048
NH = 8
HD = 64
ROT = 16
LAYERS = 2
SEQS = 4
GROUP = 2048
TOKENS = 4096
LONGEST = 1537
N_DP = 2


def draw_hidden_in(key, part):
    key = jax.random.fold_in(key, 11)
    place = jnp.arange(TOKENS, dtype=jnp.float32)[:, None] / (TOKENS - 1)
    base = jax.random.truncated_normal(key, -4.0, 4.0, (TOKENS, D), jnp.float32)
    scale = 0.6 * jnp.exp(jnp.log(3.0) * place)
    return (base * scale).astype(jnp.bfloat16)


def block_scale(own_key, shape, cuts, smallest, largest):
    level, own = 1.0, jax.random.fold_in(own_key, 6)
    for position, blocks in cuts:
        draws = jnp.exp(jax.random.uniform(jax.random.fold_in(own, position), (blocks,), jnp.float32, smallest / len(cuts), largest / len(cuts)))
        level = level * jnp.repeat(draws, shape[position] // blocks).reshape([-1 if axis == position else 1 for axis in range(len(shape))])
    return level


def split_up(number_of, total, bound, slope):
    portions = [(1 << 20) // math.isqrt(grade ** slope) + 1 for grade in range(2, number_of + 1)]
    surplus, holding = total - bound - (number_of - 1), [1] * (number_of - 1)
    while surplus > 0:
        candidates = [i for i in range(number_of - 1) if holding[i] < bound]
        pool, budget = sum([portions[i] for i in candidates]), surplus
        for i in candidates:
            addition = min(bound - holding[i], max(1, budget * portions[i] // pool), surplus)
            holding[i] = holding[i] + addition
            surplus = surplus - addition
    return np.array([bound] + holding)


def uneven(own_key, number_of, total, limit, lean):
    if number_of == 2:
        one = jax.random.randint(own_key, (), max(1, total - limit), min(limit, total - 1) + 1)
        return jnp.stack([one, total - one])
    sizes = jnp.asarray(split_up(number_of, total, limit, lean), jnp.int32)
    couples = (number_of - 1) // 2
    giver, sink = sizes[1:1 + 2 * couples:2], sizes[2:2 + 2 * couples:2]
    room = jnp.minimum(giver - 1, limit - sink)
    moved = jax.random.randint(jax.random.fold_in(own_key, 1), (couples,), 0, 1 << 20) % (room + 1)
    sizes = sizes.at[1:1 + 2 * couples:2].set(giver - moved).at[2:2 + 2 * couples:2].set(sink + moved)
    return sizes[jax.random.permutation(jax.random.fold_in(own_key, 2), number_of)]


def bell_draw(own_key, shape, spread, reach, shards=(), kind=jnp.bfloat16):
    result = spread * jax.random.normal(own_key, shape, jnp.float32)
    if shards:
        result = result * block_scale(own_key, shape, shards, -0.22, 0.18)
    return jnp.clip(result, -reach, reach).astype(kind)


def setup_inputs(seed: int = 0) -> dict:
    arg_keys = jax.random.split(jax.random.key(seed), 16)
    hidden_in = draw_hidden_in(jax.random.fold_in(arg_keys[15], 71), 0)
    lengths = jax.vmap(lambda own: uneven(own, SEQS, GROUP, LONGEST, 2))(jax.random.split(arg_keys[1], N_DP)).reshape((N_DP, SEQS)).astype(jnp.int32)
    attn_gain = jnp.clip(1.0 + 0.1 * jax.random.normal(arg_keys[2], (LAYERS, D), jnp.float32), 0.5, 1.5)
    attn_shift = bell_draw(arg_keys[3], (LAYERS, D), 0.2, 3.0, (), jnp.float32)
    mlp_gain = jnp.clip(1.0 + 0.1 * jax.random.normal(arg_keys[4], (LAYERS, D), jnp.float32), 0.5, 1.5)
    mlp_shift = bell_draw(arg_keys[5], (LAYERS, D), 0.2, 3.0, (), jnp.float32)
    qkv_weight = bell_draw(arg_keys[6], (LAYERS, D, 3 * D), D ** -0.5, 0.25)
    qkv_bias = bell_draw(arg_keys[7], (LAYERS, 3 * D), 0.2, 3.0, (), jnp.float32)
    out_weight = bell_draw(arg_keys[8], (LAYERS, D, D), (D // 32) ** -0.5, 1.5)
    out_bias = bell_draw(arg_keys[9], (LAYERS, D), 0.2, 3.0, (), jnp.float32)
    up_weight = bell_draw(arg_keys[10], (LAYERS, D, FF), D ** -0.5, 0.25)
    up_bias = bell_draw(arg_keys[11], (LAYERS, FF), 0.2, 3.0, (), jnp.float32)
    down_weight = bell_draw(arg_keys[12], (LAYERS, FF, D), (FF // 2) ** -0.5, 0.1875)
    down_bias = bell_draw(arg_keys[13], (LAYERS, D), 0.2, 3.0, (), jnp.float32)
    cotangent = bell_draw(arg_keys[14], (TOKENS, D), 1.0, 6.0, ((0, 32),))
    return {"hidden_in": hidden_in, "lengths": lengths, "attn_gain": attn_gain, "attn_shift": attn_shift, "mlp_gain": mlp_gain, "mlp_shift": mlp_shift, "qkv_weight": qkv_weight, "qkv_bias": qkv_bias, "out_weight": out_weight, "out_bias": out_bias, "up_weight": up_weight, "up_bias": up_bias, "down_weight": down_weight, "down_bias": down_bias, "cotangent": cotangent}


epsilon = 1e-05
masked_value = -1e+30
score_scale = 0.125
rope_base = 10000.0

@jax.custom_vjp
def low(v):
    return lax.optimization_barrier(v.astype(jnp.bfloat16)).astype(jnp.float32)

@jax.custom_vjp
def low_back(v):
    return v

def low_keep(v):
    return (low(v), None)

def low_pass(kept, grad):
    return (grad,)

def back_keep(v):
    return (v, None)

def back_low(kept, grad):
    return (low(grad),)
low.defvjp(low_keep, low_pass)
low_back.defvjp(back_keep, back_low)

def matmul_hi(left, right):
    return jnp.dot(left, right, preferred_element_type=jnp.float32, precision=lax.Precision.HIGHEST)

def norm_parts(hidden):
    centred = hidden - lax.optimization_barrier(jnp.mean(hidden, axis=-1, keepdims=True))
    inverse = lax.rsqrt(lax.optimization_barrier(jnp.mean(centred * centred, axis=-1, keepdims=True)) + epsilon)
    return centred * inverse

def doc_starts(lengths_row, places):
    ends = jnp.cumsum(lengths_row).astype(jnp.int32)
    before = ends[None, :] <= places[:, None]
    return lax.optimization_barrier(jnp.sum(jnp.where(before, lengths_row[None, :], 0), axis=1)).astype(jnp.int32)

def rotate(vectors, places, starts, direction):
    half_rot = ROT // 2
    inverse_freq = rope_base ** (-2.0 * jnp.arange(half_rot, dtype=jnp.float32) / ROT)
    angles = (places - starts).astype(jnp.float32)[:, None] * inverse_freq[None, :]
    cosine = jnp.cos(angles)[:, None, :]
    sine_of = direction * jnp.sin(angles)[:, None, :]
    front = vectors[..., :half_rot]
    behind = vectors[..., half_rot:ROT]
    return jnp.concatenate([front * cosine - behind * sine_of, behind * cosine + front * sine_of, vectors[..., ROT:]], axis=-1)

def attend_block(queries, keys, values, query_places, query_starts, key_places, key_starts):
    raw_scores = jnp.einsum('qhd,khd->hqk', queries, keys, precision=lax.Precision.HIGHEST) * score_scale
    scores = low_back(raw_scores)
    allowed = (key_places[None, :] <= query_places[:, None]) & (key_starts[None, :] == query_starts[:, None])
    masked = jnp.where(allowed[None], scores, masked_value)
    row_max = lax.optimization_barrier(jnp.max(masked, axis=-1, keepdims=True))
    exponent = jnp.where(allowed[None], jnp.exp(masked - row_max), 0.0)
    chances = exponent / lax.optimization_barrier(jnp.sum(exponent, axis=-1, keepdims=True))
    return jnp.einsum('hqk,khd->qhd', low(chances), values, precision=lax.Precision.HIGHEST)

def group_attention(packed, lengths_row):
    places = jnp.arange(GROUP, dtype=jnp.int32)
    starts = doc_starts(lengths_row, places)
    queries = low_back(low(rotate(packed[:, :, 0], places, starts, 1.0)))
    keys = low_back(low(rotate(packed[:, :, 1], places, starts, 1.0)))
    values = low_back(low(packed[:, :, 2]))
    block_size = math.gcd(GROUP, 512)
    block_count = GROUP // block_size

    def one_block(element):
        return attend_block(element[0], keys, values, element[1], element[2], places, starts)
    mixed = lax.map(jax.checkpoint(one_block), (queries.reshape(block_count, block_size, NH, HD), places.reshape(block_count, block_size), starts.reshape(block_count, block_size)))
    return mixed.reshape(GROUP, NH, HD)

def forward(hidden, attn_gain, attn_shift, mlp_gain, mlp_shift, qkv_weight, qkv_bias, out_weight, out_bias, up_weight, up_bias, down_weight, down_bias, lengths):
    stat_list = []
    for layer_idx in range(LAYERS):
        normal = norm_parts(hidden)
        attn_in = low(normal * attn_gain[layer_idx] + attn_shift[layer_idx])
        mlp_in = low(normal * mlp_gain[layer_idx] + mlp_shift[layer_idx])
        packed = low_back(matmul_hi(attn_in, qkv_weight[layer_idx]) + qkv_bias[layer_idx])
        packed = packed.reshape(N_DP, GROUP, NH, 3, HD)
        mixed = lax.map(lambda element: group_attention(element[0], element[1]), (packed, lengths))
        mixed = low_back(low(mixed.reshape(TOKENS, D)))
        attn_out = low_back(matmul_hi(mixed, out_weight[layer_idx]) + out_bias[layer_idx])
        gate = low_back(matmul_hi(mlp_in, up_weight[layer_idx]) + up_bias[layer_idx])
        acted = low(jax.nn.gelu(gate, approximate=False))
        mlp_out = low_back(matmul_hi(acted, down_weight[layer_idx]) + down_bias[layer_idx])
        stat_list.append(jnp.stack([jnp.sqrt(jnp.mean(hidden * hidden)), jnp.sqrt(jnp.mean(attn_out * attn_out)), jnp.sqrt(jnp.mean(mlp_out * mlp_out))]))
        hidden = hidden + attn_out + mlp_out
    return (hidden, jnp.stack(stat_list))

def reference(hidden_in, lengths, attn_gain, attn_shift, mlp_gain, mlp_shift, qkv_weight, qkv_bias, out_weight, out_bias, up_weight, up_bias, down_weight, down_bias, cotangent):
    params = [p.astype(jnp.float32) for p in (attn_gain, attn_shift, mlp_gain, mlp_shift, qkv_weight, qkv_bias, out_weight, out_bias, up_weight, up_bias, down_weight, down_bias)]

    def run(hidden, *weights):
        return forward(hidden, *weights, lengths)
    output, pull, stats = jax.vjp(run, hidden_in.astype(jnp.float32), *params, has_aux=True)
    grads = pull(cotangent.astype(jnp.float32))
    return (output.astype(jnp.bfloat16), grads[0], grads[1], grads[2], grads[3], grads[4], grads[5], grads[6], grads[7], grads[8], grads[9], grads[10], grads[11], grads[12], stats)
```

```python
import functools
import math

import jax
import jax.numpy as jnp
from jax import lax
from jax.experimental import pallas as pl
from jax.experimental.pallas import tpu as pltpu
from jax.sharding import PartitionSpec as P

D = 512
FF = 2048
NH = 8
HD = 64
ROT = 16
LAYERS = 2
PAIRS = NH // 2
epsilon = 1e-05
masked_value = -1e30
score_scale = 0.125
rope_base = 10000.0
f32 = jnp.float32
bf16 = jnp.bfloat16
STEP = 256
VMEM = pltpu.VMEM


def dot(a, b):
    return lax.dot_general(a, b, (((1,), (0,)), ((), ())), preferred_element_type=f32)


def dot_nt(a, b):
    return lax.dot_general(a, b, (((1,), (1,)), ((), ())), preferred_element_type=f32)


def norm_parts(hidden):
    centred = hidden - jnp.mean(hidden, axis=-1, keepdims=True)
    inverse = lax.rsqrt(jnp.mean(centred * centred, axis=-1, keepdims=True) + epsilon)
    return centred * inverse, inverse


def rope(x, cos_t, left_t, right_t):
    return x * cos_t + pltpu.roll(x, 128 - 8, 1) * left_t + pltpu.roll(x, 8, 1) * right_t


def start_of(place, ends):
    start = jnp.zeros_like(place)
    for end in ends:
        start = jnp.where(end <= place, end, start)
    return start


def end_of(place, ends, size):
    found = jnp.int32(size)
    for end in reversed(ends):
        found = jnp.where(place < end, end, found)
    return found


def split_low(x):
    high = x.astype(bf16)
    return high, (x - high.astype(f32)).astype(bf16)


def lane_of(rows):
    return lax.broadcasted_iota(jnp.int32, (rows, 128), 1)


def two_heads(x):
    first = lane_of(x.shape[0]) < HD
    zero = jnp.zeros_like(x)
    return jnp.concatenate([jnp.where(first, x, zero), jnp.where(first, zero, x)], axis=0)


def one_pair(x):
    rows = x.shape[0] // 2
    return jnp.where(lane_of(rows) < HD, x[:rows], x[rows:])


def head_rows(cols, rows):
    lane = lane_of(rows)
    out = jnp.zeros((rows, 128), f32)
    for n in range(NH):
        out = jnp.where(lane == n, cols[n], out)
    return out


def call(kernel, ins, outs, scratch=(), scalars=None, vmem=48 << 20, flops=10**9):
    specs, arrays = [], []
    if scalars is not None:
        specs.append(pl.BlockSpec(memory_space=pltpu.SMEM))
        arrays.append(scalars)
    for item in ins:
        if isinstance(item, tuple):
            array, layer = item
            shape = (None, *array.shape[1:])
            place = (layer, *([0] * (array.ndim - 1)))
            specs.append(pl.BlockSpec(shape, lambda i, place=place: place))
            arrays.append(array)
        else:
            specs.append(pl.BlockSpec(item.shape, lambda i, n=item.ndim: (0,) * n))
            arrays.append(item)
    out_specs = [pl.BlockSpec(o.shape, lambda i, n=len(o.shape): (0,) * n) for o in outs]
    moved = sum(a.size * a.dtype.itemsize for a in arrays)
    return pl.pallas_call(
        kernel,
        grid=(1,),
        in_specs=specs,
        out_specs=out_specs,
        out_shape=outs,
        scratch_shapes=list(scratch),
        compiler_params=pltpu.CompilerParams(vmem_limit_bytes=vmem),
        cost_estimate=pl.CostEstimate(flops=flops, bytes_accessed=moved, transcendentals=0),
    )(*arrays)


def sds(shape, dtype):
    return jax.ShapeDtypeStruct(shape, dtype)


def mlp_forward(hidden, params, layer):
    rows = hidden.shape[0]

    def kernel(h_ref, gain, shift, up, up_b, down, down_b, out_ref, factor_ref, normal_ref):
        normal, _ = norm_parts(h_ref[...].astype(f32))
        normal_ref[...] = normal.astype(bf16)
        x = (normal * gain[layer : layer + 1] + shift[layer : layer + 1]).astype(bf16)
        total = jnp.zeros((rows, D), f32)
        for j in range(0, FF, 512):
            gate = dot(x, up[:, j : j + 512]) + up_b[layer : layer + 1, j : j + 512]
            cdf = 0.5 * (1.0 + lax.erf(gate * math.sqrt(0.5)))
            pdf = jnp.exp(-0.5 * gate * gate) * (1.0 / math.sqrt(2.0 * math.pi))
            factor_ref[:, j : j + 512] = cdf + gate * pdf
            total += dot((gate * cdf).astype(bf16), down[j : j + 512])
        out_ref[...] = total + down_b[layer : layer + 1]

    return call(
        kernel,
        [
            hidden,
            params["mlp_gain"],
            params["mlp_shift"],
            (params["up_weight"], layer),
            params["up_bias"],
            (params["down_weight"], layer),
            params["down_bias"],
        ],
        [sds((rows, D), f32), sds((rows, FF), f32), sds((rows, D), bf16)],
        flops=2 * 2 * rows * D * FF,
    )


class Place:
    def __init__(self, n_ctx, n_head, rows):
        self.n_ctx, self.n_head, self.rows = n_ctx, n_head, rows
        self.blocks = n_ctx * n_head
        self.group = self.blocks * rows

    def position(self, scal, slot):
        shift, flip = slot // self.n_head, slot % self.n_head
        ctx = lax.rem(scal[0] - shift + self.n_ctx, self.n_ctx)
        return ctx * self.n_head + (scal[1] ^ flip)

    def ends(self, scal):
        return [scal[3 + k] for k in range(4)]


def delta_columns(grad_mixed, mixed):
    cols = []
    for p in range(PAIRS):
        prod = grad_mixed[:, 128 * p : 128 * p + 128].astype(f32) * mixed[:, 128 * p : 128 * p + 128]
        first = lane_of(prod.shape[0]) < HD
        cols.append(jnp.sum(jnp.where(first, prod, 0.0), axis=1, keepdims=True))
        cols.append(jnp.sum(jnp.where(first, 0.0, prod), axis=1, keepdims=True))
    return head_rows(cols, grad_mixed.shape[0])


def stat_payload(log_cols, delta_cols):
    logs, deltas = log_cols.T[:NH], delta_cols.T[:NH]
    parts = [*split_low(logs), *split_low(deltas)]
    top = jnp.concatenate(parts, axis=1)
    return jnp.concatenate([top, jnp.zeros_like(top)], axis=0)


def attention_forward(place, scalars, blocks, tables, params, layer, hidden, mlp_out, last_grad):
    rows, group = place.rows, place.group
    first_layer = layer == 0
    last = last_grad is not None
    tile = min(512, group)

    def kernel(scal, *refs):
        refs = list(refs)
        xs = [refs.pop(0) for _ in range(place.blocks)]
        cos_t, left_t, right_t, gain, shift, w, b, out_w, out_b, h_ref, mlp_ref = refs[:11]
        refs = refs[11:]
        g_ref = refs.pop(0) if last else None
        (normal_all, k_all, v_all, q_own, mixed_ref, mixed_low_ref, log_ref, delta_ref, dmix_ref, h_out, stats_ref, low_ref) = refs[:12]
        a_all = refs[12]
        own_at = pl.multiple_of(scal[2] * rows, rows)
        ends = place.ends(scal)
        gain_l, shift_l = gain[layer : layer + 1], shift[layer : layer + 1]
        for slot in range(place.blocks):
            at = pl.multiple_of(place.position(scal, slot) * rows, rows)
            x = xs[slot][...].astype(f32)
            normal = norm_parts(x)[0] if first_layer else x
            normal_all[pl.ds(at, rows)] = normal.astype(bf16)
            a_all[pl.ds(at, rows)] = (normal * gain_l + shift_l).astype(bf16)

        def project(i, _):
            at = pl.multiple_of(i * tile, tile)
            k = dot(a_all[pl.ds(at, tile)], w[:, D : 2 * D]) + b[layer : layer + 1, D : 2 * D]
            tabs = [t[pl.ds(at, tile)] for t in (cos_t, left_t, right_t)]
            for p in range(PAIRS):
                k_all[pl.ds(at, tile), 128 * p : 128 * p + 128] = rope(k[:, 128 * p : 128 * p + 128], *tabs).astype(bf16)
            v = dot(a_all[pl.ds(at, tile)], w[:, 2 * D :]) + b[layer : layer + 1, 2 * D :]
            v_all[pl.ds(at, tile)] = v.astype(bf16)
            return 0

        lax.fori_loop(0, group // tile, project, 0)
        q = dot(a_all[pl.ds(own_at, rows)], w[:, :D]) + b[layer : layer + 1, :D]
        tabs = [t[pl.ds(own_at, rows)] for t in (cos_t, left_t, right_t)]
        for p in range(PAIRS):
            turned = rope(q[:, 128 * p : 128 * p + 128], *tabs).astype(bf16)
            q_own[:, 128 * p : 128 * p + 128] = turned * jnp.asarray(score_scale, bf16)
        t = own_at + lax.broadcasted_iota(jnp.int32, (rows, 1), 0)
        start = start_of(t, ends)
        low = start_of(own_at, ends) // STEP
        high = (own_at + rows - 1) // STEP + 1
        cols = []
        doubled = [two_heads(q_own[:, 128 * p : 128 * p + 128]) for p in range(PAIRS)]

        def attend(i, carry):
            at = pl.multiple_of(i * STEP, STEP)
            s_at = at + lax.broadcasted_iota(jnp.int32, (1, STEP), 1)
            bias = jnp.where((s_at >= start) & (s_at <= t), 0.0, masked_value)
            bias = jnp.concatenate([bias, bias], axis=0)
            new = []
            for p in range(PAIRS):
                most, total, acc = carry[p]
                scores = dot_nt(doubled[p], k_all[pl.ds(at, STEP), 128 * p : 128 * p + 128]) + bias
                newest = jnp.maximum(most, jnp.max(scores, axis=1, keepdims=True))
                chance = jnp.exp(scores - newest)
                scale = jnp.exp(most - newest)
                total = total * scale + jnp.sum(chance, axis=1, keepdims=True)
                acc = acc * scale + dot(chance.astype(bf16), v_all[pl.ds(at, STEP), 128 * p : 128 * p + 128])
                new.append((newest, total, acc))
            return tuple(new)

        begin = tuple(
            (jnp.full((2 * rows, 1), masked_value, f32), jnp.zeros((2 * rows, 1), f32), jnp.zeros((2 * rows, 128), f32))
            for _ in range(PAIRS)
        )
        done = lax.fori_loop(low, high, attend, begin)
        for p in range(PAIRS):
            most, total, acc = done[p]
            mixed_ref[:, 128 * p : 128 * p + 128] = one_pair(acc / total)
            log = most + jnp.log(total)
            cols += [log[:rows], log[rows:]]
        log_cols = head_rows(cols, rows)
        log_ref[...] = log_cols
        mixed = mixed_ref[...]
        mixed_low = mixed.astype(bf16)
        mixed_low_ref[...] = mixed_low
        attn_out = dot(mixed_low, out_w[...]) + out_b[layer : layer + 1]
        h = h_ref[...].astype(f32)
        mlp = mlp_ref[...]
        result = h + attn_out + mlp
        lane = lane_of(8)
        sums = [jnp.sum(jnp.sum(v * v, axis=1, keepdims=True), axis=0, keepdims=True) for v in (h, attn_out, mlp)]
        stats_ref[...] = jnp.where(lane == 0, sums[0], jnp.where(lane == 1, sums[1], jnp.where(lane == 2, sums[2], 0.0)))
        if last:
            h_out[...] = result.astype(bf16)
            dmix = dot_nt(g_ref[...], out_w[...]).astype(bf16)
            dmix_ref[...] = dmix
            deltas = delta_columns(dmix, mixed)
            delta_ref[...] = deltas
            low_ref[...] = stat_payload(log_cols, deltas)
        else:
            h_out[...] = result
            low_ref[...] = norm_parts(result)[0].astype(bf16)
            dmix_ref[...] = jnp.zeros_like(dmix_ref)
            delta_ref[...] = jnp.zeros_like(delta_ref)

    ins = [
        *blocks,
        *tables,
        params["attn_gain"],
        params["attn_shift"],
        (params["qkv_sorted"], layer),
        params["qkv_bias_sorted"],
        (params["out_weight"], layer),
        params["out_bias"],
        hidden,
        mlp_out,
    ]
    if last:
        ins.append(last_grad)
    outs = [
        sds((group, D), bf16),
        sds((group, D), bf16),
        sds((group, D), bf16),
        sds((rows, D), bf16),
        sds((rows, D), f32),
        sds((rows, D), bf16),
        sds((rows, 128), f32),
        sds((rows, 128), f32),
        sds((rows, D), bf16),
        sds((rows, D), bf16 if last else f32),
        sds((8, 128), f32),
        sds((16, D) if last else (rows, D), bf16),
    ]
    return call(kernel, ins, outs, [VMEM((group, D), bf16)], scalars, flops=8 * 10**9)


def mlp_backward(grad, factor, hidden, params, layer):
    rows = grad.shape[0]

    def kernel(g_ref, factor_ref, down, up, out_ref):
        g_low = g_ref[...].astype(bf16)
        total = jnp.zeros((rows, D), f32)
        for j in range(0, FF, 512):
            grad_gate = (dot_nt(g_low, down[j : j + 512]) * factor_ref[:, j : j + 512]).astype(bf16)
            total += dot_nt(grad_gate, up[:, j : j + 512])
        out_ref[...] = total

    return call(
        kernel,
        [grad, factor, (params["down_weight"], layer), (params["up_weight"], layer)],
        [sds((rows, D), f32)],
        flops=2 * 2 * rows * D * FF,
    )[0]


def attention_backward(place, scalars, blocks, stats, tables, params, layer, kept, grad, grad_mlp_in, mixed_below):
    rows, group = place.rows, place.group
    follows = stats is None
    below = layer > 0
    tile = min(512, group)
    per_chunk = 8 // place.n_ctx
    width = 64 * per_chunk

    def kernel(scal, *refs):
        refs = list(refs)
        gs = [refs.pop(0) for _ in range(place.blocks)]
        ss = None if follows else [refs.pop(0) for _ in range(place.blocks)]
        (cos_t, left_t, right_t, gain, shift, mlp_gain, w, b, out_w, normal_all, k_all, v_all, q_own, dmix_ref, log_ref, delta_ref, h_ref, g_ref, gmlp_ref, mixed_ref, stats_ref) = refs[:21]
        refs = refs[21:]
        if below:
            below_mixed, below_log, below_w = refs[:3]
            refs = refs[3:]
        g_all, chunks_ref, g_out, payload_ref, dmix_out, delta_out = refs[:6]
        q_all, dm_all, log_all, delta_all = refs[6:]
        own_at = pl.multiple_of(scal[2] * rows, rows)
        ends = place.ends(scal)
        gain_l, shift_l = gain[layer : layer + 1], shift[layer : layer + 1]
        for slot in range(place.blocks):
            at = pl.multiple_of(place.position(scal, slot) * rows, rows)
            g_all[pl.ds(at, rows)] = gs[slot][0:rows]
            info = (gs[slot][rows : rows + 16] if follows else ss[slot][...]).astype(f32)[:NH]
            log_all[:, pl.ds(at, rows)] = info[:, 0:128] + info[:, 128:256]
            delta_all[:, pl.ds(at, rows)] = info[:, 256:384] + info[:, 384:512]
        last_end = end_of(own_at + rows - 1, ends, group)

        def project(i, _):
            at = pl.multiple_of(i * tile, tile)
            a = (normal_all[pl.ds(at, tile)].astype(f32) * gain_l + shift_l).astype(bf16)
            q = dot(a, w[:, :D]) + b[layer : layer + 1, :D]
            tabs = [t[pl.ds(at, tile)] for t in (cos_t, left_t, right_t)]
            for p in range(PAIRS):
                turned = rope(q[:, 128 * p : 128 * p + 128], *tabs).astype(bf16)
                q_all[pl.ds(at, tile), 128 * p : 128 * p + 128] = turned * jnp.asarray(score_scale, bf16)
            dm_all[pl.ds(at, tile)] = dot_nt(g_all[pl.ds(at, tile)], out_w[...]).astype(bf16)
            return 0

        lax.fori_loop(own_at // tile, (last_end + tile - 1) // tile, project, 0)

        s_at = own_at + lax.broadcasted_iota(jnp.int32, (rows, 1), 0)
        k2 = [two_heads(k_all[pl.ds(own_at, rows), 128 * p : 128 * p + 128]) for p in range(PAIRS)]
        v2 = [two_heads(v_all[pl.ds(own_at, rows), 128 * p : 128 * p + 128]) for p in range(PAIRS)]

        def keys(i, carry):
            at = pl.multiple_of(i * STEP, STEP)
            t = at + lax.broadcasted_iota(jnp.int32, (1, STEP), 1)
            start = start_of(t, ends)
            bias = jnp.where((s_at >= start) & (s_at <= t), 0.0, masked_value)
            new = []
            for p in range(PAIRS):
                dk, dv = carry[p]
                qs = q_all[pl.ds(at, STEP), 128 * p : 128 * p + 128]
                dms = dm_all[pl.ds(at, STEP), 128 * p : 128 * p + 128]
                scores = dot_nt(k2[p], qs)
                pulled = dot_nt(v2[p], dms)
                chances, grads = [], []
                for half in range(2):
                    n = 2 * p + half
                    part = slice(half * rows, half * rows + rows)
                    chance = jnp.exp(scores[part] + bias - log_all[n : n + 1, pl.ds(at, STEP)])
                    grads.append(chance * (pulled[part] - delta_all[n : n + 1, pl.ds(at, STEP)]))
                    chances.append(chance)
                chance = jnp.concatenate(chances, axis=0).astype(bf16)
                grad_s = jnp.concatenate(grads, axis=0).astype(bf16)
                new.append((dk + dot(grad_s, qs), dv + dot(chance, dms)))
            return tuple(new)

        zero = jnp.zeros((2 * rows, 128), f32)
        done = lax.fori_loop(own_at // STEP, (last_end + STEP - 1) // STEP, keys, tuple((zero, zero) for _ in range(PAIRS)))
        grad_k = [one_pair(done[p][0]) for p in range(PAIRS)]
        grad_v = [one_pair(done[p][1]) for p in range(PAIRS)]

        t = s_at
        start = start_of(t, ends)
        q2 = [two_heads(q_own[:, 128 * p : 128 * p + 128]) for p in range(PAIRS)]
        d2 = [two_heads(dmix_ref[:, 128 * p : 128 * p + 128]) for p in range(PAIRS)]
        logs, deltas = log_ref[...], delta_ref[...]
        log2 = [jnp.concatenate([logs[:, 2 * p : 2 * p + 1], logs[:, 2 * p + 1 : 2 * p + 2]], axis=0) for p in range(PAIRS)]
        delta2 = [jnp.concatenate([deltas[:, 2 * p : 2 * p + 1], deltas[:, 2 * p + 1 : 2 * p + 2]], axis=0) for p in range(PAIRS)]

        def queries(i, carry):
            at = pl.multiple_of(i * STEP, STEP)
            s = at + lax.broadcasted_iota(jnp.int32, (1, STEP), 1)
            bias = jnp.where((s >= start) & (s <= t), 0.0, masked_value)
            bias = jnp.concatenate([bias, bias], axis=0)
            new = []
            for p in range(PAIRS):
                ks = k_all[pl.ds(at, STEP), 128 * p : 128 * p + 128]
                vs = v_all[pl.ds(at, STEP), 128 * p : 128 * p + 128]
                chance = jnp.exp(dot_nt(q2[p], ks) + bias - log2[p])
                grad_s = (chance * (dot_nt(d2[p], vs) - delta2[p])).astype(bf16)
                new.append(carry[p] + dot(grad_s, ks))
            return tuple(new)

        done = lax.fori_loop(
            start_of(own_at, ends) // STEP, (own_at + rows - 1) // STEP + 1, queries, tuple(zero for _ in range(PAIRS))
        )
        grad_q = [one_pair(done[p]) * score_scale for p in range(PAIRS)]
        tabs = [cos_t[pl.ds(own_at, rows)], -left_t[pl.ds(own_at, rows)], -right_t[pl.ds(own_at, rows)]]
        grad_q = [rope(x, *tabs).astype(bf16) for x in grad_q]
        grad_k = [rope(x, *tabs).astype(bf16) for x in grad_k]
        grad_v = [x.astype(bf16) for x in grad_v]
        grad_in = jnp.zeros((rows, D), f32)
        for j, parts in enumerate((grad_q, grad_k, grad_v)):
            grad_in += dot_nt(jnp.concatenate(parts, axis=1), w[:, j * D : j * D + D])

        normal, inverse = norm_parts(h_ref[...].astype(f32))
        grad_mlp = gmlp_ref[...]
        grad_normal = grad_in * gain_l + grad_mlp * mlp_gain[layer : layer + 1]
        back = inverse * (
            grad_normal
            - jnp.mean(grad_normal, axis=-1, keepdims=True)
            - normal * jnp.mean(grad_normal * normal, axis=-1, keepdims=True)
        )
        g_new = g_ref[...].astype(f32) + back
        g_out[...] = g_new

        sums = [
            jnp.sum(v, axis=0, keepdims=True)
            for v in (grad_in * normal, grad_in, grad_mlp * normal, grad_mlp)
        ]
        mixed = mixed_ref[...]
        first = lane_of(rows) < HD

        def row_piece(index, where):
            if index < 3 * NH:
                n, j = index // 3, index % 3
                pair, half = (grad_q, grad_k, grad_v)[j][n // 2], n % 2
            else:
                n = index - 3 * NH
                pair, half = mixed[:, 128 * (n // 2) : 128 * (n // 2) + 128], n % 2
            return pair if half == where else pltpu.roll(pair.astype(f32), HD, 1).astype(bf16)

        lane16 = lane_of(16)
        row16 = lax.broadcasted_iota(jnp.int32, (16, 128), 0)
        layer_sums = jnp.broadcast_to(stats_ref[0:1], (16, 128))
        for q in range(place.n_head):
            pieces = [6 * q + i for i in range(6)] + [3 * NH + 2 * q + i for i in range(2)]
            for c in range(place.n_ctx):
                target = c * place.n_head + q
                mine = pieces[c * per_chunk : (c + 1) * per_chunk]
                if per_chunk == 2:
                    chunk = jnp.where(first, row_piece(mine[0], 0), row_piece(mine[1], 1))
                    total = sums[c][:, 128 * q : 128 * q + 128]
                else:
                    chunk = row_piece(mine[0], 0)[:, :HD]
                    total = sums[c // 2][:, 128 * q + 64 * (c % 2) : 128 * q + 64 * (c % 2) + 64]
                chunks_ref[target, 0:rows] = chunk
                extra = jnp.broadcast_to(total, (16, width))
                extra = jnp.where(row16[:, :width] < 2, extra, jnp.where(row16[:, :width] < 4, layer_sums[:, :width], 0.0))
                high, rest = split_low(extra)
                chunks_ref[target, rows : rows + 16] = jnp.where((row16[:, :width] & 1) == 0, high, rest)

        g_low = g_new.astype(bf16)
        if below:
            payload_ref[0:rows] = g_low
            dmix = dot_nt(g_low, below_w[...]).astype(bf16)
            dmix_out[...] = dmix
            delta = delta_columns(dmix, below_mixed[...])
            delta_out[...] = delta
            payload_ref[rows : rows + 16] = stat_payload(below_log[...], delta)
        else:
            payload_ref[...] = jnp.zeros_like(payload_ref)
            dmix_out[...] = jnp.zeros_like(dmix_out)
            delta_out[...] = jnp.zeros_like(delta_out)

    ins = [*blocks]
    if not follows:
        ins += stats
    ins += [
        *tables,
        params["attn_gain"],
        params["attn_shift"],
        params["mlp_gain"],
        (params["qkv_sorted"], layer),
        params["qkv_bias_sorted"],
        (params["out_weight"], layer),
        kept["normal_all"],
        kept["k_all"],
        kept["v_all"],
        kept["q_own"],
        kept["dmix"],
        kept["log"],
        kept["delta"],
        kept["hidden"],
        grad,
        grad_mlp_in,
        kept["mixed_low"],
        kept["stats"],
    ]
    if below:
        ins += [mixed_below["mixed"], mixed_below["log"], (params["out_weight"], layer - 1)]
    outs = [
        sds((group, D), bf16),
        sds((place.blocks, rows + 16, width), bf16),
        sds((rows, D), f32),
        sds((rows + 16, D) if below else (16, D), bf16),
        sds((rows, D) if below else (16, D), bf16),
        sds((rows, 128), f32),
    ]
    scratch = [VMEM((group, D), bf16), VMEM((group, D), bf16), VMEM((NH, group), f32), VMEM((NH, group), f32)]
    return call(kernel, ins, outs, scratch, scalars, flops=10 * 10**9)


def mlp_weight_grads(place, scalars, normal_all, g_all, params, layer):
    group = place.group
    units = FF // place.blocks
    tile = min(512, group)

    def kernel(scal, normal_ref, g_ref, gain, shift, up, up_b, down, up_out, down_out, bias_out):
        gain_l, shift_l = gain[layer : layer + 1], shift[layer : layer + 1]

        def step(i, carry):
            up_t, down_g, bias, g_sum = carry
            at = pl.multiple_of(i * tile, tile)
            x = (normal_ref[pl.ds(at, tile)].astype(f32) * gain_l + shift_l).astype(bf16)
            g = g_ref[pl.ds(at, tile)]
            gate = dot(x, up[...]) + up_b[...]
            cdf = 0.5 * (1.0 + lax.erf(gate * math.sqrt(0.5)))
            pdf = jnp.exp(-0.5 * gate * gate) * (1.0 / math.sqrt(2.0 * math.pi))
            acted = (gate * cdf).astype(bf16)
            grad_gate = (dot_nt(g, down[...]) * (cdf + gate * pdf)).astype(bf16)
            up_t += dot(grad_gate.T, x)
            down_g += dot(acted.T, g)
            bias += jnp.sum(grad_gate.astype(f32), axis=0, keepdims=True)
            g_sum += jnp.sum(g.astype(f32), axis=0, keepdims=True)
            return up_t, down_g, bias, g_sum

        zero = jnp.zeros((units, D), f32)
        up_t, down_g, bias, g_sum = lax.fori_loop(
            0, group // tile, step, (zero, zero, jnp.zeros((1, units), f32), jnp.zeros((1, D), f32))
        )
        up_out[...] = up_t.T.astype(bf16)
        for m in range(place.n_head):
            down_out[m] = down_g[:, 128 * m : 128 * m + 128].astype(bf16)
        bias_out[...] = jnp.zeros_like(bias_out)
        bias_out[0:1, 0:units] = bias
        bias_out[1:2] = g_sum

    first = scalars[1] * (FF // place.n_head) + scalars[0] * units
    up = lax.dynamic_slice(params["up_weight"][layer], (0, first), (D, units))
    up_b = lax.dynamic_slice(params["up_bias"][layer], (first,), (units,))[None]
    down = lax.dynamic_slice(params["down_weight"][layer], (first, 0), (units, D))
    return call(
        kernel,
        [normal_all, g_all, params["mlp_gain"], params["mlp_shift"], up, up_b, down],
        [sds((D, units), bf16), sds((place.n_head, units, 128), bf16), sds((8, D), f32)],
        (),
        scalars,
        flops=4 * 2 * group * D * units,
    )


def attention_weight_grads(place, scalars, received, normal_all, g_all, params, layer):
    group, rows = place.group, place.rows
    width = received.shape[2]

    def kernel(scal, chunk_ref, normal_ref, g_ref, gain, shift, cols_out, rows_out, extra_out, chunk_t, total_ref):
        gain_l, shift_l = gain[layer : layer + 1], shift[layer : layer + 1]
        bias = jnp.zeros((1, width), f32)
        extra = jnp.zeros((16, width), f32)
        for j in range(place.blocks):
            chunk = chunk_ref[j, 0:rows]
            bias += jnp.sum(chunk.astype(f32), axis=0, keepdims=True)
            extra += chunk_ref[j, rows : rows + 16].astype(f32)
            chunk_t[:, j * rows : (j + 1) * rows] = chunk.T
        outward = scal[0] >= place.n_ctx * 3 // 4

        @pl.when(jnp.logical_not(outward))
        def _():
            total = jnp.zeros((width, D), f32)
            for at in range(0, group, 512):
                x = (normal_ref[at : at + 512].astype(f32) * gain_l + shift_l).astype(bf16)
                total += dot(chunk_t[:, at : at + 512], x)
            total_ref[...] = total

        @pl.when(outward)
        def _():
            total_ref[...] = dot(chunk_t[...], g_ref[...])

        total = total_ref[...]
        cols_out[...] = total.T.astype(bf16)
        for m in range(place.n_head):
            rows_out[m] = total[:, 128 * m : 128 * m + 128].astype(bf16)
        extra_out[...] = jnp.zeros_like(extra_out)
        extra_out[0:1] = bias
        extra_out[1:2] = extra[0:1] + extra[1:2]
        extra_out[2:3] = extra[2:3] + extra[3:4]

    return call(
        kernel,
        [received, normal_all, g_all, params["attn_gain"], params["attn_shift"]],
        [sds((D, width), bf16), sds((place.n_head, width, 128), bf16), sds((8, width), f32)],
        [VMEM((width, group), bf16), VMEM((width, D), f32)],
        scalars,
        flops=2 * group * D * width,
    )


def gather_group(own, n_ctx, n_head):
    rings = [own] + [
        lax.ppermute(own, "ctx", [(i, (i + s) % n_ctx) for i in range(n_ctx)]) for s in range(1, n_ctx)
    ]
    slots = {(s, 0): rings[s] for s in range(n_ctx)}
    for flip in (2, 1):
        for (s, f), block in list(slots.items()):
            slots[s, f ^ flip] = lax.ppermute(block, "head", [(i, i ^ flip) for i in range(n_head)])
    return [slots[s, f] for s in range(n_ctx) for f in range(n_head)]


def sum_dp(x, n_dp):
    if n_dp == 2:
        other = lax.ppermute(x, "dp", [(0, 1), (1, 0)])
        return (x.astype(f32) + other.astype(f32)).astype(x.dtype)
    return lax.psum(x, "dp")


def finish_mlp(up_g, down_g, bias, place, n_dp):
    up_g, down_g, bias = (sum_dp(v, n_dp) for v in (up_g, down_g, bias))
    down_g = lax.all_to_all(down_g, "head", 0, 0, tiled=True)
    units = up_g.shape[1]
    up_all = lax.all_gather(up_g, "ctx", axis=1, tiled=True).astype(f32)
    down_all = lax.all_gather(down_g, "ctx", axis=1, tiled=True).astype(f32).reshape(FF, 128)
    up_bias = lax.all_gather(bias[0, :units], "ctx", axis=0, tiled=True)
    g_sum = lax.dynamic_slice(bias[1], (lax.axis_index("head") * 128,), (128,))
    return up_all, up_bias, down_all, g_sum


def finish_attention(cols_g, rows_g, extra, place, n_dp):
    n_ctx = place.n_ctx
    cut = n_ctx * 3 // 4
    cols_g, rows_g, extra = (sum_dp(v, n_dp) for v in (cols_g, rows_g, extra))
    rows_g = lax.all_to_all(rows_g, "head", 0, 0, tiled=True)
    width = cols_g.shape[1]
    cols_all = lax.all_gather(cols_g, "ctx", axis=0)
    rows_all = lax.all_gather(rows_g, "ctx", axis=0)
    extra_all = lax.all_gather(extra, "ctx", axis=0)
    qkv = jnp.swapaxes(cols_all[:cut], 0, 1).reshape(D, cut * width).astype(f32)
    out = jnp.swapaxes(rows_all[cut:], 0, 1).reshape(D, 128).astype(f32)
    qkv_b = extra_all[:cut, 0].reshape(-1)
    four = extra_all[:, 1].reshape(4, 128)
    stats = extra[2, :3]
    return qkv, qkv_b, out, four, stats


def per_device(
    hidden_in,
    lengths,
    attn_gain,
    attn_shift,
    mlp_gain,
    mlp_shift,
    qkv_weight,
    qkv_bias,
    out_weight,
    out_bias,
    up_weight,
    up_bias,
    down_weight,
    down_bias,
    cotangent,
):
    rows = hidden_in.shape[0]
    n_dp, n_ctx, n_head = (lax.axis_size(a) for a in ("dp", "ctx", "head"))
    place = Place(n_ctx, n_head, rows)
    group = place.group
    ctx, head = lax.axis_index("ctx"), lax.axis_index("head")
    ends = [jnp.sum(lengths[0, : k + 1]) for k in range(4)]
    scalars = jnp.stack([ctx, head, ctx * n_head + head, *ends, ctx]).astype(jnp.int32)

    def by_kind(x):
        lead = x.shape[:-1]
        return jnp.swapaxes(x.reshape(*lead, NH, 3, HD), -3, -2).reshape(*lead, 3 * D)

    params = {
        "attn_gain": attn_gain,
        "attn_shift": attn_shift,
        "mlp_gain": mlp_gain,
        "mlp_shift": mlp_shift,
        "qkv_sorted": by_kind(qkv_weight),
        "qkv_bias_sorted": by_kind(qkv_bias),
        "out_weight": out_weight,
        "out_bias": out_bias,
        "up_weight": up_weight,
        "up_bias": up_bias,
        "down_weight": down_weight,
        "down_bias": down_bias,
    }
    where = jnp.arange(group, dtype=jnp.int32)
    turn = (where - start_of(where, ends)).astype(f32)[:, None]
    dim = jnp.arange(128, dtype=jnp.int32)[None, :] % HD
    freq = rope_base ** (-2.0 * (dim % (ROT // 2)).astype(f32) / ROT)
    angle = turn * freq
    sine = jnp.sin(angle)
    tables = [
        jnp.where(dim < ROT, jnp.cos(angle), 1.0),
        jnp.where(dim < ROT // 2, -sine, 0.0),
        jnp.where((dim >= ROT // 2) & (dim < ROT), sine, 0.0),
    ]
    gather = functools.partial(gather_group, n_ctx=n_ctx, n_head=n_head)

    hidden = hidden_in
    blocks = gather(hidden_in)
    cot_blocks = gather(cotangent)
    kept = []
    for layer in range(LAYERS):
        mlp_out, factor, _ = mlp_forward(hidden, params, layer)
        last = layer == LAYERS - 1
        (normal_all, k_all, v_all, q_own, mixed, mixed_low, log, delta, dmix, h_out, stats, low) = attention_forward(
            place, scalars, blocks, tables, params, layer, hidden, mlp_out, cotangent if last else None
        )
        kept.append(
            {
                "hidden": hidden,
                "factor": factor,
                "normal_all": normal_all,
                "k_all": k_all,
                "v_all": v_all,
                "q_own": q_own,
                "mixed": mixed,
                "mixed_low": mixed_low,
                "log": log,
                "delta": delta,
                "dmix": dmix,
                "stats": stats,
            }
        )
        hidden = h_out
        low_blocks = gather(low)
        blocks = low_blocks
    output_rows = hidden
    stat_blocks = low_blocks
    blocks = cot_blocks
    grad = cotangent
    done = [None] * LAYERS
    for layer in reversed(range(LAYERS)):
        own = kept[layer]
        grad_mlp_in = mlp_backward(grad, own["factor"], own["hidden"], params, layer)
        g_all, chunks, grad, payload, dmix, delta = attention_backward(
            place, scalars, blocks, stat_blocks, tables, params, layer, own, grad, grad_mlp_in, kept[layer - 1] if layer else None
        )
        if layer:
            blocks, stat_blocks = gather(payload), None
            kept[layer - 1]["dmix"], kept[layer - 1]["delta"] = dmix, delta
        up_g, down_g, mlp_bias = mlp_weight_grads(place, scalars, own["normal_all"], g_all, params, layer)
        up_all, up_b, down_all, g_sum = finish_mlp(up_g, down_g, mlp_bias, place, n_dp)
        received = lax.all_to_all(chunks, ("ctx", "head"), 0, 0, tiled=True)
        cols_g, rows_g, extra = attention_weight_grads(place, scalars, received, own["normal_all"], g_all, params, layer)
        qkv, qkv_b, out, four, stats = finish_attention(cols_g, rows_g, extra, place, n_dp)
        done[layer] = (four[0], four[1], four[2], four[3], qkv, qkv_b, out, g_sum, up_all, up_b, down_all, g_sum, stats)
    totals = [jnp.stack([done[layer][i] for layer in range(LAYERS)]) for i in range(13)]
    layer_stats = jnp.sqrt(totals[12] / float(group * n_dp * D))
    return (output_rows, grad, *totals[:12], layer_stats)


def solution(mesh):
    rows = P(("dp", "ctx", "head"), None)
    return jax.shard_map(
        per_device,
        mesh=mesh,
        in_specs=(rows, P("dp", None), *([P()] * 12), rows),
        out_specs=(
            rows,
            rows,
            P(None, "head"),
            P(None, "head"),
            P(None, "head"),
            P(None, "head"),
            P(None, None, "head"),
            P(None, "head"),
            P(None, None, "head"),
            P(None, "head"),
            P(None, None, "head"),
            P(None, "head"),
            P(None, None, "head"),
            P(None, "head"),
            P(),
        ),
        check_vma=False,
    )
```

```python
import math

import jax
import jax.numpy as jnp
from jax import lax
from jax.experimental import pallas as pl
from jax.experimental.pallas import tpu as pltpu
from jax.sharding import PartitionSpec as P

D = 512
FF = 2048
NH = 8
HD = 64
ROT = 16
LAYERS = 2
PAIRS = NH // 2
epsilon = 1e-05
masked_value = -1e30
score_scale = 0.125
rope_base = 10000.0
f32 = jnp.float32
bf16 = jnp.bfloat16
STEP = 256
VMEM = pltpu.VMEM


def dot(a, b):
    return lax.dot_general(a, b, (((1,), (0,)), ((), ())), preferred_element_type=f32)


def dot_nt(a, b):
    return lax.dot_general(a, b, (((1,), (1,)), ((), ())), preferred_element_type=f32)


def norm_parts(hidden):
    centred = hidden - jnp.mean(hidden, axis=-1, keepdims=True)
    inverse = lax.rsqrt(jnp.mean(centred * centred, axis=-1, keepdims=True) + epsilon)
    return centred * inverse, inverse


def rope(x, cos_t, left_t, right_t):
    return x * cos_t + pltpu.roll(x, 128 - 8, 1) * left_t + pltpu.roll(x, 8, 1) * right_t


def start_of(place, ends):
    start = jnp.zeros_like(place)
    for end in ends:
        start = jnp.where(end <= place, end, start)
    return start


def end_of(place, ends, size):
    found = jnp.int32(size)
    for end in reversed(ends):
        found = jnp.where(place < end, end, found)
    return found


def split_low(x):
    high = x.astype(bf16)
    return high, (x - high.astype(f32)).astype(bf16)


def lane_of(rows):
    return lax.broadcasted_iota(jnp.int32, (rows, 128), 1)


def two_heads(x):
    first = lane_of(x.shape[0]) < HD
    zero = jnp.zeros_like(x)
    return jnp.concatenate([jnp.where(first, x, zero), jnp.where(first, zero, x)], axis=0)


def one_pair(x):
    rows = x.shape[0] // 2
    return jnp.where(lane_of(rows) < HD, x[:rows], x[rows:])


def dot_tn(a, b):
    return lax.dot_general(a, b, (((0,), (0,)), ((), ())), preferred_element_type=f32)


def two_heads_t(x):
    first = lax.broadcasted_iota(jnp.int32, x.shape, 0) < HD
    zero = jnp.zeros_like(x)
    return jnp.concatenate([jnp.where(first, x, zero), jnp.where(first, zero, x)], axis=1)


def one_pair_t(x):
    rows = x.shape[1] // 2
    return jnp.where(lax.broadcasted_iota(jnp.int32, (128, rows), 0) < HD, x[:, :rows], x[:, rows:])


def rope_t(x, cos_t, left_t, right_t):
    return x * cos_t + pltpu.roll(x, 128 - 8, 0) * left_t + pltpu.roll(x, 8, 0) * right_t


class Far:
    def __init__(self, array):
        self.array = array


def call(kernel, ins, outs, scratch=(), scalars=None, vmem=60 << 20, flops=10**9, into=None):
    specs, arrays = [], []

    def block(shape, layer, cols=None):
        place = (layer, *([0] * (len(shape) - 1)))
        return pl.BlockSpec((None, *shape[1:-1], cols or shape[-1]), lambda i: place)

    def whole(shape):
        return pl.BlockSpec(shape, lambda i: (0,) * len(shape))

    if scalars is not None:
        specs.append(pl.BlockSpec(memory_space=pltpu.SMEM))
        arrays.append(scalars)
        body = kernel

        def kernel(lengths_ref, *refs):
            ctx, head = lax.axis_index("ctx"), lax.axis_index("head")
            ends = [lengths_ref[0, 0]]
            for k in range(1, 4):
                ends.append(ends[-1] + lengths_ref[0, k])
            body([ctx, head, ctx * lax.axis_size("head") + head, *ends, lax.axis_index("dp")], *refs)

    for item in ins:
        if isinstance(item, Far):
            specs.append(pl.BlockSpec(memory_space=pl.ANY))
            arrays.append(item.array)
            continue
        array = item[0] if isinstance(item, tuple) else item
        specs.append(block(array.shape, *item[1:]) if isinstance(item, tuple) else whole(array.shape))
        arrays.append(array)
    aliases = {}
    if into is not None:
        spots = [k for k, o in enumerate(outs) if isinstance(o, tuple)]
        for spot, array in zip(spots, into):
            aliases[len(arrays)] = spot
            specs.append(pl.BlockSpec(memory_space=pl.ANY))
            arrays.append(array)
    shapes = [o[0] if isinstance(o, tuple) else o for o in outs]
    out_specs = [block(o[0].shape, o[1]) if isinstance(o, tuple) else whole(o.shape) for o in outs]
    moved = sum(x.size * x.dtype.itemsize for x in arrays)
    return pl.pallas_call(
        kernel,
        grid=(1,),
        in_specs=specs,
        out_specs=out_specs,
        out_shape=shapes,
        scratch_shapes=list(scratch),
        input_output_aliases=aliases,
        compiler_params=pltpu.CompilerParams(vmem_limit_bytes=vmem),
        cost_estimate=pl.CostEstimate(flops=flops, bytes_accessed=moved, transcendentals=0),
    )(*arrays)


def sds(shape, dtype):
    return jax.ShapeDtypeStruct(shape, dtype)


def mlp_forward(hidden, params, layer):
    rows = hidden.shape[0]

    def kernel(h_ref, gain, shift, up, up_b, down, down_b, out_ref, factor_ref, normal_ref):
        normal, _ = norm_parts(h_ref[...].astype(f32))
        normal_ref[...] = normal.astype(bf16)
        x = (normal * gain[layer : layer + 1] + shift[layer : layer + 1]).astype(bf16)
        total = jnp.zeros((rows, D), f32)
        for j in range(0, FF, 512):
            gate = dot(x, up[:, j : j + 512]) + up_b[layer : layer + 1, j : j + 512]
            cdf = 0.5 * (1.0 + lax.erf(gate * math.sqrt(0.5)))
            pdf = jnp.exp(-0.5 * gate * gate) * (1.0 / math.sqrt(2.0 * math.pi))
            factor_ref[:, j : j + 512] = cdf + gate * pdf
            total += dot((gate * cdf).astype(bf16), down[j : j + 512])
        out_ref[...] = total + down_b[layer : layer + 1]

    return call(
        kernel,
        [
            hidden,
            params["mlp_gain"],
            params["mlp_shift"],
            (params["up_weight"], layer),
            params["up_bias"],
            (params["down_weight"], layer),
            params["down_bias"],
        ],
        [sds((rows, D), f32), sds((rows, FF), f32), sds((rows, D), bf16)],
        flops=2 * 2 * rows * D * FF,
    )


class Place:
    def __init__(self, n_dp, n_ctx, n_head, rows):
        self.n_ctx, self.n_head, self.rows = n_ctx, n_head, rows
        self.halves = n_dp == 2
        self.blocks = n_ctx * n_head
        self.group = self.blocks * rows
        self.units = FF // self.blocks
        self.packed_rows = 3 * D // self.blocks
        self.out_rows = 128 // n_ctx
        self.share_rows = self.packed_rows + self.out_rows + 32

    def position(self, scal, slot):
        shift, flip = slot // self.n_head, slot % self.n_head
        ctx = lax.rem(scal[0] - shift + self.n_ctx, self.n_ctx)
        return ctx * self.n_head + (scal[1] ^ flip)

    def ends(self, scal):
        return [scal[3 + k] for k in range(4)]


def delta_rows(grad_mixed_t, mixed_t):
    return jnp.concatenate(
        [
            jnp.sum(grad_mixed_t[n * HD : (n + 1) * HD].astype(f32) * mixed_t[n * HD : (n + 1) * HD], axis=0, keepdims=True)
            for n in range(NH)
        ],
        axis=0,
    )


def stat_payload(logs, deltas):
    parts = [*split_low(logs), *split_low(deltas)]
    top = jnp.concatenate(parts, axis=1)
    return jnp.concatenate([top, jnp.zeros_like(top)], axis=0)


def attention_forward(place, scalars, blocks, tables, params, layer, hidden, mlp_out, last_grad):
    rows, group = place.rows, place.group
    first_layer = layer == 0
    last = last_grad is not None
    tile = min(512, group)

    def kernel(scal, *refs):
        refs = list(refs)
        xs = [refs.pop(0) for _ in range(place.blocks)]
        cos_t, left_t, right_t, gain, shift, w, b, out_w, out_b, h_ref, mlp_ref = refs[:11]
        refs = refs[11:]
        g_ref, below_ref = (refs.pop(0), refs.pop(0)) if last else (None, None)
        (normal_all, k_all, v_all, q_own, kv_own, mixed_ref, mixed_low_ref, log_ref, delta_ref, dmix_ref, h_out, stats_ref, low_ref) = refs[:13]
        a_all = refs[13]
        own_at = pl.multiple_of(scal[2] * rows, rows)
        ends = place.ends(scal)
        gain_l, shift_l = gain[layer : layer + 1], shift[layer : layer + 1]
        for slot in range(place.blocks):
            at = pl.multiple_of(place.position(scal, slot) * rows, rows)
            x = xs[slot][...].astype(f32)
            normal = norm_parts(x)[0] if first_layer else x
            normal_all[pl.ds(at, rows)] = normal.astype(bf16)
            a_all[pl.ds(at, rows)] = (normal * gain_l + shift_l).astype(bf16)

        def project(i, _):
            at = pl.multiple_of(i * tile, tile)
            k = dot(a_all[pl.ds(at, tile)], w[:, D : 2 * D]) + b[layer : layer + 1, D : 2 * D]
            tabs = [t[pl.ds(at, tile)] for t in (cos_t, left_t, right_t)]
            for p in range(PAIRS):
                k_all[pl.ds(at, tile), 128 * p : 128 * p + 128] = rope(k[:, 128 * p : 128 * p + 128], *tabs).astype(bf16)
            v = dot(a_all[pl.ds(at, tile)], w[:, 2 * D :]) + b[layer : layer + 1, 2 * D :]
            v_all[pl.ds(at, tile)] = v.astype(bf16)
            return 0

        first_key = start_of(own_at, ends)
        lax.fori_loop(first_key // tile, (own_at + rows - 1) // tile + 1, project, 0)
        kv_own[0:rows], kv_own[rows : 2 * rows] = k_all[pl.ds(own_at, rows)], v_all[pl.ds(own_at, rows)]
        q = dot(a_all[pl.ds(own_at, rows)], w[:, :D]) + b[layer : layer + 1, :D]
        tabs = [t[pl.ds(own_at, rows)] for t in (cos_t, left_t, right_t)]
        for p in range(PAIRS):
            turned = rope(q[:, 128 * p : 128 * p + 128], *tabs).astype(bf16)
            q_own[:, 128 * p : 128 * p + 128] = turned * jnp.asarray(score_scale, bf16)
        t = own_at + lax.broadcasted_iota(jnp.int32, (1, rows), 1)
        start = start_of(t, ends)
        low = first_key // STEP
        high = (own_at + rows - 1) // STEP + 1
        doubled = [two_heads(q_own[:, 128 * p : 128 * p + 128]) for p in range(PAIRS)]

        def attend(i, carry):
            at = pl.multiple_of(i * STEP, STEP)
            s_at = at + lax.broadcasted_iota(jnp.int32, (STEP, 1), 0)
            bias = jnp.where((s_at >= start) & (s_at <= t), 0.0, masked_value)
            bias = jnp.concatenate([bias, bias], axis=1)
            new = []
            for p in range(PAIRS):
                most, total, acc = carry[p]
                scores = dot_nt(k_all[pl.ds(at, STEP), 128 * p : 128 * p + 128], doubled[p]) + bias
                newest = jnp.maximum(most, jnp.max(scores, axis=0, keepdims=True))
                chance = jnp.exp(scores - newest)
                scale = jnp.exp(most - newest)
                total = total * scale + jnp.sum(chance, axis=0, keepdims=True)
                acc = acc * scale + dot_tn(v_all[pl.ds(at, STEP), 128 * p : 128 * p + 128], chance.astype(bf16))
                new.append((newest, total, acc))
            return tuple(new)

        begin = tuple(
            (jnp.full((1, 2 * rows), masked_value, f32), jnp.zeros((1, 2 * rows), f32), jnp.zeros((128, 2 * rows), f32))
            for _ in range(PAIRS)
        )
        done = lax.fori_loop(low, high, attend, begin)
        logs = []
        for p in range(PAIRS):
            most, total, acc = done[p]
            mixed_ref[128 * p : 128 * p + 128] = one_pair_t(acc / total)
            log = most + jnp.log(total)
            logs += [log[:, :rows], log[:, rows:]]
        log_rows = jnp.concatenate(logs, axis=0)
        log_ref[...] = log_rows
        mixed_low = mixed_ref[...].astype(bf16)
        mixed_low_ref[layer * D : layer * D + D] = mixed_low
        if last:
            mixed_low_ref[0 : layer * D] = below_ref[...]
        attn_out = dot_tn(mixed_low, out_w[...]) + out_b[layer : layer + 1]
        h = h_ref[...].astype(f32)
        mlp = mlp_ref[...]
        result = h + attn_out + mlp
        lane = lane_of(8)
        sums = [jnp.sum(jnp.sum(v * v, axis=1, keepdims=True), axis=0, keepdims=True) for v in (h, attn_out, mlp)]
        stats_ref[...] = jnp.where(lane == 0, sums[0], jnp.where(lane == 1, sums[1], jnp.where(lane == 2, sums[2], 0.0)))
        if last:
            h_out[...] = result.astype(bf16)
            dmix = dot_nt(out_w[...], g_ref[...]).astype(bf16)
            dmix_ref[...] = dmix
            deltas = delta_rows(dmix, mixed_ref[...])
            delta_ref[...] = deltas
            low_ref[...] = stat_payload(log_rows, deltas)
        else:
            h_out[...] = result
            low_ref[...] = norm_parts(result)[0].astype(bf16)
            dmix_ref[...] = jnp.zeros_like(dmix_ref)
            delta_ref[...] = jnp.zeros_like(delta_ref)

    ins = [
        *blocks,
        *tables,
        params["attn_gain"],
        params["attn_shift"],
        (params["qkv_sorted"], layer),
        params["qkv_bias_sorted"],
        (params["out_weight"], layer),
        params["out_bias"],
        hidden,
        mlp_out,
    ]
    if last:
        ins += last_grad
    outs = [
        sds((group, D), bf16),
        sds((group, D), bf16),
        sds((group, D), bf16),
        sds((rows, D), bf16),
        sds((2 * rows, D), bf16),
        sds((D, rows), f32),
        sds(((layer + 1) * D, rows), bf16),
        sds((NH, rows), f32),
        sds((NH, rows), f32),
        sds((D, rows), bf16),
        sds((rows, D), bf16 if last else f32),
        sds((8, 128), f32),
        sds((16, D) if last else (rows, D), bf16),
    ]
    return call(kernel, ins, outs, [VMEM((group, D), bf16)], scalars, flops=60 * 10**9)


def mlp_backward(grad, factor, hidden, params, layer):
    rows = grad.shape[0]

    def kernel(g_ref, factor_ref, down, up, out_ref):
        g_low = g_ref[...].astype(bf16)
        total = jnp.zeros((rows, D), f32)
        for j in range(0, FF, 512):
            grad_gate = (dot_nt(g_low, down[j : j + 512]) * factor_ref[:, j : j + 512]).astype(bf16)
            total += dot_nt(grad_gate, up[:, j : j + 512])
        out_ref[...] = total

    return call(
        kernel,
        [grad, factor, (params["down_weight"], layer), (params["up_weight"], layer)],
        [sds((rows, D), f32)],
        flops=2 * 2 * rows * D * FF,
    )[0]


def query_backward(place, scalars, tables, own_tables, params, layer, kept):
    rows, group = place.rows, place.group
    tile = min(512, group)

    def kernel(scal, cos_t, left_t, right_t, own_tabs, gain, shift, w, b, normal_all, k_all, v_all, q_own, dmix_ref, log_ref, delta_ref, q_all, grad_ref, grad_t_ref):
        own_at = pl.multiple_of(scal[2] * rows, rows)
        ends = place.ends(scal)
        gain_l, shift_l = gain[layer : layer + 1], shift[layer : layer + 1]

        def project(i, _):
            at = pl.multiple_of(i * tile, tile)
            a = (normal_all[pl.ds(at, tile)].astype(f32) * gain_l + shift_l).astype(bf16)
            q = dot(a, w[...]) + b[layer : layer + 1, :D]
            tabs = [t[pl.ds(at, tile)] for t in (cos_t, left_t, right_t)]
            for p in range(PAIRS):
                turned = rope(q[:, 128 * p : 128 * p + 128], *tabs).astype(bf16)
                q_all[pl.ds(at, tile), 128 * p : 128 * p + 128] = turned * jnp.asarray(score_scale, bf16)
            return 0

        last_end = end_of(own_at + rows - 1, ends, group)
        lax.fori_loop(own_at // tile, (last_end + tile - 1) // tile, project, 0)
        t = own_at + lax.broadcasted_iota(jnp.int32, (1, rows), 1)
        start = start_of(t, ends)
        q2 = [two_heads(q_own[:, 128 * p : 128 * p + 128]) for p in range(PAIRS)]
        d2 = [two_heads_t(dmix_ref[128 * p : 128 * p + 128]) for p in range(PAIRS)]
        log2 = [jnp.concatenate([log_ref[2 * p : 2 * p + 1], log_ref[2 * p + 1 : 2 * p + 2]], axis=1) for p in range(PAIRS)]
        delta2 = [
            jnp.concatenate([delta_ref[2 * p : 2 * p + 1], delta_ref[2 * p + 1 : 2 * p + 2]], axis=1) for p in range(PAIRS)
        ]

        def queries(i, carry):
            at = pl.multiple_of(i * STEP, STEP)
            s = at + lax.broadcasted_iota(jnp.int32, (STEP, 1), 0)
            bias = jnp.where((s >= start) & (s <= t), 0.0, masked_value)
            bias = jnp.concatenate([bias, bias], axis=1)
            new = []
            for p in range(PAIRS):
                ks = k_all[pl.ds(at, STEP), 128 * p : 128 * p + 128]
                vs = v_all[pl.ds(at, STEP), 128 * p : 128 * p + 128]
                chance = jnp.exp(dot_nt(ks, q2[p]) + bias - log2[p])
                grad_s = (chance * (dot(vs, d2[p]) - delta2[p])).astype(bf16)
                new.append(carry[p] + dot_tn(ks, grad_s))
            return tuple(new)

        zero = jnp.zeros((128, 2 * rows), f32)
        done = lax.fori_loop(
            start_of(own_at, ends) // STEP, (own_at + rows - 1) // STEP + 1, queries, tuple(zero for _ in range(PAIRS))
        )
        tabs = [own_tabs[0:rows].T, -own_tabs[rows : 2 * rows].T, -own_tabs[2 * rows : 3 * rows].T]
        for p in range(PAIRS):
            grad_t = rope_t(one_pair_t(done[p]) * score_scale, *tabs)
            grad_t_ref[128 * p : 128 * p + 128] = grad_t.astype(bf16)
            grad_ref[:, 128 * p : 128 * p + 128] = grad_t.T.astype(bf16)

    return call(
        kernel,
        [
            *tables,
            own_tables,
            params["attn_gain"],
            params["attn_shift"],
            (params["qkv_sorted"], layer, D),
            params["qkv_bias_sorted"],
            kept["normal_all"],
            kept["k_all"],
            kept["v_all"],
            kept["q_own"],
            kept["dmix"],
            kept["log"],
            kept["delta"],
        ],
        [sds((group, D), bf16), sds((rows, D), bf16), sds((D, rows), bf16)],
        (),
        scalars,
        flops=30 * 10**9,
    )


def key_backward(place, scalars, g_whole, stats, own_tables, params, layer, kept, queries, grad, grad_mlp_in, mixed_below):
    rows, group = place.rows, place.group
    below = layer > 0
    n_stats = len(stats)
    tile = min(512, group)

    def kernel(scal, *refs):
        refs = list(refs)
        ss = [refs.pop(0) for _ in range(n_stats)]
        (g_all, own_tabs, gain, mlp_gain, w, out_w, q_all, gq_ref, gq_t_ref, kv_own, h_ref, g_ref, gmlp_ref, stats_ref) = refs[:14]
        refs = refs[14:]
        if below:
            below_mixed, below_log, below_w = refs[:3]
            refs = refs[3:]
        pieces_out, g_out, payload_ref, dmix_out, delta_out = refs[:5]
        dm_all, log_all, delta_all, packed_t = refs[5:]
        own_at = pl.multiple_of(scal[2] * rows, rows)
        ends = place.ends(scal)
        gain_l = gain[layer : layer + 1]
        for slot in range(place.blocks):
            at = pl.multiple_of(place.position(scal, slot) * rows, rows)
            if below:
                flip = slot % place.n_head
                info = ss[slot // place.n_head][16 * flip : 16 * flip + 16].astype(f32)[:NH]
            else:
                info = ss[slot][rows : rows + 16].astype(f32)[:NH]
            log_all[:, pl.ds(at, rows)] = info[:, 0:128] + info[:, 128:256]
            delta_all[:, pl.ds(at, rows)] = info[:, 256:384] + info[:, 384:512]
        last_end = end_of(own_at + rows - 1, ends, group)

        def project(i, _):
            at = pl.multiple_of(i * tile, tile)
            dm_all[pl.ds(at, tile)] = dot_nt(g_all[pl.ds(at, tile)], out_w[...]).astype(bf16)
            return 0

        lax.fori_loop(own_at // tile, (last_end + tile - 1) // tile, project, 0)
        s_at = own_at + lax.broadcasted_iota(jnp.int32, (rows, 1), 0)
        k2 = [two_heads(kv_own[0:rows, 128 * p : 128 * p + 128]) for p in range(PAIRS)]
        v2 = [two_heads(kv_own[rows : 2 * rows, 128 * p : 128 * p + 128]) for p in range(PAIRS)]

        def keys(i, carry):
            at = pl.multiple_of(i * STEP, STEP)
            t = at + lax.broadcasted_iota(jnp.int32, (1, STEP), 1)
            start = start_of(t, ends)
            bias = jnp.where((s_at >= start) & (s_at <= t), 0.0, masked_value)
            new = []
            for p in range(PAIRS):
                dk, dv = carry[p]
                qs = q_all[pl.ds(at, STEP), 128 * p : 128 * p + 128]
                dms = dm_all[pl.ds(at, STEP), 128 * p : 128 * p + 128]
                scores = dot_nt(k2[p], qs)
                pulled = dot_nt(v2[p], dms)
                chances, grads = [], []
                for half in range(2):
                    n = 2 * p + half
                    part = slice(half * rows, half * rows + rows)
                    chance = jnp.exp(scores[part] + bias - log_all[n : n + 1, pl.ds(at, STEP)])
                    grads.append(chance * (pulled[part] - delta_all[n : n + 1, pl.ds(at, STEP)]))
                    chances.append(chance)
                chance = jnp.concatenate(chances, axis=0).astype(bf16)
                grad_s = jnp.concatenate(grads, axis=0).astype(bf16)
                new.append((dk + dot(grad_s, qs), dv + dot(chance, dms)))
            return tuple(new)

        zero = jnp.zeros((2 * rows, 128), f32)
        done = lax.fori_loop(own_at // STEP, (last_end + STEP - 1) // STEP, keys, tuple((zero, zero) for _ in range(PAIRS)))
        tabs = [own_tabs[0:rows], -own_tabs[rows : 2 * rows], -own_tabs[2 * rows : 3 * rows]]
        grad_k = [rope(one_pair(done[p][0]), *tabs).astype(bf16) for p in range(PAIRS)]
        grad_v = [one_pair(done[p][1]).astype(bf16) for p in range(PAIRS)]
        grad_in = dot_nt(gq_ref[...], w[:, 0:D])
        for j, parts in ((1, grad_k), (2, grad_v)):
            grad_in += dot_nt(jnp.concatenate(parts, axis=1), w[:, j * D : j * D + D])

        normal, inverse = norm_parts(h_ref[...].astype(f32))
        grad_mlp = gmlp_ref[...]
        grad_normal = grad_in * gain_l + grad_mlp * mlp_gain[layer : layer + 1]
        back = inverse * (
            grad_normal
            - jnp.mean(grad_normal, axis=-1, keepdims=True)
            - normal * jnp.mean(grad_normal * normal, axis=-1, keepdims=True)
        )
        g_new = g_ref[...].astype(f32) + back
        g_out[...] = g_new

        sums = [
            jnp.sum(v, axis=0, keepdims=True)
            for v in (grad_in * normal, grad_in, grad_mlp * normal, grad_mlp)
        ]
        for j in range(3):
            for p in range(PAIRS):
                if j == 0:
                    turned = gq_t_ref[128 * p : 128 * p + 128]
                else:
                    turned = (grad_k, grad_v)[j - 1][p].astype(f32).T.astype(bf16)
                for half in range(2):
                    at = (2 * p + half) * 3 * HD + j * HD
                    packed_t[at : at + HD] = turned[half * HD : half * HD + HD]
        layer_sums = jnp.where(lane_of(8) < 4, stats_ref[...], 0.0)
        layer_sums = jnp.broadcast_to(pltpu.roll(layer_sums, scal[2] * 4, 1)[0:1], (16, 128))
        row16 = lax.broadcasted_iota(jnp.int32, (16, 128), 0)
        for p in range(place.n_head):
            extra = jnp.concatenate([x[:, 128 * p : 128 * p + 128] for x in sums] + [jnp.zeros((4, 128), f32)], axis=0)
            extra = jnp.concatenate([extra, extra], axis=0)
            extra = jnp.where((row16 & 7) == 4, layer_sums, extra)
            high, rest = split_low(extra)
            pieces_out[p, 0 : 3 * 128] = packed_t[3 * 128 * p : 3 * 128 * (p + 1)]
            pieces_out[p, 3 * 128 : 3 * 128 + 16] = jnp.where(row16 < 8, high, rest)

        g_low = g_new.astype(bf16)
        if below:
            payload_ref[0:rows] = g_low
            dmix = dot_nt(below_w[...], g_low).astype(bf16)
            dmix_out[...] = dmix
            deltas = delta_rows(dmix, below_mixed[...])
            delta_out[...] = deltas
            payload_ref[rows : rows + 16] = stat_payload(below_log[...], deltas)
        else:
            payload_ref[...] = jnp.zeros_like(payload_ref)
            dmix_out[...] = jnp.zeros_like(dmix_out)
            delta_out[...] = jnp.zeros_like(delta_out)

    ins = [
        *stats,
        g_whole,
        own_tables,
        params["attn_gain"],
        params["mlp_gain"],
        (params["qkv_sorted"], layer),
        (params["out_weight"], layer),
        *queries,
        kept["kv_own"],
        kept["hidden"],
        grad,
        grad_mlp_in,
        kept["stats"],
    ]
    if below:
        ins += [mixed_below["mixed"], mixed_below["log"], (params["out_weight"], layer - 1)]
    outs = [
        sds((place.n_head, 3 * 128 + 16, rows), bf16),
        sds((rows, D), f32),
        sds((rows + 16, D) if below else (16, D), bf16),
        sds((D, rows) if below else (16, rows), bf16),
        sds((NH, rows), f32),
    ]
    scratch = [VMEM((group, D), bf16), VMEM((NH, group), f32), VMEM((NH, group), f32), VMEM((3 * D, rows), bf16)]
    return call(kernel, ins, outs, scratch, scalars, flops=60 * 10**9)


def mlp_weight_grads(place, scalars, blocks, normal_all, params, layer):
    group, rows, units = place.group, place.rows, place.units
    tile = min(512, group)

    def kernel(scal, *refs):
        gs = refs[: place.blocks]
        normal_ref, gain, shift, up, up_b, down, g_ref, up_out = refs[place.blocks : place.blocks + 8]
        (down_out,) = refs[place.blocks + 8 :]
        gain_l, shift_l = gain[layer : layer + 1], shift[layer : layer + 1]
        for slot in range(place.blocks):
            at = pl.multiple_of(place.position(scal, slot) * rows, rows)
            g_ref[pl.ds(at, rows)] = gs[slot][0:rows]

        def step(i, carry):
            up_t, down_g, bias, g_sum = carry
            at = pl.multiple_of(i * tile, tile)
            x = (normal_ref[pl.ds(at, tile)].astype(f32) * gain_l + shift_l).astype(bf16)
            g = g_ref[pl.ds(at, tile)]
            gate = dot(x, up[...]) + up_b[...]
            cdf = 0.5 * (1.0 + lax.erf(gate * math.sqrt(0.5)))
            pdf = jnp.exp(-0.5 * gate * gate) * (1.0 / math.sqrt(2.0 * math.pi))
            acted = (gate * cdf).astype(bf16)
            grad_gate = (dot_nt(g, down[...]) * (cdf + gate * pdf)).astype(bf16)
            up_t += dot(grad_gate.T, x)
            down_g += dot(acted.T, g)
            bias += jnp.sum(grad_gate.astype(f32), axis=0, keepdims=True)
            g_sum += jnp.sum(g.astype(f32), axis=0, keepdims=True)
            return up_t, down_g, bias, g_sum

        zero = jnp.zeros((units, D), f32)
        up_t, down_g, bias, g_sum = lax.fori_loop(
            0, group // tile, step, (zero, zero, jnp.zeros((1, units), f32), jnp.zeros((1, D), f32))
        )
        up_out[0:units] = up_t.astype(bf16)
        if units < 128:
            bias = jnp.concatenate([bias, jnp.zeros((1, 128 - units), f32)], axis=1)
        wide = jnp.concatenate([bias, jnp.zeros((1, D - 128), f32)], axis=1)
        row = lax.broadcasted_iota(jnp.int32, (32, D), 0)
        extra = jnp.where((row & 7) == 0, wide, jnp.where((row & 7) == 1, g_sum, 0.0))
        high, rest = split_low(extra)
        up_out[units : units + 32] = jnp.where(row < 8, high, jnp.where(row < 16, rest, jnp.zeros_like(rest)))
        for p in range(place.n_head):
            down_out[p] = down_g[:, 128 * p : 128 * p + 128].astype(bf16)

    up, up_b, down = params["units"][layer]
    made = call(
        kernel,
        [*blocks, normal_all, params["mlp_gain"], params["mlp_shift"], up, up_b, down],
        [sds((group, D), bf16), sds((units + 32, D), bf16), sds((place.n_head, units, 128), bf16)],
        (),
        scalars,
        flops=4 * 2 * group * D * units,
    )
    return made


def attention_weight_grads(place, scalars, pieces, mixed, normal_all, g_all, params, layer):
    rows, part, out_rows = place.rows, place.packed_rows, place.out_rows
    n_ctx, n_head = place.n_ctx, place.n_head
    block = rows * n_head
    cols = 3 * 128

    share, parts = place.share_rows, 2 if place.halves else 1

    def kernel(scal, *refs):
        pieces_ref, *mixed_refs = refs[: 1 + n_head]
        normal_far, g_far, gain, shift, mine_ref, other_ref = refs[1 + n_head : 7 + n_head]
        packed_t, mixed_t, total_ref, out_ref, extra_ref, bias_ref, full, normal_ref, g_ref, sems = refs[7 + n_head :]
        own_at = pl.multiple_of(scal[0] * block, block)
        copies = [
            pltpu.make_async_copy(far.at[pl.ds(own_at, block)], near, sems.at[k])
            for k, (far, near) in enumerate(((normal_far, normal_ref), (g_far, g_ref)))
        ]
        for copy in copies:
            copy.start()
        extra = jnp.zeros((16, 128), f32)
        for m in range(n_head):
            at = pl.multiple_of((scal[1] ^ m) * rows, rows)
            mixed_t[:, pl.ds(at, rows)] = mixed_refs[m][layer * D : layer * D + D]
            packed_t[:, m * rows : (m + 1) * rows] = pieces_ref[m, 0:cols]
            extra += pieces_ref[m, cols : cols + 16].astype(f32)
        for copy in copies:
            copy.wait()
        x = (normal_ref[...].astype(f32) * gain[layer : layer + 1] + shift[layer : layer + 1]).astype(bf16)
        total_ref[...] = dot(packed_t[...], x).astype(bf16)
        own_cols = pl.ds(pl.multiple_of(scal[1] * 128, 128), 128)
        out_ref[...] = dot(mixed_t[...], g_ref[:, own_cols]).astype(bf16)
        extra_ref[...] = extra[0:8] + extra[8:16]
        for c in range(n_ctx):
            bias = dot_nt(jnp.ones((16, block), bf16), packed_t[c * part : (c + 1) * part])[0:8]
            bias_ref[c] = jnp.concatenate([bias, jnp.zeros((8, 128 - part), f32)], axis=1)
        stats = extra_ref[4:5]
        row = lax.broadcasted_iota(jnp.int32, (32, D), 0)
        for c in range(n_ctx):
            full[c, 0:part] = total_ref[c * part : (c + 1) * part]
            for j in range(4):
                at = c * (D // n_ctx) + j * out_rows
                full[c, part : part + out_rows, 128 * j : 128 * j + 128] = out_ref[at : at + out_rows]
            quantity = extra_ref[c // (n_ctx // 4) : c // (n_ctx // 4) + 1]
            wide = jnp.concatenate([bias_ref[c][0:1], quantity, stats, jnp.zeros((1, 128), f32)], axis=1)
            high, rest = split_low(jnp.broadcast_to(wide, (32, D)))
            full[c, part + out_rows : share] = jnp.where(row < 8, high, rest)
            if place.halves:
                half = share // 2
                at = pl.multiple_of(scal[7] * half, half)
                mine_ref[c] = full[c, pl.ds(at, half)]
                other_ref[c] = full[c, pl.ds(pl.multiple_of(half - at, half), half)]
            else:
                mine_ref[c] = full[c]

    return call(
        kernel,
        [pieces, *mixed, Far(normal_all), Far(g_all), params["attn_gain"], params["attn_shift"]],
        [sds((n_ctx, share // parts, D), bf16), sds((n_ctx, share // 2, D), bf16)],
        [
            VMEM((cols, block), bf16),
            VMEM((D, block), bf16),
            VMEM((cols, D), bf16),
            VMEM((D, 128), bf16),
            VMEM((8, 128), f32),
            VMEM((n_ctx, 8, 128), f32),
            VMEM((n_ctx, share, D), bf16),
            VMEM((block, D), bf16),
            VMEM((block, D), bf16),
            pltpu.SemaphoreType.DMA((2,)),
        ],
        scalars,
        flops=2 * block * D * (cols + 128),
    )


def pack_mlp(place, scalars, up_share, pieces, halves):
    rows = 2 * place.units + 32
    half = rows // 2

    def kernel(scal, up_ref, pieces_ref, *refs):
        if halves:
            mine, other, full = refs
        else:
            (full,) = refs
        full[0 : place.units + 32] = up_ref[...]
        for p in range(place.n_head):
            full[place.units + 32 :, 128 * p : 128 * p + 128] = pieces_ref[p]
        if halves:
            at = pl.multiple_of(scal[7] * half, half)
            mine[...] = full[pl.ds(at, half)]
            other[...] = full[pl.ds(pl.multiple_of(half - at, half), half)]

    outs = [sds((half, D), bf16)] * 2 if halves else [sds((rows, D), bf16)]
    scratch = [VMEM((rows, D), bf16)] if halves else []
    return call(kernel, [up_share, pieces], outs, scratch, scalars, flops=10**7)


def along_lanes(rows, width):
    if width == 128:
        return jnp.concatenate(rows, axis=1)
    full = len(rows) * width
    out = jnp.zeros((8, full), f32)
    for k, row in enumerate(rows):
        lane = lax.broadcasted_iota(jnp.int32, (8, full), 1)
        row = jnp.concatenate([row, jnp.zeros((1, full - 128), f32)], axis=1)
        row = jnp.where(lane < width, jnp.broadcast_to(row, (8, full)), 0.0)
        out += pltpu.roll(row, k * width, 1) if k else row
    return out[0:1]


def whole_shares(place, scal, refs, at, size, full, halves):
    if not halves:
        return [x.at[at : at + size] for x in refs]
    half = size // 2
    for s in range(place.n_ctx):
        full[s, pl.ds(pl.multiple_of(scal[7] * half, half), half)] = refs[s][at : at + half]
        start = s * half
        full[s, pl.ds(pl.multiple_of((1 - scal[7]) * half, half), half)] = refs[-1][start : start + half]
    return [full.at[s] for s in range(place.n_ctx)]


def place_mlp(place, scalars, shares, layer, into):
    n_ctx, units = place.n_ctx, place.units
    taken = 0 if into is None else 2
    halves = len(shares) > n_ctx
    rows = 2 * units + 32

    def kernel(scal, *refs):
        up_out, down_out, small_out, up_t, bias_rows, full = refs[len(shares) + taken :]
        srcs = whole_shares(place, scal, refs[: len(shares)], 0, rows, full, halves)
        for s in range(n_ctx):
            c = lax.rem(scal[0] - s + n_ctx, n_ctx)
            at = pl.multiple_of(c * units, units)
            up_t[pl.ds(at, units)] = srcs[s][0:units].astype(f32)
            extra = srcs[s][units : units + 16].astype(f32)
            extra = extra[0:8] + extra[8:16]
            bias_rows[c] = jnp.broadcast_to(extra[0:1, :128], (8, 128))
            if s == 0:
                small_out[...] = jnp.zeros_like(small_out)
                for q in range(place.n_head):

                    @pl.when(scal[1] == q)
                    def _():
                        small_out[1:2, 0:128] = extra[1:2, 128 * q : 128 * q + 128]

            for p in range(place.n_head):
                at = pl.multiple_of(p * (FF // place.n_head) + c * units, units)
                down_out[pl.ds(at, units)] = srcs[s][units + 32 : rows, 128 * p : 128 * p + 128].astype(f32)
        up_out[...] = up_t[...].T
        small_out[0:1] = along_lanes([bias_rows[c][0:1] for c in range(n_ctx)], units)

    wide = FF // place.n_head
    return call(
        kernel,
        shares,
        [
            (sds((LAYERS, D, wide), f32), layer),
            (sds((LAYERS, FF, 128), f32), layer),
            sds((8, wide), f32),
        ],
        [VMEM((wide, D), f32), VMEM((n_ctx, 8, 128), f32), VMEM((n_ctx, rows, D) if halves else (1, 16, D), bf16)],
        scalars,
        flops=10**7,
        into=into,
    )


def place_attention(place, scalars, shares, at_row, layer, into, smalls=None, count=1):
    n_ctx, part, out_rows = place.n_ctx, place.packed_rows, place.out_rows
    taken = 0 if into is None else 2
    halves = place.halves
    rows = place.share_rows
    wide = 3 * D // place.n_head
    wide_up = FF // place.n_head
    given = [] if smalls is None else smalls

    def kernel(scal, *refs):
        shares_in, given_in = refs[: len(shares)], refs[len(shares) : len(shares) + len(given)]
        qkv_out, out_out, *small_outs, qkv_t, info, small, full = refs[len(shares) + len(given) + taken :]
        srcs = whole_shares(place, scal, shares_in, at_row, rows, full, halves)
        small[...] = jnp.zeros_like(small)
        for s in range(n_ctx):
            c = lax.rem(scal[0] - s + n_ctx, n_ctx)
            at = pl.multiple_of(c * part, part)
            qkv_t[pl.ds(at, part)] = srcs[s][0:part].astype(f32)
            for j in range(4):
                at = pl.multiple_of(c * (D // n_ctx) + j * out_rows, out_rows)
                out_out[pl.ds(at, out_rows)] = srcs[s][part : part + out_rows, 128 * j : 128 * j + 128].astype(f32)
            extra = srcs[s][part + out_rows : part + out_rows + 16].astype(f32)
            info[c] = extra[0:8] + extra[8:16]
        qkv_out[...] = qkv_t[...].T
        for k in range(4):
            small[k : k + 1, 0:128] = info[k * (n_ctx // 4), 0:1, 128:256]
        small[4:5, 0:128] = info[0, 0:1, 256:384]
        small[5:6] = along_lanes([info[c, 0:1, 0:128] for c in range(n_ctx)], part)
        if smalls is None:
            small_outs[0][...] = small[...]
            return
        attn_1, mlp_0, mlp_1 = given_in
        lane = lane_of(1)
        for spot, attn, mlp in ((0, small, mlp_0), (1, attn_1, mlp_1)):
            row = slice(spot, spot + 1)
            for k in range(4):
                small_outs[k][row] = attn[k : k + 1, 0:128]
            small_outs[4][row] = attn[5:6]
            small_outs[5][row] = mlp[0:1]
            small_outs[6][row] = mlp[1:2, 0:128]
            small_outs[7][row] = mlp[1:2, 0:128]
            for k in range(3):
                picked = jnp.where((lane & 3) == k, attn[4:5, 0:128], 0.0)
                small_outs[8][row, k : k + 1] = jnp.sqrt(jnp.sum(picked, axis=1, keepdims=True) * (1.0 / count))

    if smalls is None:
        outs = [sds((8, wide), f32)]
    else:
        widths = [128, 128, 128, 128, wide, wide_up, 128, 128, 3]
        outs = [sds((LAYERS, width), f32) for width in widths]
    return call(
        kernel,
        [*shares, *given],
        [(sds((LAYERS, D, wide), f32), layer), (sds((LAYERS, D, 128), f32), layer), *outs],
        [
            VMEM((wide, D), f32),
            VMEM((n_ctx, 8, D), f32),
            VMEM((8, wide), f32),
            VMEM((n_ctx, rows, D) if halves else (1, 16, D), bf16),
        ],
        scalars,
        flops=10**7,
        into=into,
    )


def prepare(place, lengths, qkv_weight, qkv_bias):
    group = place.group
    blocks = group // 128
    dim = jnp.arange(128, dtype=jnp.int32)[None, :] % HD
    freq = rope_base ** (-2.0 * (dim % (ROT // 2)).astype(f32) / ROT)
    starts = jnp.concatenate([jnp.zeros((1,), jnp.int32), lengths[0, :3]])
    starts = jnp.stack([starts[0], starts[1], starts[1] + starts[2], starts[1] + starts[2] + starts[3]])
    first = (jnp.arange(blocks, dtype=jnp.int32)[:, None] * 128 - starts[None, :]).reshape(-1, 1)
    whole = jnp.concatenate([first, jnp.arange(128, dtype=jnp.int32)[:, None]], axis=0).astype(f32) * freq
    cosines, sines = jnp.cos(whole), jnp.sin(whole)
    base = 4 * blocks

    def kernel(scal, w_ref, b_ref, cos_ref, sin_ref, w_out, b_out, cos_t, left_t, right_t, own_t):
        def sort(read, write):
            for p in range(PAIRS):
                a, b, c = (read(slice(128 * (3 * p + i), 128 * (3 * p + i) + 128)).astype(f32) for i in range(3))
                first = lane_of(a.shape[0]) < HD
                made = (jnp.where(first, a, b), pltpu.roll(jnp.where(first, c, a), HD, 1), jnp.where(first, b, c))
                for j in range(3):
                    write(slice(j * D + 128 * p, j * D + 128 * p + 128), made[j])

        for layer in range(LAYERS):

            def store(to, x, layer=layer):
                w_out[layer, :, to] = x.astype(bf16)

            sort(lambda at, layer=layer: w_ref[layer, :, at], store)

        def store_bias(to, x):
            b_out[:, to] = x

        sort(lambda at: b_ref[:, at], store_bias)
        ends = place.ends(scal)
        dim = lane_of(128) & (HD - 1)
        cos_b, sin_b = cos_ref[base : base + 128], sin_ref[base : base + 128]

        def table(i, _):
            at = pl.multiple_of(i * 128, 128)
            t = at + lax.broadcasted_iota(jnp.int32, (128, 1), 0)
            cos_a, sin_a = cos_ref[pl.ds(4 * i, 1)], sin_ref[pl.ds(4 * i, 1)]
            for k in range(1, 4):
                later = t >= ends[k - 1]
                cos_a = jnp.where(later, cos_ref[pl.ds(4 * i + k, 1)], cos_a)
                sin_a = jnp.where(later, sin_ref[pl.ds(4 * i + k, 1)], sin_a)
            cosine = cos_a * cos_b - sin_a * sin_b
            sine = sin_a * cos_b + cos_a * sin_b
            cos_t[pl.ds(at, 128)] = jnp.where(dim < ROT, cosine, 1.0)
            left_t[pl.ds(at, 128)] = jnp.where(dim < ROT // 2, -sine, 0.0)
            right_t[pl.ds(at, 128)] = jnp.where((dim >= ROT // 2) & (dim < ROT), sine, 0.0)
            return 0

        lax.fori_loop(0, blocks, table, 0)
        own_at = pl.multiple_of(scal[2] * place.rows, place.rows)
        for k, ref in enumerate((cos_t, left_t, right_t)):
            own_t[k * place.rows : (k + 1) * place.rows] = ref[pl.ds(own_at, place.rows)]

    bias = jnp.concatenate([qkv_bias, jnp.zeros((8 - LAYERS, 3 * D), f32)], axis=0)
    made = call(
        kernel,
        [qkv_weight, bias, cosines, sines],
        [sds(qkv_weight.shape, bf16), sds((8, 3 * D), f32), *[sds((group, 128), f32)] * 3, sds((3 * place.rows, 128), f32)],
        (),
        lengths,
        flops=10**7,
    )
    return made[0], made[1], made[2:5], made[5]


def tie(x, *after):
    return lax.optimization_barrier((x, *after))[0] if after else x


def flip_heads(x, flip):
    return lax.ppermute(x, "head", [(i, i ^ flip) for i in range(lax.axis_size("head"))])


def turn_ctx(x, shift):
    n = lax.axis_size("ctx")
    return lax.ppermute(x, "ctx", [(i, (i + shift) % n) for i in range(n)])


def gather_rings(own):
    return [own] + [turn_ctx(own, s) for s in range(1, lax.axis_size("ctx"))]


def gather_flips(rings, flip, *after):
    return [flip_heads(tie(x, *after), flip) for x in rings]


def by_slot(rings, far, near, far_near):
    return [x for four in zip(rings, near, far, far_near) for x in four]


def with_flip(own, flip):
    return jnp.concatenate([own, flip_heads(own, flip)], axis=0)


def swap_dp(x):
    return lax.ppermute(x, "dp", [(0, 1), (1, 0)])


def per_device(
    hidden_in,
    lengths,
    attn_gain,
    attn_shift,
    mlp_gain,
    mlp_shift,
    qkv_weight,
    qkv_bias,
    out_weight,
    out_bias,
    up_weight,
    up_bias,
    down_weight,
    down_bias,
    cotangent,
):
    rows = hidden_in.shape[0]
    n_dp, n_ctx, n_head = (lax.axis_size(a) for a in ("dp", "ctx", "head"))
    place = Place(n_dp, n_ctx, n_head, rows)
    group = place.group
    scalars = lengths
    qkv_sorted, qkv_bias_sorted, tables, own_tables = prepare(place, lengths, qkv_weight, qkv_bias)
    params = {
        "attn_gain": attn_gain,
        "attn_shift": attn_shift,
        "mlp_gain": mlp_gain,
        "mlp_shift": mlp_shift,
        "qkv_sorted": qkv_sorted,
        "qkv_bias_sorted": qkv_bias_sorted,
        "out_weight": out_weight,
        "out_bias": out_bias,
        "up_weight": up_weight,
        "up_bias": up_bias,
        "down_weight": down_weight,
        "down_bias": down_bias,
    }
    units = place.units
    at = lax.axis_index("head") * (FF // n_head) + lax.axis_index("ctx") * units
    params["units"] = [
        (
            lax.dynamic_slice(up_weight, (layer, 0, at), (1, D, units))[0],
            lax.dynamic_slice(up_bias, (layer, at), (1, units)),
            lax.dynamic_slice(down_weight, (layer, at, 0), (1, units, D))[0],
        )
        for layer in range(LAYERS)
    ]
    def attention(layer, blocks, hidden, mlp_out, last_grad):
        names = ("normal_all", "k_all", "v_all", "q_own", "kv_own", "mixed", "mixed_low", "log", "delta", "dmix", "h_out", "stats", "low")
        made = attention_forward(place, scalars, blocks, tables, params, layer, hidden, mlp_out, last_grad)
        return dict(zip(names, made), hidden=hidden)

    def backward_queries(layer, kept):
        return query_backward(place, scalars, tables, own_tables, params, layer, kept)

    def backward_keys(layer, g_all, stats, kept, queries, grad, grad_mlp_in, below):
        return key_backward(
            place, scalars, g_all, stats, own_tables, params, layer, kept, queries, grad, grad_mlp_in, below
        )

    def head_swap(pieces):
        return lax.all_to_all(pieces, "head", 0, 0, tiled=True)

    def head_gather(x):
        return [x] + [flip_heads(x, m) for m in range(1, n_head)]

    def reduce_mlp(up_share, pieces, halves):
        made = pack_mlp(place, scalars, up_share, pieces, halves)
        if n_dp == 2:
            return (made[0].astype(f32) + swap_dp(made[-1]).astype(f32)).astype(bf16)
        return lax.psum(made[0], "dp")

    def reduce_attn(mine, other, *after):
        if n_dp == 2:
            summed = (mine.astype(f32) + swap_dp(other).astype(f32)).astype(bf16)
        else:
            summed = lax.psum(mine, "dp")
        parts = lax.all_to_all(tie(summed, *after), "ctx", 0, 0, tiled=True)
        return jnp.sum(parts.astype(f32), axis=0).astype(bf16)

    def finish(rings, at=0):
        return [*rings, swap_dp(jnp.concatenate([x[at:] for x in rings], axis=0))] if n_dp == 2 else rings

    rings = gather_rings(hidden_in)
    mlp_0, factor_0, _ = mlp_forward(hidden_in, params, 0)
    sliced = [x for made in params["units"] for x in made]
    far = [flip_heads(hidden_in, 2)] + gather_flips(rings[1:], 2, mlp_0)
    near, far_near = gather_flips(rings, 1), gather_flips(far, 1, qkv_sorted)
    cot_rings = gather_rings(tie(cotangent, *near, *far_near))
    first = attention(0, by_slot(rings, far, near, far_near), hidden_in, mlp_0, None)
    hidden = first["h_out"]
    low = tie(first["low"], *cot_rings)
    rings = gather_rings(low)
    mlp_1, factor_1, _ = mlp_forward(hidden, params, 1)
    back_1 = mlp_backward(tie(cotangent, mlp_1), factor_1, hidden, params, 1)
    far = [flip_heads(low, 2)] + gather_flips(rings[1:], 2, back_1)
    near, far_near = gather_flips(rings, 1), gather_flips(far, 1)
    cot_far = gather_flips(cot_rings, 2, *near, *far_near)
    second = attention(1, by_slot(rings, far, near, far_near), hidden, mlp_1, [cotangent, first["mixed_low"]])
    output_rows = second["h_out"]

    low = tie(second["low"], *cot_far)
    cot_near, cot_far_near = gather_flips(cot_rings, 1, low), gather_flips(cot_far, 1, low)
    pair = with_flip(low, 1)
    cot_all, up_share_1, pieces_1 = mlp_weight_grads(
        place,
        scalars,
        by_slot([tie(cot_rings[0], pair), *cot_rings[1:]], cot_far, cot_near, cot_far_near),
        second["normal_all"],
        params,
        1,
    )
    four = with_flip(pair, 2)
    stats = gather_rings(four)
    queries_1 = backward_queries(1, dict(second, delta=tie(second["delta"], four, up_share_1)))
    stats[0] = tie(stats[0], *queries_1)
    mixed = head_gather(tie(second["mixed_low"], *stats, cot_all))
    pieces_1 = head_swap(tie(pieces_1, *stats))
    packed_1, grad, payload, dmix, delta = backward_keys(1, cot_all, stats, second, queries_1, cotangent, back_1, first)
    first["dmix"], first["delta"] = dmix, delta
    payload = tie(payload, pieces_1, *mixed)
    rings = gather_rings(payload)
    packed_1 = head_swap(packed_1)
    back_0 = mlp_backward(grad, factor_0, hidden_in, params, 0)
    far = [flip_heads(payload, 2)] + gather_flips(rings[1:], 2, back_0)
    queries_0 = backward_queries(0, dict(first, delta=tie(delta, back_0, *rings)))
    near, far_near = gather_flips(rings, 1), gather_flips(far, 1, *queries_0)
    blocks = by_slot(rings, far, near, far_near)
    mlp_share_1 = reduce_mlp(tie(up_share_1, *far), pieces_1, False)
    g_all, up_share_0, pieces_0 = mlp_weight_grads(place, scalars, blocks, first["normal_all"], params, 0)
    mlp_rings_1 = gather_rings(tie(mlp_share_1, g_all))
    pieces_0 = head_swap(pieces_0)
    packed_0, grad, _, _, _ = backward_keys(0, g_all, blocks, first, queries_0, grad, back_0, None)
    packed_0 = head_swap(tie(packed_0, pieces_0, *mlp_rings_1))
    mine_1, other_1 = attention_weight_grads(
        place, scalars, tie(packed_1, grad), mixed, second["normal_all"], cot_all, params, 1
    )
    half_0 = reduce_mlp(tie(up_share_0, mine_1), pieces_0, n_dp == 2)
    mine_0, other_0 = attention_weight_grads(
        place, scalars, tie(packed_0, half_0), mixed, first["normal_all"], g_all, params, 0
    )
    attn_share_1 = reduce_attn(mine_1, other_1)
    mlp_rings_0 = gather_rings(half_0)
    attn_share_0 = reduce_attn(mine_0, other_0, attn_share_1)
    attn_rings_1 = gather_rings(attn_share_1)
    *big, mlp_small_1 = place_mlp(place, scalars, mlp_rings_1, 1, None)
    attn_rings_0 = gather_rings(tie(attn_share_0, mlp_small_1))
    mlp_shares_0 = finish(mlp_rings_0)
    attn_shares_1 = finish(attn_rings_1)
    *attn_big, attn_small_1 = place_attention(place, scalars, attn_shares_1, 0, 1, None)
    *big, mlp_small_0 = place_mlp(place, scalars, mlp_shares_0, 0, big)
    attn_shares_0 = finish(attn_rings_0)
    qkv_grad, out_grad, gain, shift, mlp_g, mlp_s, qkv_b, up_b, down_b, out_b, layer_stats = place_attention(
        place, scalars, attn_shares_0, 0, 0, attn_big, [attn_small_1, mlp_small_0, mlp_small_1], group * n_dp * D
    )
    up_grad, down_grad = big
    return (
        output_rows, grad, gain, shift, mlp_g, mlp_s, qkv_grad, qkv_b, out_grad, out_b, up_grad, up_b, down_grad, down_b, layer_stats
    )


def solution(mesh):
    rows = P(("dp", "ctx", "head"), None)
    return jax.shard_map(
        per_device,
        mesh=mesh,
        in_specs=(rows, P("dp", None), *([P()] * 12), rows),
        out_specs=(
            rows,
            rows,
            P(None, "head"),
            P(None, "head"),
            P(None, "head"),
            P(None, "head"),
            P(None, None, "head"),
            P(None, "head"),
            P(None, None, "head"),
            P(None, "head"),
            P(None, None, "head"),
            P(None, "head"),
            P(None, None, "head"),
            P(None, "head"),
            P(),
        ),
        check_vma=False,
    )
```

```python
import math

import jax
import jax.numpy as jnp
from jax import lax
from jax.experimental import pallas as pl
from jax.experimental.pallas import tpu as pltpu
from jax.sharding import PartitionSpec as P

D = 512
FF = 2048
NH = 8
HD = 64
ROT = 16
LAYERS = 2
PAIRS = NH // 2
epsilon = 1e-05
masked_value = -1e30
score_scale = 0.125
rope_base = 10000.0
f32 = jnp.float32
bf16 = jnp.bfloat16
STEP = 1024
VMEM = pltpu.VMEM


def dot(a, b):
    return lax.dot_general(a, b, (((1,), (0,)), ((), ())), preferred_element_type=f32)


def dot_nt(a, b):
    return lax.dot_general(a, b, (((1,), (1,)), ((), ())), preferred_element_type=f32)


def norm_parts(hidden):
    centred = hidden - jnp.mean(hidden, axis=-1, keepdims=True)
    inverse = lax.rsqrt(jnp.mean(centred * centred, axis=-1, keepdims=True) + epsilon)
    return centred * inverse, inverse


def rope(x, cos_t, left_t, right_t):
    return x * cos_t + pltpu.roll(x, 128 - 8, 1) * left_t + pltpu.roll(x, 8, 1) * right_t


def start_of(place, ends):
    start = jnp.zeros_like(place)
    for end in ends:
        start = jnp.where(end <= place, end, start)
    return start


def end_of(place, ends, size):
    found = jnp.int32(size)
    for end in reversed(ends):
        found = jnp.where(place < end, end, found)
    return found


def split_low(x):
    high = x.astype(bf16)
    return high, (x - high.astype(f32)).astype(bf16)


def lane_of(rows):
    return lax.broadcasted_iota(jnp.int32, (rows, 128), 1)


def two_heads(x):
    first = lane_of(x.shape[0]) < HD
    zero = jnp.zeros_like(x)
    return jnp.concatenate([jnp.where(first, x, zero), jnp.where(first, zero, x)], axis=0)


def one_pair(x):
    rows = x.shape[0] // 2
    return jnp.where(lane_of(rows) < HD, x[:rows], x[rows:])


def dot_tn(a, b):
    return lax.dot_general(a, b, (((0,), (0,)), ((), ())), preferred_element_type=f32)


def two_heads_t(x):
    first = lax.broadcasted_iota(jnp.int32, x.shape, 0) < HD
    zero = jnp.zeros_like(x)
    return jnp.concatenate([jnp.where(first, x, zero), jnp.where(first, zero, x)], axis=1)


def one_pair_t(x):
    rows = x.shape[1] // 2
    return jnp.where(lax.broadcasted_iota(jnp.int32, (128, rows), 0) < HD, x[:, :rows], x[:, rows:])


def rope_t(x, cos_t, left_t, right_t):
    return x * cos_t + pltpu.roll(x, 128 - 8, 0) * left_t + pltpu.roll(x, 8, 0) * right_t


class Far:
    def __init__(self, array):
        self.array = array


class Lazy:
    def __init__(self, array, at=None, shape=None):
        self.array, self.at = array, at or (lambda ref: ref)
        self.shape = shape or array.shape


class Out:
    def __init__(self, shape, dtype):
        self.shape, self.dtype = shape, dtype


class Coming:
    def __init__(self, ref, copy):
        self.ref, self.copy, self.there = ref, copy, False

    def get(self):
        if not self.there:
            self.copy.wait()
            self.there = True
        return self.ref


class Going:
    def __init__(self, ref, copy):
        self.ref, self.copy, self.gone = ref, copy, False

    def send(self):
        self.copy.start()
        self.gone = True


def call(kernel, ins, outs, scratch=(), scalars=None, vmem=60 << 20, flops=10**9, into=None):
    specs, arrays = [], []

    def block(shape, layer, cols=None):
        place = (layer, *([0] * (len(shape) - 1)))
        return pl.BlockSpec((None, *shape[1:-1], cols or shape[-1]), lambda i: place)

    def whole(shape):
        return pl.BlockSpec(shape, lambda i: (0,) * len(shape))

    n_ins, n_outs = len(ins), len(outs)
    lead = 0
    if scalars is not None:
        specs.append(pl.BlockSpec(memory_space=pltpu.SMEM))
        arrays.append(scalars)
        lead = 1
    for item in ins:
        if isinstance(item, (Far, Lazy)):
            specs.append(pl.BlockSpec(memory_space=pl.ANY))
            arrays.append(item.array)
            continue
        array = item[0] if isinstance(item, tuple) else item
        specs.append(block(array.shape, *item[1:]) if isinstance(item, tuple) else whole(array.shape))
        arrays.append(array)
    aliases = {}
    if into is not None:
        spots = [k for k, o in enumerate(outs) if isinstance(o, tuple)]
        for spot, array in zip(spots, into):
            aliases[len(arrays)] = spot
            specs.append(pl.BlockSpec(memory_space=pl.ANY))
            arrays.append(array)
    shapes, out_specs = [], []
    for o in outs:
        if isinstance(o, tuple):
            shapes.append(o[0])
            out_specs.append(block(o[0].shape, o[1]))
        elif isinstance(o, Out):
            shapes.append(sds(o.shape, o.dtype))
            out_specs.append(pl.BlockSpec(memory_space=pl.ANY))
        else:
            shapes.append(o)
            out_specs.append(whole(o.shape))
    coming = [k for k, item in enumerate(ins) if isinstance(item, Lazy)]
    going = [k for k, o in enumerate(outs) if isinstance(o, Out)]
    slow = [VMEM(ins[k].shape, ins[k].array.dtype) for k in coming] + [VMEM(outs[k].shape, outs[k].dtype) for k in going]
    if slow:
        slow.append(pltpu.SemaphoreType.DMA((len(slow),)))

    def body(*refs):
        refs = list(refs)
        given = []
        if scalars is not None:
            lengths_ref = refs.pop(0)
            ctx, head = lax.axis_index("ctx"), lax.axis_index("head")
            ends = [lengths_ref[0, 0]]
            for k in range(1, 4):
                ends.append(ends[-1] + lengths_ref[0, k])
            given = [[ctx, head, ctx * lax.axis_size("head") + head, *ends, lax.axis_index("dp")]]
        finals = []
        if slow:
            extra = refs[len(refs) - len(slow) :]
            refs = refs[: len(refs) - len(slow)]
            sems = extra[-1]
            for j, k in enumerate(coming):
                copy = pltpu.make_async_copy(ins[k].at(refs[k]), extra[j], sems.at[j])
                copy.start()
                refs[k] = Coming(extra[j], copy)
            first_out = len(arrays) - lead
            for j, k in enumerate(going):
                j += len(coming)
                refs[first_out + k] = Going(extra[j], pltpu.make_async_copy(extra[j], refs[first_out + k], sems.at[j]))
                finals.append(refs[first_out + k])
        kernel(*given, *refs)
        for item in finals:
            if not item.gone:
                item.send()
        for item in finals:
            item.copy.wait()

    moved = sum(x.size * x.dtype.itemsize for x in arrays)
    return pl.pallas_call(
        body,
        grid=(1,),
        in_specs=specs,
        out_specs=out_specs,
        out_shape=shapes,
        scratch_shapes=[*scratch, *slow],
        input_output_aliases=aliases,
        compiler_params=pltpu.CompilerParams(vmem_limit_bytes=vmem),
        cost_estimate=pl.CostEstimate(flops=flops, bytes_accessed=moved, transcendentals=0),
    )(*arrays)


def lazy_layer(array, layer, cols=None):
    if cols is None:
        return Lazy(array, lambda ref: ref.at[layer], array.shape[1:])
    return Lazy(array, lambda ref: ref.at[layer, :, 0:cols], (*array.shape[1:-1], cols))


def sds(shape, dtype):
    return jax.ShapeDtypeStruct(shape, dtype)


def mlp_forward(hidden, params, layer):
    rows = hidden.shape[0]

    def kernel(h_ref, gain, shift, up, up_b, down, down_b, out_ref, factor_ref, normal_ref):
        normal, _ = norm_parts(h_ref[...].astype(f32))
        normal_ref[...] = normal.astype(bf16)
        x = (normal * gain[layer : layer + 1] + shift[layer : layer + 1]).astype(bf16)
        total = jnp.zeros((rows, D), f32)
        for j in range(0, FF, 512):
            gate = dot(x, up[:, j : j + 512]) + up_b[layer : layer + 1, j : j + 512]
            cdf = 0.5 * (1.0 + lax.erf(gate * math.sqrt(0.5)))
            pdf = jnp.exp(-0.5 * gate * gate) * (1.0 / math.sqrt(2.0 * math.pi))
            factor_ref[:, j : j + 512] = cdf + gate * pdf
            total += dot((gate * cdf).astype(bf16), down[j : j + 512])
        out_ref[...] = total + down_b[layer : layer + 1]

    return call(
        kernel,
        [
            hidden,
            params["mlp_gain"],
            params["mlp_shift"],
            (params["up_weight"], layer),
            params["up_bias"],
            (params["down_weight"], layer),
            params["down_bias"],
        ],
        [sds((rows, D), f32), sds((rows, FF), f32), sds((rows, D), bf16)],
        flops=2 * 2 * rows * D * FF,
    )


class Place:
    def __init__(self, n_dp, n_ctx, n_head, rows):
        self.n_ctx, self.n_head, self.rows = n_ctx, n_head, rows
        self.halves = n_dp == 2
        self.blocks = n_ctx * n_head
        self.group = self.blocks * rows
        self.units = FF // self.blocks
        self.packed_rows = 3 * D // self.blocks
        self.mixed_rows = D // self.blocks

    def position(self, scal, slot):
        shift, flip = slot // self.n_head, slot % self.n_head
        ctx = lax.rem(scal[0] - shift + self.n_ctx, self.n_ctx)
        return ctx * self.n_head + (scal[1] ^ flip)

    def ends(self, scal):
        return [scal[3 + k] for k in range(4)]


def delta_rows(grad_mixed_t, mixed_t):
    return jnp.concatenate(
        [
            jnp.sum(grad_mixed_t[n * HD : (n + 1) * HD].astype(f32) * mixed_t[n * HD : (n + 1) * HD], axis=0, keepdims=True)
            for n in range(NH)
        ],
        axis=0,
    )


def stat_payload(logs, deltas):
    parts = [*split_low(logs), *split_low(deltas)]
    top = jnp.concatenate(parts, axis=1)
    return jnp.concatenate([top, jnp.zeros_like(top)], axis=0)


def attention_forward(place, scalars, blocks, tables, params, layer, hidden, mlp_out, last_grad):
    rows, group = place.rows, place.group
    first_layer = layer == 0
    last = last_grad is not None
    tile = min(512, group)

    def kernel(scal, *refs):
        refs = list(refs)
        xs = [refs.pop(0) for _ in range(place.blocks)]
        cos_t, left_t, right_t, gain, shift, w, b, out_w, out_b, h_ref, mlp_ref = refs[:11]
        refs = refs[11:]
        g_ref, below_ref = (refs.pop(0), refs.pop(0)) if last else (None, None)
        (normal_out, k_out, v_out, q_own, kv_own, mixed_ref, mixed_low_ref, log_ref, delta_ref, dmix_ref, h_out, stats_ref, low_ref) = refs[:13]
        a_all = refs[13]
        normal_all, k_all, v_all = normal_out.ref, k_out.ref, v_out.ref
        own_at = pl.multiple_of(scal[2] * rows, rows)
        ends = place.ends(scal)
        gain_l, shift_l = gain[layer : layer + 1], shift[layer : layer + 1]
        for slot in range(place.blocks):
            at = pl.multiple_of(place.position(scal, slot) * rows, rows)
            x = xs[slot][...].astype(f32)
            normal = norm_parts(x)[0] if first_layer else x
            normal_all[pl.ds(at, rows)] = normal.astype(bf16)
            a_all[pl.ds(at, rows)] = (normal * gain_l + shift_l).astype(bf16)
        normal_out.send()
        w, cos_t, left_t, right_t = (x.get() for x in (w, cos_t, left_t, right_t))

        def project(i, _):
            at = pl.multiple_of(i * tile, tile)
            k = dot(a_all[pl.ds(at, tile)], w[:, D : 2 * D]) + b[layer : layer + 1, D : 2 * D]
            tabs = [t[pl.ds(at, tile)] for t in (cos_t, left_t, right_t)]
            for p in range(PAIRS):
                k_all[pl.ds(at, tile), 128 * p : 128 * p + 128] = rope(k[:, 128 * p : 128 * p + 128], *tabs).astype(bf16)
            v = dot(a_all[pl.ds(at, tile)], w[:, 2 * D :]) + b[layer : layer + 1, 2 * D :]
            v_all[pl.ds(at, tile)] = v.astype(bf16)
            return 0

        first_key = start_of(own_at, ends)
        low, high = first_key // STEP, (own_at + rows - 1) // STEP + 1
        lax.fori_loop(low * (STEP // tile), high * (STEP // tile), project, 0)
        k_out.send()
        v_out.send()
        kv_own[0:rows], kv_own[rows : 2 * rows] = k_all[pl.ds(own_at, rows)], v_all[pl.ds(own_at, rows)]
        q = dot(a_all[pl.ds(own_at, rows)], w[:, :D]) + b[layer : layer + 1, :D]
        tabs = [t[pl.ds(own_at, rows)] for t in (cos_t, left_t, right_t)]
        for p in range(PAIRS):
            turned = rope(q[:, 128 * p : 128 * p + 128], *tabs).astype(bf16)
            q_own[:, 128 * p : 128 * p + 128] = turned * jnp.asarray(score_scale, bf16)
        t = own_at + lax.broadcasted_iota(jnp.int32, (1, rows), 1)
        start = start_of(t, ends)
        doubled = [two_heads(q_own[:, 128 * p : 128 * p + 128]) for p in range(PAIRS)]

        def attend(i, carry):
            at = pl.multiple_of(i * STEP, STEP)
            s_at = at + lax.broadcasted_iota(jnp.int32, (STEP, 1), 0)
            bias = jnp.where((s_at >= start) & (s_at <= t), 0.0, masked_value)
            bias = jnp.concatenate([bias, bias], axis=1)
            new = []
            for p in range(PAIRS):
                most, total, acc = carry[p]
                scores = dot_nt(k_all[pl.ds(at, STEP), 128 * p : 128 * p + 128], doubled[p]) + bias
                newest = jnp.maximum(most, jnp.max(scores, axis=0, keepdims=True))
                chance = jnp.exp(scores - newest)
                scale = jnp.exp(most - newest)
                total = total * scale + jnp.sum(chance, axis=0, keepdims=True)
                acc = acc * scale + dot_tn(v_all[pl.ds(at, STEP), 128 * p : 128 * p + 128], chance.astype(bf16))
                new.append((newest, total, acc))
            return tuple(new)

        begin = tuple(
            (jnp.full((1, 2 * rows), masked_value, f32), jnp.zeros((1, 2 * rows), f32), jnp.zeros((128, 2 * rows), f32))
            for _ in range(PAIRS)
        )
        done = lax.fori_loop(low, high, attend, begin)
        logs = []
        for p in range(PAIRS):
            most, total, acc = done[p]
            mixed_ref[128 * p : 128 * p + 128] = one_pair_t(acc / total)
            log = most + jnp.log(total)
            logs += [log[:, :rows], log[:, rows:]]
        log_rows = jnp.concatenate(logs, axis=0)
        log_ref[...] = log_rows
        mixed_low = mixed_ref[...].astype(bf16)
        if last:
            size = place.mixed_rows
            for p in range(place.n_head):
                for c in range(place.n_ctx):
                    at = 128 * p + size * c
                    mixed_low_ref[c * place.n_head + p, 0:size] = below_ref[at : at + size]
                    mixed_low_ref[c * place.n_head + p, size : 2 * size] = mixed_low[at : at + size]
        else:
            mixed_low_ref[...] = mixed_low
        out_w = out_w.get()
        attn_out = dot_tn(mixed_low, out_w[...]) + out_b[layer : layer + 1]
        h = h_ref.get()[...].astype(f32)
        mlp = mlp_ref.get()[...]
        result = h + attn_out + mlp
        lane = lane_of(8)
        sums = [jnp.sum(jnp.sum(v * v, axis=1, keepdims=True), axis=0, keepdims=True) for v in (h, attn_out, mlp)]
        stats_ref[...] = jnp.where(lane == 0, sums[0], jnp.where(lane == 1, sums[1], jnp.where(lane == 2, sums[2], 0.0)))
        if last:
            h_out[...] = result.astype(bf16)
            dmix = dot_nt(out_w[...], g_ref[...]).astype(bf16)
            dmix_ref[...] = dmix
            deltas = delta_rows(dmix, mixed_ref[...])
            delta_ref[...] = deltas
            low_ref[...] = stat_payload(log_rows, deltas)
        else:
            h_out[...] = result
            low_ref[...] = norm_parts(result)[0].astype(bf16)
            dmix_ref[...] = jnp.zeros_like(dmix_ref)
            delta_ref[...] = jnp.zeros_like(delta_ref)

    ins = [
        *blocks,
        *[Lazy(x) for x in tables],
        params["attn_gain"],
        params["attn_shift"],
        lazy_layer(params["qkv_sorted"], layer),
        params["qkv_bias_sorted"],
        lazy_layer(params["out_weight"], layer),
        params["out_bias"],
        Lazy(hidden),
        Lazy(mlp_out),
    ]
    if last:
        ins += last_grad
    outs = [
        Out((group, D), bf16),
        Out((group, D), bf16),
        Out((group, D), bf16),
        sds((rows, D), bf16),
        sds((2 * rows, D), bf16),
        sds((D, rows), f32),
        sds((place.blocks, 2 * place.mixed_rows, rows) if last else (D, rows), bf16),
        sds((NH, rows), f32),
        sds((NH, rows), f32),
        sds((D, rows), bf16),
        sds((rows, D), bf16 if last else f32),
        sds((8, 128), f32),
        sds((16, D) if last else (rows, D), bf16),
    ]
    return call(kernel, ins, outs, [VMEM((group, D), bf16)], scalars, flops=60 * 10**9)


def mlp_backward(grad, factor, hidden, params, layer):
    rows = grad.shape[0]

    def kernel(g_ref, factor_ref, down, up, out_ref):
        g_low = g_ref[...].astype(bf16)
        total = jnp.zeros((rows, D), f32)
        for j in range(0, FF, 512):
            grad_gate = (dot_nt(g_low, down[j : j + 512]) * factor_ref[:, j : j + 512]).astype(bf16)
            total += dot_nt(grad_gate, up[:, j : j + 512])
        out_ref[...] = total

    return call(
        kernel,
        [grad, factor, (params["down_weight"], layer), (params["up_weight"], layer)],
        [sds((rows, D), f32)],
        flops=2 * 2 * rows * D * FF,
    )[0]


def query_backward(place, scalars, tables, own_tables, params, layer, kept):
    rows, group = place.rows, place.group
    tile = min(512, group)

    def kernel(scal, cos_t, left_t, right_t, own_tabs, gain, shift, w, b, normal_all, k_all, v_all, q_own, dmix_ref, log_ref, delta_ref, q_all, grad_ref, grad_t_ref):
        own_at = pl.multiple_of(scal[2] * rows, rows)
        ends = place.ends(scal)
        gain_l, shift_l = gain[layer : layer + 1], shift[layer : layer + 1]

        def project(i, _):
            at = pl.multiple_of(i * tile, tile)
            a = (normal_all[pl.ds(at, tile)].astype(f32) * gain_l + shift_l).astype(bf16)
            q = dot(a, w[...]) + b[layer : layer + 1, :D]
            tabs = [t[pl.ds(at, tile)] for t in (cos_t, left_t, right_t)]
            for p in range(PAIRS):
                turned = rope(q[:, 128 * p : 128 * p + 128], *tabs).astype(bf16)
                q_all[pl.ds(at, tile), 128 * p : 128 * p + 128] = turned * jnp.asarray(score_scale, bf16)
            return 0

        last_end = end_of(own_at + rows - 1, ends, group)
        low, high = own_at // STEP, (last_end + STEP - 1) // STEP
        lax.fori_loop(low * (STEP // tile), high * (STEP // tile), project, 0)
        t = own_at + lax.broadcasted_iota(jnp.int32, (1, rows), 1)
        start = start_of(t, ends)
        q2 = [two_heads(q_own[:, 128 * p : 128 * p + 128]) for p in range(PAIRS)]
        d2 = [two_heads_t(dmix_ref[128 * p : 128 * p + 128]) for p in range(PAIRS)]
        log2 = [jnp.concatenate([log_ref[2 * p : 2 * p + 1], log_ref[2 * p + 1 : 2 * p + 2]], axis=1) for p in range(PAIRS)]
        delta2 = [
            jnp.concatenate([delta_ref[2 * p : 2 * p + 1], delta_ref[2 * p + 1 : 2 * p + 2]], axis=1) for p in range(PAIRS)
        ]

        def queries(i, carry):
            at = pl.multiple_of(i * STEP, STEP)
            s = at + lax.broadcasted_iota(jnp.int32, (STEP, 1), 0)
            bias = jnp.where((s >= start) & (s <= t), 0.0, masked_value)
            bias = jnp.concatenate([bias, bias], axis=1)
            new = []
            for p in range(PAIRS):
                ks = k_all[pl.ds(at, STEP), 128 * p : 128 * p + 128]
                vs = v_all[pl.ds(at, STEP), 128 * p : 128 * p + 128]
                chance = jnp.exp(dot_nt(ks, q2[p]) + bias - log2[p])
                grad_s = (chance * (dot(vs, d2[p]) - delta2[p])).astype(bf16)
                new.append(carry[p] + dot_tn(ks, grad_s))
            return tuple(new)

        zero = jnp.zeros((128, 2 * rows), f32)
        done = lax.fori_loop(
            start_of(own_at, ends) // STEP, (own_at + rows - 1) // STEP + 1, queries, tuple(zero for _ in range(PAIRS))
        )
        tabs = [own_tabs[0:rows].T, -own_tabs[rows : 2 * rows].T, -own_tabs[2 * rows : 3 * rows].T]
        for p in range(PAIRS):
            grad_t = rope_t(one_pair_t(done[p]) * score_scale, *tabs)
            grad_t_ref[128 * p : 128 * p + 128] = grad_t.astype(bf16)
            grad_ref[:, 128 * p : 128 * p + 128] = grad_t.T.astype(bf16)

    return call(
        kernel,
        [
            *tables,
            own_tables,
            params["attn_gain"],
            params["attn_shift"],
            (params["qkv_sorted"], layer, D),
            params["qkv_bias_sorted"],
            kept["normal_all"],
            kept["k_all"],
            kept["v_all"],
            kept["q_own"],
            kept["dmix"],
            kept["log"],
            kept["delta"],
        ],
        [sds((group, D), bf16), sds((rows, D), bf16), sds((D, rows), bf16)],
        (),
        scalars,
        flops=30 * 10**9,
    )


def key_backward(place, scalars, g_whole, stats, own_tables, params, layer, kept, queries, grad, grad_mlp_in, mixed_below):
    rows, group = place.rows, place.group
    below = layer > 0
    n_stats = len(stats)
    tile = min(512, group)
    part = place.packed_rows

    def kernel(scal, *refs):
        refs = list(refs)
        ss = [refs.pop(0) for _ in range(n_stats)]
        (g_all, own_tabs, gain, mlp_gain, w, out_w, q_all, gq_ref, gq_t_ref, kv_own, h_ref, g_ref, gmlp_ref, stats_ref) = refs[:14]
        refs = refs[14:]
        if below:
            below_mixed, below_log, below_w = refs[:3]
            refs = refs[3:]
        pieces_out, g_out, payload_ref, dmix_out, delta_out = refs[:5]
        dm_all, log_all, delta_all, packed_t = refs[5:]
        own_at = pl.multiple_of(scal[2] * rows, rows)
        ends = place.ends(scal)
        gain_l = gain[layer : layer + 1]
        for slot in range(place.blocks):
            at = pl.multiple_of(place.position(scal, slot) * rows, rows)
            if below:
                flip = slot % place.n_head
                info = ss[slot // place.n_head][16 * flip : 16 * flip + 16].astype(f32)[:NH]
            else:
                info = ss[slot][rows : rows + 16].astype(f32)[:NH]
            log_all[:, pl.ds(at, rows)] = info[:, 0:128] + info[:, 128:256]
            delta_all[:, pl.ds(at, rows)] = info[:, 256:384] + info[:, 384:512]
        last_end = end_of(own_at + rows - 1, ends, group)

        def project(i, _):
            at = pl.multiple_of(i * tile, tile)
            dm_all[pl.ds(at, tile)] = dot_nt(g_all[pl.ds(at, tile)], out_w[...]).astype(bf16)
            return 0

        low, high = own_at // STEP, (last_end + STEP - 1) // STEP
        lax.fori_loop(low * (STEP // tile), high * (STEP // tile), project, 0)
        s_at = own_at + lax.broadcasted_iota(jnp.int32, (rows, 1), 0)
        k2 = [two_heads(kv_own[0:rows, 128 * p : 128 * p + 128]) for p in range(PAIRS)]
        v2 = [two_heads(kv_own[rows : 2 * rows, 128 * p : 128 * p + 128]) for p in range(PAIRS)]

        def keys(i, carry):
            at = pl.multiple_of(i * STEP, STEP)
            t = at + lax.broadcasted_iota(jnp.int32, (1, STEP), 1)
            start = start_of(t, ends)
            bias = jnp.where((s_at >= start) & (s_at <= t), 0.0, masked_value)
            new = []
            for p in range(PAIRS):
                dk, dv = carry[p]
                qs = q_all[pl.ds(at, STEP), 128 * p : 128 * p + 128]
                dms = dm_all[pl.ds(at, STEP), 128 * p : 128 * p + 128]
                scores = dot_nt(k2[p], qs)
                pulled = dot_nt(v2[p], dms)
                chances, grads = [], []
                for half in range(2):
                    n = 2 * p + half
                    part = slice(half * rows, half * rows + rows)
                    chance = jnp.exp(scores[part] + bias - log_all[n : n + 1, pl.ds(at, STEP)])
                    grads.append(chance * (pulled[part] - delta_all[n : n + 1, pl.ds(at, STEP)]))
                    chances.append(chance)
                chance = jnp.concatenate(chances, axis=0).astype(bf16)
                grad_s = jnp.concatenate(grads, axis=0).astype(bf16)
                new.append((dk + dot(grad_s, qs), dv + dot(chance, dms)))
            return tuple(new)

        zero = jnp.zeros((2 * rows, 128), f32)
        done = lax.fori_loop(low, high, keys, tuple((zero, zero) for _ in range(PAIRS)))
        tabs = [own_tabs[0:rows], -own_tabs[rows : 2 * rows], -own_tabs[2 * rows : 3 * rows]]
        grad_k = [rope(one_pair(done[p][0]), *tabs).astype(bf16) for p in range(PAIRS)]
        grad_v = [one_pair(done[p][1]).astype(bf16) for p in range(PAIRS)]
        grad_in = dot_nt(gq_ref[...], w[:, 0:D])
        for j, parts in ((1, grad_k), (2, grad_v)):
            grad_in += dot_nt(jnp.concatenate(parts, axis=1), w[:, j * D : j * D + D])

        normal, inverse = norm_parts(h_ref[...].astype(f32))
        grad_mlp = gmlp_ref[...]
        grad_normal = grad_in * gain_l + grad_mlp * mlp_gain[layer : layer + 1]
        back = inverse * (
            grad_normal
            - jnp.mean(grad_normal, axis=-1, keepdims=True)
            - normal * jnp.mean(grad_normal * normal, axis=-1, keepdims=True)
        )
        g_new = g_ref[...].astype(f32) + back
        g_out[...] = g_new

        sums = [
            jnp.sum(v, axis=0, keepdims=True)
            for v in (grad_in * normal, grad_in, grad_mlp * normal, grad_mlp)
        ]
        for j in range(3):
            for p in range(PAIRS):
                if j == 0:
                    turned = gq_t_ref[128 * p : 128 * p + 128]
                else:
                    turned = (grad_k, grad_v)[j - 1][p].astype(f32).T.astype(bf16)
                for half in range(2):
                    at = (2 * p + half) * 3 * HD + j * HD
                    packed_t[at : at + HD] = turned[half * HD : half * HD + HD]
        layer_sums = jnp.where(lane_of(8) < 4, stats_ref[...], 0.0)
        layer_sums = jnp.broadcast_to(pltpu.roll(layer_sums, scal[2] * 4, 1)[0:1], (16, 128))
        row16 = lax.broadcasted_iota(jnp.int32, (16, 128), 0)
        for p in range(place.n_head):
            extra = jnp.concatenate([x[:, 128 * p : 128 * p + 128] for x in sums] + [jnp.zeros((4, 128), f32)], axis=0)
            extra = jnp.concatenate([extra, extra], axis=0)
            extra = jnp.where((row16 & 7) == 4, layer_sums, extra)
            high, rest = split_low(extra)
            extra = jnp.where(row16 < 8, high, rest)
            for c in range(place.n_ctx):
                at = (p * place.n_ctx + c) * part
                pieces_out[c * place.n_head + p, 0:part] = packed_t[at : at + part]
                pieces_out[c * place.n_head + p, part : part + 16] = extra

        g_low = g_new.astype(bf16)
        if below:
            payload_ref[0:rows] = g_low
            dmix = dot_nt(below_w[...], g_low).astype(bf16)
            dmix_out[...] = dmix
            deltas = delta_rows(dmix, below_mixed[...])
            delta_out[...] = deltas
            payload_ref[rows : rows + 16] = stat_payload(below_log[...], deltas)
        else:
            payload_ref[...] = jnp.zeros_like(payload_ref)
            dmix_out[...] = jnp.zeros_like(dmix_out)
            delta_out[...] = jnp.zeros_like(delta_out)

    ins = [
        *stats,
        g_whole,
        own_tables,
        params["attn_gain"],
        params["mlp_gain"],
        (params["qkv_sorted"], layer),
        (params["out_weight"], layer),
        *queries,
        kept["kv_own"],
        kept["hidden"],
        grad,
        grad_mlp_in,
        kept["stats"],
    ]
    if below:
        ins += [mixed_below["mixed"], mixed_below["log"], (params["out_weight"], layer - 1)]
    outs = [
        sds((place.blocks, part + 16, rows), bf16),
        sds((rows, D), f32),
        sds((rows + 16, D) if below else (16, D), bf16),
        sds((D, rows) if below else (16, rows), bf16),
        sds((NH, rows), f32),
    ]
    scratch = [VMEM((group, D), bf16), VMEM((NH, group), f32), VMEM((NH, group), f32), VMEM((3 * D, rows), bf16)]
    return call(kernel, ins, outs, scratch, scalars, flops=60 * 10**9)


def mlp_weight_grads(place, scalars, blocks, normal_all, params, layer, mixed=None):
    group, rows, units = place.group, place.rows, place.units
    tile = min(512, group)
    size = 0 if mixed is None else place.mixed_rows

    def kernel(scal, *refs):
        gs = refs[: place.blocks]
        refs = list(refs[place.blocks :])
        mixed_ref, other_ref = (refs.pop(0), refs.pop(0)) if size else (None, None)
        normal_ref, gain, shift, up, up_b, down, g_ref, up_out, down_out = refs[:9]
        mixed_t = refs[9] if size else None
        gain_l, shift_l = gain[layer : layer + 1], shift[layer : layer + 1]
        for slot in range(place.blocks):
            at = pl.multiple_of(place.position(scal, slot) * rows, rows)
            g_ref[pl.ds(at, rows)] = gs[slot][0:rows]
            if size:
                mixed_t[:, slot * rows : (slot + 1) * rows] = mixed_ref[slot]

        def step(i, carry):
            up_t, down_g, bias, g_sum = carry
            at = pl.multiple_of(i * tile, tile)
            x = (normal_ref[pl.ds(at, tile)].astype(f32) * gain_l + shift_l).astype(bf16)
            g = g_ref[pl.ds(at, tile)]
            gate = dot(x, up[...]) + up_b[...]
            cdf = 0.5 * (1.0 + lax.erf(gate * math.sqrt(0.5)))
            pdf = jnp.exp(-0.5 * gate * gate) * (1.0 / math.sqrt(2.0 * math.pi))
            acted = (gate * cdf).astype(bf16)
            grad_gate = (dot_nt(g, down[...]) * (cdf + gate * pdf)).astype(bf16)
            up_t += dot(grad_gate.T, x)
            down_g += dot(acted.T, g)
            bias += jnp.sum(grad_gate.astype(f32), axis=0, keepdims=True)
            g_sum += jnp.sum(g.astype(f32), axis=0, keepdims=True)
            return up_t, down_g, bias, g_sum

        zero = jnp.zeros((units, D), f32)
        up_t, down_g, bias, g_sum = lax.fori_loop(
            0, group // tile, step, (zero, zero, jnp.zeros((1, units), f32), jnp.zeros((1, D), f32))
        )
        up_out[0:units] = up_t.astype(bf16)
        if units < 128:
            bias = jnp.concatenate([bias, jnp.zeros((1, 128 - units), f32)], axis=1)
        wide = jnp.concatenate([bias, jnp.zeros((1, D - 128), f32)], axis=1)
        row = lax.broadcasted_iota(jnp.int32, (32, D), 0)
        extra = jnp.where((row & 7) == 0, wide, jnp.where((row & 7) == 1, g_sum, 0.0))
        high, rest = split_low(extra)
        up_out[units : units + 32] = jnp.where(row < 8, high, jnp.where(row < 16, rest, jnp.zeros_like(rest)))
        if size:
            out_g = [dot(mixed_t[k * size : (k + 1) * size], g[...]) for k, g in enumerate((g_ref, other_ref))]
        for p in range(place.n_head):
            cols = slice(128 * p, 128 * p + 128)
            down_out[p, 0:units] = down_g[:, cols].astype(bf16)
            for k in range(2 if size else 0):
                down_out[p, units + k * size : units + (k + 1) * size] = out_g[k][:, cols].astype(bf16)

    up, up_b, down = params["units"][layer]
    made = call(
        kernel,
        [*blocks, *([] if mixed is None else mixed), normal_all, params["mlp_gain"], params["mlp_shift"], up, up_b, down],
        [sds((group, D), bf16), sds((units + 32, D), bf16), sds((place.n_head, units + 2 * size, 128), bf16)],
        [VMEM((2 * size, group), bf16)] if size else [],
        scalars,
        flops=4 * 2 * group * D * units,
    )
    return made


def attention_weight_grads(place, scalars, received, normal_all, params, layer):
    group, rows, part = place.group, place.rows, place.packed_rows
    tile = min(512, group)

    def kernel(received_ref, normal_ref, gain, shift, out_ref, chunk_t):
        gain_l, shift_l = gain[layer : layer + 1], shift[layer : layer + 1]
        extra = jnp.zeros((16, 128), f32)
        for j in range(place.blocks):
            chunk_t[:, j * rows : (j + 1) * rows] = received_ref[j, 0:part]
            extra += received_ref[j, part : part + 16].astype(f32)
        total = jnp.zeros((part, D), f32)
        for at in range(0, group, tile):
            x = (normal_ref[at : at + tile].astype(f32) * gain_l + shift_l).astype(bf16)
            total += dot(chunk_t[:, at : at + tile], x)
        out_ref[0:part] = total.astype(bf16)
        bias = dot_nt(jnp.ones((16, group), bf16), chunk_t[...])
        bias = jnp.concatenate([bias, jnp.zeros((16, 128 - part), f32)], axis=1)
        extra = extra[0:8] + extra[8:16]
        wide = jnp.concatenate([extra[k : k + 1] for k in range(4)], axis=1)
        none = jnp.zeros((1, D - 256), f32)
        second = jnp.concatenate([bias[0:1], extra[4:5], none], axis=1)
        row = lax.broadcasted_iota(jnp.int32, (16, D), 0)
        high, rest = split_low(jnp.where((row & 7) == 0, wide, jnp.where((row & 7) == 1, second, 0.0)))
        out_ref[part : part + 16] = jnp.where(row < 8, high, rest)

    return call(
        kernel,
        [received, normal_all, params["attn_gain"], params["attn_shift"]],
        [sds((part + 16, D), bf16)],
        [VMEM((part, group), bf16)],
        flops=2 * group * D * part,
    )[0]


def pack_mlp(place, scalars, up_share, pieces, halves):
    rows = place.units + 32 + pieces.shape[1]
    half = rows // 2

    def kernel(scal, up_ref, pieces_ref, *refs):
        if halves:
            mine, other, full = refs
        else:
            (full,) = refs
        full[0 : place.units + 32] = up_ref[...]
        for p in range(place.n_head):
            full[place.units + 32 :, 128 * p : 128 * p + 128] = pieces_ref[p]
        if halves:
            at = pl.multiple_of(scal[7] * half, half)
            mine[...] = full[pl.ds(at, half)]
            other[...] = full[pl.ds(pl.multiple_of(half - at, half), half)]

    outs = [sds((half, D), bf16)] * 2 if halves else [sds((rows, D), bf16)]
    scratch = [VMEM((rows, D), bf16)] if halves else []
    return call(kernel, [up_share, pieces], outs, scratch, scalars, flops=10**7)


def along_lanes(rows, width):
    if width == 128:
        return jnp.concatenate(rows, axis=1)
    full = len(rows) * width
    out = jnp.zeros((8, full), f32)
    for k, row in enumerate(rows):
        lane = lax.broadcasted_iota(jnp.int32, (8, full), 1)
        row = jnp.concatenate([row, jnp.zeros((1, full - 128), f32)], axis=1)
        row = jnp.where(lane < width, jnp.broadcast_to(row, (8, full)), 0.0)
        out += pltpu.roll(row, k * width, 1) if k else row
    return out[0:1]


def whole_shares(place, scal, refs, at, size, full, halves):
    if not halves:
        return [x.at[at : at + size] for x in refs]
    half = size // 2
    for s in range(place.n_ctx):
        full[s, pl.ds(pl.multiple_of(scal[7] * half, half), half)] = refs[s][at : at + half]
        start = s * half
        full[s, pl.ds(pl.multiple_of((1 - scal[7]) * half, half), half)] = refs[-1][start : start + half]
    return [full.at[s] for s in range(place.n_ctx)]


def place_mlp(place, scalars, shares, layer, into):
    n_ctx, units = place.n_ctx, place.units
    taken = 0 if into is None else 2
    halves = len(shares) > n_ctx
    size = place.mixed_rows if layer == 0 else 0
    rows = 2 * units + 32 + 2 * size

    def kernel(scal, *refs):
        up_out, down_out, small_out, *out_outs, up_t, bias_rows, full = refs[len(shares) + taken :]
        ordered = len(shares) == 1
        if ordered:
            srcs = [refs[0].at[c * rows : (c + 1) * rows] for c in range(n_ctx)]
        else:
            srcs = whole_shares(place, scal, refs[: len(shares)], 0, rows, full, halves)
        for s in range(n_ctx):
            c = s if ordered else lax.rem(scal[0] - s + n_ctx, n_ctx)
            at = pl.multiple_of(c * units, units)
            up_t[pl.ds(at, units)] = srcs[s][0:units].astype(f32)
            extra = srcs[s][units : units + 16].astype(f32)
            extra = extra[0:8] + extra[8:16]
            bias_rows[c] = jnp.broadcast_to(extra[0:1, :128], (8, 128))
            if s == 0:
                small_out[...] = jnp.zeros_like(small_out)
                for q in range(place.n_head):

                    @pl.when(scal[1] == q)
                    def _():
                        small_out[1:2, 0:128] = extra[1:2, 128 * q : 128 * q + 128]

            for p in range(place.n_head):
                at = pl.multiple_of(p * (FF // place.n_head) + c * units, units)
                base = units + 32
                down_out[pl.ds(at, units)] = srcs[s][base : base + units, 128 * p : 128 * p + 128].astype(f32)
                at = pl.multiple_of(p * 128 + c * place.mixed_rows, place.mixed_rows)
                for k in range(2 if size else 0):
                    start = base + units + k * size
                    out_outs[0][k, pl.ds(at, size)] = srcs[s][start : start + size, 128 * p : 128 * p + 128].astype(f32)
        up_out[...] = up_t[...].T
        small_out[0:1] = along_lanes([bias_rows[c][0:1] for c in range(n_ctx)], units)

    wide = FF // place.n_head
    return call(
        kernel,
        shares,
        [
            (sds((LAYERS, D, wide), f32), layer),
            (sds((LAYERS, FF, 128), f32), layer),
            sds((8, wide), f32),
            *([sds((LAYERS, D, 128), f32)] if size else []),
        ],
        [VMEM((wide, D), f32), VMEM((n_ctx, 8, 128), f32), VMEM((n_ctx, rows, D) if halves else (1, 16, D), bf16)],
        scalars,
        flops=10**7,
        into=into,
    )


def place_attention(place, scalars, shares, layer, into, smalls=None, count=1):
    n_ctx, part = place.n_ctx, place.packed_rows
    taken = 0 if into is None else 1
    wide = 3 * D // place.n_head
    wide_up = FF // place.n_head
    given = [] if smalls is None else smalls

    def kernel(scal, *refs):
        shares_in, given_in = refs[: len(shares)], refs[len(shares) : len(shares) + len(given)]
        qkv_out, *small_outs, qkv_t, info, small = refs[len(shares) + len(given) + taken :]
        small[...] = jnp.zeros_like(small)
        for s in range(n_ctx):
            c = lax.rem(scal[0] - s + n_ctx, n_ctx)
            at = pl.multiple_of(c * part, part)
            qkv_t[pl.ds(at, part)] = shares_in[s][0:part].astype(f32)
            extra = shares_in[s][part : part + 16].astype(f32)
            extra = extra[0:8] + extra[8:16]
            info[c] = extra
            if s == 0:
                for k in range(4):
                    small[k : k + 1, 0:128] = extra[0:1, 128 * k : 128 * k + 128]
                small[4:5, 0:128] = extra[1:2, 128:256]
        qkv_out[...] = qkv_t[...].T
        small[5:6] = along_lanes([info[c, 1:2, 0:128] for c in range(n_ctx)], part)
        if smalls is None:
            small_outs[0][...] = small[...]
            return
        attn_1, mlp_0, mlp_1 = given_in
        lane = lane_of(1)
        for spot, attn, mlp in ((0, small, mlp_0), (1, attn_1, mlp_1)):
            row = slice(spot, spot + 1)
            for k in range(4):
                small_outs[k][row] = attn[k : k + 1, 0:128]
            small_outs[4][row] = attn[5:6]
            small_outs[5][row] = mlp[0:1]
            small_outs[6][row] = mlp[1:2, 0:128]
            small_outs[7][row] = mlp[1:2, 0:128]
            for k in range(3):
                picked = jnp.where((lane & 3) == k, attn[4:5, 0:128], 0.0)
                small_outs[8][row, k : k + 1] = jnp.sqrt(jnp.sum(picked, axis=1, keepdims=True) * (1.0 / count))

    if smalls is None:
        outs = [sds((8, wide), f32)]
    else:
        widths = [128, 128, 128, 128, wide, wide_up, 128, 128, 3]
        outs = [sds((LAYERS, width), f32) for width in widths]
    return call(
        kernel,
        [*shares, *given],
        [(sds((LAYERS, D, wide), f32), layer), *outs],
        [
            VMEM((wide, D), f32),
            VMEM((n_ctx, 8, D), f32),
            VMEM((8, wide), f32),
        ],
        scalars,
        flops=10**7,
        into=into,
    )


def prepare(place, lengths, qkv_weight, qkv_bias):
    group = place.group
    blocks = group // 128
    dim = jnp.arange(128, dtype=jnp.int32)[None, :] % HD
    freq = rope_base ** (-2.0 * (dim % (ROT // 2)).astype(f32) / ROT)
    starts = jnp.concatenate([jnp.zeros((1,), jnp.int32), lengths[0, :3]])
    starts = jnp.stack([starts[0], starts[1], starts[1] + starts[2], starts[1] + starts[2] + starts[3]])
    first = (jnp.arange(blocks, dtype=jnp.int32)[:, None] * 128 - starts[None, :]).reshape(-1, 1)
    whole = jnp.concatenate([first, jnp.arange(128, dtype=jnp.int32)[:, None]], axis=0).astype(f32) * freq
    cosines, sines = jnp.cos(whole), jnp.sin(whole)
    base = 4 * blocks

    def kernel(scal, w_ref, b_ref, cos_ref, sin_ref, w_out, b_out, cos_t, left_t, right_t, own_t):
        def sort(read, write):
            for p in range(PAIRS):
                a, b, c = (read(slice(128 * (3 * p + i), 128 * (3 * p + i) + 128)).astype(f32) for i in range(3))
                first = lane_of(a.shape[0]) < HD
                made = (jnp.where(first, a, b), pltpu.roll(jnp.where(first, c, a), HD, 1), jnp.where(first, b, c))
                for j in range(3):
                    write(slice(j * D + 128 * p, j * D + 128 * p + 128), made[j])

        for layer in range(LAYERS):

            def store(to, x, layer=layer):
                w_out[layer, :, to] = x.astype(bf16)

            sort(lambda at, layer=layer: w_ref[layer, :, at], store)

        def store_bias(to, x):
            b_out[:, to] = x

        sort(lambda at: b_ref[:, at], store_bias)
        ends = place.ends(scal)
        dim = lane_of(128) & (HD - 1)
        cos_b, sin_b = cos_ref[base : base + 128], sin_ref[base : base + 128]

        def table(i, _):
            at = pl.multiple_of(i * 128, 128)
            t = at + lax.broadcasted_iota(jnp.int32, (128, 1), 0)
            cos_a, sin_a = cos_ref[pl.ds(4 * i, 1)], sin_ref[pl.ds(4 * i, 1)]
            for k in range(1, 4):
                later = t >= ends[k - 1]
                cos_a = jnp.where(later, cos_ref[pl.ds(4 * i + k, 1)], cos_a)
                sin_a = jnp.where(later, sin_ref[pl.ds(4 * i + k, 1)], sin_a)
            cosine = cos_a * cos_b - sin_a * sin_b
            sine = sin_a * cos_b + cos_a * sin_b
            cos_t[pl.ds(at, 128)] = jnp.where(dim < ROT, cosine, 1.0)
            left_t[pl.ds(at, 128)] = jnp.where(dim < ROT // 2, -sine, 0.0)
            right_t[pl.ds(at, 128)] = jnp.where((dim >= ROT // 2) & (dim < ROT), sine, 0.0)
            return 0

        lax.fori_loop(0, blocks, table, 0)
        own_at = pl.multiple_of(scal[2] * place.rows, place.rows)
        for k, ref in enumerate((cos_t, left_t, right_t)):
            own_t[k * place.rows : (k + 1) * place.rows] = ref[pl.ds(own_at, place.rows)]

    bias = jnp.concatenate([qkv_bias, jnp.zeros((8 - LAYERS, 3 * D), f32)], axis=0)
    made = call(
        kernel,
        [qkv_weight, bias, cosines, sines],
        [sds(qkv_weight.shape, bf16), sds((8, 3 * D), f32), *[sds((group, 128), f32)] * 3, sds((3 * place.rows, 128), f32)],
        (),
        lengths,
        flops=10**7,
    )
    return made[0], made[1], made[2:5], made[5]


def tie(x, *after):
    return lax.optimization_barrier((x, *after))[0] if after else x


def flip_heads(x, flip):
    return lax.ppermute(x, "head", [(i, i ^ flip) for i in range(lax.axis_size("head"))])


def turn_ctx(x, shift):
    n = lax.axis_size("ctx")
    return lax.ppermute(x, "ctx", [(i, (i + shift) % n) for i in range(n)])


def gather_rings(own):
    return [own] + [turn_ctx(own, s) for s in range(1, lax.axis_size("ctx"))]


def gather_flips(rings, flip, *after):
    return [flip_heads(tie(x, *after), flip) for x in rings]


def by_slot(rings, far, near, far_near):
    return [x for four in zip(rings, near, far, far_near) for x in four]


def with_flip(own, flip):
    return jnp.concatenate([own, flip_heads(own, flip)], axis=0)


def swap_dp(x):
    return lax.ppermute(x, "dp", [(0, 1), (1, 0)])


def per_device(
    hidden_in,
    lengths,
    attn_gain,
    attn_shift,
    mlp_gain,
    mlp_shift,
    qkv_weight,
    qkv_bias,
    out_weight,
    out_bias,
    up_weight,
    up_bias,
    down_weight,
    down_bias,
    cotangent,
):
    rows = hidden_in.shape[0]
    n_dp, n_ctx, n_head = (lax.axis_size(a) for a in ("dp", "ctx", "head"))
    place = Place(n_dp, n_ctx, n_head, rows)
    group = place.group
    scalars = lengths
    qkv_sorted, qkv_bias_sorted, tables, own_tables = prepare(place, lengths, qkv_weight, qkv_bias)
    params = {
        "attn_gain": attn_gain,
        "attn_shift": attn_shift,
        "mlp_gain": mlp_gain,
        "mlp_shift": mlp_shift,
        "qkv_sorted": qkv_sorted,
        "qkv_bias_sorted": qkv_bias_sorted,
        "out_weight": out_weight,
        "out_bias": out_bias,
        "up_weight": up_weight,
        "up_bias": up_bias,
        "down_weight": down_weight,
        "down_bias": down_bias,
    }
    units = place.units
    at = lax.axis_index("head") * (FF // n_head) + lax.axis_index("ctx") * units
    params["units"] = [
        (
            lax.dynamic_slice(up_weight, (layer, 0, at), (1, D, units))[0],
            lax.dynamic_slice(up_bias, (layer, at), (1, units)),
            lax.dynamic_slice(down_weight, (layer, at, 0), (1, units, D))[0],
        )
        for layer in range(LAYERS)
    ]
    def attention(layer, blocks, hidden, mlp_out, last_grad):
        names = ("normal_all", "k_all", "v_all", "q_own", "kv_own", "mixed", "mixed_low", "log", "delta", "dmix", "h_out", "stats", "low")
        made = attention_forward(place, scalars, blocks, tables, params, layer, hidden, mlp_out, last_grad)
        return dict(zip(names, made), hidden=hidden)

    def backward_queries(layer, kept):
        return query_backward(place, scalars, tables, own_tables, params, layer, kept)

    def backward_keys(layer, g_all, stats, kept, queries, grad, grad_mlp_in, below):
        return key_backward(
            place, scalars, g_all, stats, own_tables, params, layer, kept, queries, grad, grad_mlp_in, below
        )

    def head_swap(pieces):
        return lax.all_to_all(pieces, "head", 0, 0, tiled=True)

    def group_swap(pieces):
        return lax.all_to_all(pieces, ("ctx", "head"), 0, 0, tiled=True)

    def reduce_mlp(up_share, pieces, halves):
        made = pack_mlp(place, scalars, up_share, pieces, halves)
        if n_dp == 2:
            return (made[0].astype(f32) + swap_dp(made[-1]).astype(f32)).astype(bf16)
        return lax.psum(made[0], "dp")

    def sum_dp(x):
        if n_dp == 2:
            return (x.astype(f32) + swap_dp(x).astype(f32)).astype(bf16)
        return lax.psum(x, "dp")

    def finish(rings):
        return [*rings, swap_dp(jnp.concatenate(rings, axis=0))] if n_dp == 2 else rings

    together = lax.optimization_barrier

    mlp_0, factor_0, _ = mlp_forward(hidden_in, params, 0)
    rings, mlp_0, factor_0 = together((gather_rings(hidden_in), mlp_0, factor_0))
    far = gather_flips(rings, 2)
    far, rings, params["qkv_sorted"], tables, own_tables = together((far, rings, qkv_sorted, tables, own_tables))
    near, far_near = together((gather_flips(rings, 1), gather_flips(far, 1)))
    first, cot_rings = together(
        (attention(0, by_slot(rings, far, near, far_near), hidden_in, mlp_0, None), gather_rings(tie(cotangent, near)))
    )
    hidden, low = first["h_out"], first["low"]
    mlp_1, factor_1, _ = mlp_forward(hidden, params, 1)
    back_1 = mlp_backward(tie(cotangent, mlp_1), factor_1, hidden, params, 1)
    rings, mlp_1, back_1 = together((gather_rings(low), mlp_1, back_1))
    far, rings, params["units"] = together((gather_flips(rings, 2), rings, params["units"]))
    near, far_near = together((gather_flips(rings, 1), gather_flips(far, 1)))
    second = attention(1, by_slot(rings, far, near, far_near), hidden, mlp_1, [cotangent, first["mixed_low"]])
    second, cot_far, cot_rings = together((second, gather_flips(cot_rings, 2, near), cot_rings))
    output_rows, low = second["h_out"], second["low"]

    pair, cot_near, cot_far_near = together((with_flip(low, 1), gather_flips(cot_rings, 1), gather_flips(cot_far, 1)))
    made = mlp_weight_grads(
        place, scalars, by_slot(cot_rings, cot_far, cot_near, cot_far_near), second["normal_all"], params, 1
    )
    (cot_all, up_share_1, pieces_1), four = together((made, with_flip(pair, 2)))
    queries_1, stats = together((backward_queries(1, second), gather_rings(four)))
    made = backward_keys(1, cot_all, stats, second, queries_1, cotangent, back_1, first)
    (packed_1, grad, payload, dmix, delta), mixed = together((made, group_swap(second["mixed_low"])))
    first["dmix"], first["delta"] = dmix, delta
    back_0 = mlp_backward(grad, factor_0, hidden_in, params, 0)
    rings, back_0, pieces_1 = together((gather_rings(payload), back_0, head_swap(tie(pieces_1, payload))))
    half_1 = reduce_mlp(up_share_1, pieces_1, n_dp == 2)
    far, rings, queries_0, half_1, received_1 = together(
        (
            gather_flips(rings, 2),
            rings,
            backward_queries(0, dict(first, delta=tie(delta, back_0))),
            half_1,
            group_swap(tie(packed_1, back_0)),
        )
    )
    near, far_near = together((gather_flips(rings, 1), gather_flips(far, 1)))
    blocks = by_slot(rings, far, near, far_near)
    mlp_rings_1 = gather_rings(tie(half_1, near))
    g_all, up_share_0, pieces_0 = mlp_weight_grads(
        place, scalars, blocks, first["normal_all"], params, 0, [mixed, cot_all]
    )
    made = backward_keys(0, g_all, blocks, first, queries_0, grad, back_0, None)
    (packed_0, grad, _, _, _), pieces_0, mlp_rings_1, up_share_0, received_1 = together(
        (made, head_swap(pieces_0), mlp_rings_1, up_share_0, received_1)
    )
    half_0 = reduce_mlp(up_share_0, pieces_0, n_dp == 2)
    mlp_rings_0 = gather_rings(half_0)
    share_1 = attention_weight_grads(place, scalars, tie(received_1, half_0), second["normal_all"], params, 1)
    sum_1 = sum_dp(share_1)
    received_0, sum_1, mlp_rings_0, mlp_shares_1 = together(
        (group_swap(packed_0), sum_1, mlp_rings_0, finish([tie(x, half_0) for x in mlp_rings_1]))
    )
    share_0 = attention_weight_grads(place, scalars, received_0, first["normal_all"], params, 0)
    *big, mlp_small_1 = place_mlp(place, scalars, [tie(mlp_shares_1[0], share_0), *mlp_shares_1[1:]], 1, None)
    sum_0 = sum_dp(share_0)
    mlp_shares_0 = finish([tie(x, sum_0) for x in mlp_rings_0])
    sum_0, attn_rings_1, big, mlp_small_1 = together((sum_0, gather_rings(sum_1), big, mlp_small_1))
    *attn_big, attn_small_1 = place_attention(place, scalars, attn_rings_1, 1, None)
    up_grad, down_grad, mlp_small_0, out_grad = place_mlp(place, scalars, mlp_shares_0, 0, big)
    attn_rings_0, mlp_small_0, attn_big, attn_small_1 = together(
        (gather_rings(sum_0), mlp_small_0, attn_big, attn_small_1)
    )
    qkv_grad, gain, shift, mlp_g, mlp_s, qkv_b, up_b, down_b, out_b, layer_stats = place_attention(
        place, scalars, attn_rings_0, 0, attn_big, [attn_small_1, mlp_small_0, mlp_small_1], group * n_dp * D
    )
    return (
        output_rows, grad, gain, shift, mlp_g, mlp_s, qkv_grad, qkv_b, out_grad, out_b, up_grad, up_b, down_grad, down_b, layer_stats
    )


def solution(mesh):
    rows = P(("dp", "ctx", "head"), None)
    return jax.shard_map(
        per_device,
        mesh=mesh,
        in_specs=(rows, P("dp", None), *([P()] * 12), rows),
        out_specs=(
            rows,
            rows,
            P(None, "head"),
            P(None, "head"),
            P(None, "head"),
            P(None, "head"),
            P(None, None, "head"),
            P(None, "head"),
            P(None, None, "head"),
            P(None, "head"),
            P(None, None, "head"),
            P(None, "head"),
            P(None, None, "head"),
            P(None, "head"),
            P(),
        ),
        check_vma=False,
    )
```

```python
import math

import jax
import jax.numpy as jnp
from jax import lax
from jax.experimental import pallas as pl
from jax.experimental.pallas import tpu as pltpu
from jax.sharding import PartitionSpec as P

D = 512
FF = 2048
NH = 8
HD = 64
ROT = 16
LAYERS = 2
PAIRS = NH // 2
epsilon = 1e-05
masked_value = -1e30
score_scale = 0.125
rope_base = 10000.0
f32 = jnp.float32
bf16 = jnp.bfloat16
STEP = 1024
VMEM = pltpu.VMEM


def dot(a, b):
    return lax.dot_general(a, b, (((1,), (0,)), ((), ())), preferred_element_type=f32)


def dot_nt(a, b):
    return lax.dot_general(a, b, (((1,), (1,)), ((), ())), preferred_element_type=f32)


def norm_parts(hidden):
    centred = hidden - jnp.mean(hidden, axis=-1, keepdims=True)
    inverse = lax.rsqrt(jnp.mean(centred * centred, axis=-1, keepdims=True) + epsilon)
    return centred * inverse, inverse


def rope(x, cos_t, left_t, right_t):
    return x * cos_t + pltpu.roll(x, 128 - 8, 1) * left_t + pltpu.roll(x, 8, 1) * right_t


def start_of(place, ends):
    start = jnp.zeros_like(place)
    for end in ends:
        start = jnp.where(end <= place, end, start)
    return start


def end_of(place, ends, size):
    found = jnp.int32(size)
    for end in reversed(ends):
        found = jnp.where(place < end, end, found)
    return found


def split_low(x):
    high = x.astype(bf16)
    return high, (x - high.astype(f32)).astype(bf16)


def lane_of(rows):
    return lax.broadcasted_iota(jnp.int32, (rows, 128), 1)


def two_heads(x):
    first = lane_of(x.shape[0]) < HD
    zero = jnp.zeros_like(x)
    return jnp.concatenate([jnp.where(first, x, zero), jnp.where(first, zero, x)], axis=0)


def one_pair(x):
    rows = x.shape[0] // 2
    return jnp.where(lane_of(rows) < HD, x[:rows], x[rows:])


def dot_tn(a, b):
    return lax.dot_general(a, b, (((0,), (0,)), ((), ())), preferred_element_type=f32)


def two_heads_t(x):
    first = lax.broadcasted_iota(jnp.int32, x.shape, 0) < HD
    zero = jnp.zeros_like(x)
    return jnp.concatenate([jnp.where(first, x, zero), jnp.where(first, zero, x)], axis=1)


def one_pair_t(x):
    rows = x.shape[1] // 2
    return jnp.where(lax.broadcasted_iota(jnp.int32, (128, rows), 0) < HD, x[:, :rows], x[:, rows:])


def rope_t(x, cos_t, left_t, right_t):
    return x * cos_t + pltpu.roll(x, 128 - 8, 0) * left_t + pltpu.roll(x, 8, 0) * right_t


class Far:
    def __init__(self, array):
        self.array = array


class Lazy:
    def __init__(self, array, at=None, shape=None):
        self.array, self.at = array, at or (lambda ref: ref)
        self.shape = shape or array.shape


class Out:
    def __init__(self, shape, dtype):
        self.shape, self.dtype = shape, dtype


class Coming:
    def __init__(self, ref, copy):
        self.ref, self.copy, self.there = ref, copy, False

    def get(self):
        if not self.there:
            self.copy.wait()
            self.there = True
        return self.ref


class Going:
    def __init__(self, ref, copy):
        self.ref, self.copy, self.gone = ref, copy, False

    def send(self):
        self.copy.start()
        self.gone = True


def call(kernel, ins, outs, scratch=(), scalars=None, vmem=60 << 20, flops=10**9, into=None):
    specs, arrays = [], []

    def block(shape, layer, cols=None):
        place = (layer, *([0] * (len(shape) - 1)))
        return pl.BlockSpec((None, *shape[1:-1], cols or shape[-1]), lambda i: place)

    def whole(shape):
        return pl.BlockSpec(shape, lambda i: (0,) * len(shape))

    n_ins, n_outs = len(ins), len(outs)
    lead = 0
    if scalars is not None:
        specs.append(pl.BlockSpec(memory_space=pltpu.SMEM))
        arrays.append(scalars)
        lead = 1
    for item in ins:
        if isinstance(item, (Far, Lazy)):
            specs.append(pl.BlockSpec(memory_space=pl.ANY))
            arrays.append(item.array)
            continue
        array = item[0] if isinstance(item, tuple) else item
        specs.append(block(array.shape, *item[1:]) if isinstance(item, tuple) else whole(array.shape))
        arrays.append(array)
    aliases = {}
    if into is not None:
        spots = [k for k, o in enumerate(outs) if isinstance(o, tuple)]
        for spot, array in zip(spots, into):
            aliases[len(arrays)] = spot
            specs.append(pl.BlockSpec(memory_space=pl.ANY))
            arrays.append(array)
    shapes, out_specs = [], []
    for o in outs:
        if isinstance(o, tuple):
            shapes.append(o[0])
            out_specs.append(block(o[0].shape, o[1]))
        elif isinstance(o, Out):
            shapes.append(sds(o.shape, o.dtype))
            out_specs.append(pl.BlockSpec(memory_space=pl.ANY))
        else:
            shapes.append(o)
            out_specs.append(whole(o.shape))
    coming = [k for k, item in enumerate(ins) if isinstance(item, Lazy)]
    going = [k for k, o in enumerate(outs) if isinstance(o, Out)]
    slow = [VMEM(ins[k].shape, ins[k].array.dtype) for k in coming] + [VMEM(outs[k].shape, outs[k].dtype) for k in going]
    if slow:
        slow.append(pltpu.SemaphoreType.DMA((len(slow),)))

    def body(*refs):
        refs = list(refs)
        given = []
        if scalars is not None:
            lengths_ref = refs.pop(0)
            ctx, head = lax.axis_index("ctx"), lax.axis_index("head")
            ends = [lengths_ref[0, 0]]
            for k in range(1, 4):
                ends.append(ends[-1] + lengths_ref[0, k])
            given = [[ctx, head, ctx * lax.axis_size("head") + head, *ends, lax.axis_index("dp")]]
        finals = []
        if slow:
            extra = refs[len(refs) - len(slow) :]
            refs = refs[: len(refs) - len(slow)]
            sems = extra[-1]
            for j, k in enumerate(coming):
                copy = pltpu.make_async_copy(ins[k].at(refs[k]), extra[j], sems.at[j])
                copy.start()
                refs[k] = Coming(extra[j], copy)
            first_out = len(arrays) - lead
            for j, k in enumerate(going):
                j += len(coming)
                refs[first_out + k] = Going(extra[j], pltpu.make_async_copy(extra[j], refs[first_out + k], sems.at[j]))
                finals.append(refs[first_out + k])
        kernel(*given, *refs)
        for item in finals:
            if not item.gone:
                item.send()
        for item in finals:
            item.copy.wait()

    moved = sum(x.size * x.dtype.itemsize for x in arrays)
    return pl.pallas_call(
        body,
        grid=(1,),
        in_specs=specs,
        out_specs=out_specs,
        out_shape=shapes,
        scratch_shapes=[*scratch, *slow],
        input_output_aliases=aliases,
        compiler_params=pltpu.CompilerParams(vmem_limit_bytes=vmem),
        cost_estimate=pl.CostEstimate(flops=flops, bytes_accessed=moved, transcendentals=0),
    )(*arrays)


def lazy_layer(array, layer, cols=None):
    if cols is None:
        return Lazy(array, lambda ref: ref.at[layer], array.shape[1:])
    return Lazy(array, lambda ref: ref.at[layer, :, 0:cols], (*array.shape[1:-1], cols))


def sds(shape, dtype):
    return jax.ShapeDtypeStruct(shape, dtype)


def mlp_forward(hidden, params, layer):
    rows = hidden.shape[0]

    def kernel(h_ref, gain, shift, up, up_b, down, down_b, out_ref, factor_ref, normal_ref):
        normal, _ = norm_parts(h_ref[...].astype(f32))
        normal_ref[...] = normal.astype(bf16)
        x = (normal * gain[layer : layer + 1] + shift[layer : layer + 1]).astype(bf16)
        total = jnp.zeros((rows, D), f32)
        for j in range(0, FF, 512):
            gate = dot(x, up[:, j : j + 512]) + up_b[layer : layer + 1, j : j + 512]
            cdf = 0.5 * (1.0 + lax.erf(gate * math.sqrt(0.5)))
            pdf = jnp.exp(-0.5 * gate * gate) * (1.0 / math.sqrt(2.0 * math.pi))
            factor_ref[:, j : j + 512] = cdf + gate * pdf
            total += dot((gate * cdf).astype(bf16), down[j : j + 512])
        out_ref[...] = total + down_b[layer : layer + 1]

    return call(
        kernel,
        [
            hidden,
            params["mlp_gain"],
            params["mlp_shift"],
            (params["up_weight"], layer),
            params["up_bias"],
            (params["down_weight"], layer),
            params["down_bias"],
        ],
        [sds((rows, D), f32), sds((rows, FF), f32), sds((rows, D), bf16)],
        flops=2 * 2 * rows * D * FF,
    )


def mlp_both(hidden, grad, params, layer):
    rows = hidden.shape[0]

    def kernel(h_ref, g_ref, gain, shift, up, up_b, down, down_b, out_ref, back_ref):
        normal, _ = norm_parts(h_ref[...].astype(f32))
        x = (normal * gain[layer : layer + 1] + shift[layer : layer + 1]).astype(bf16)
        g_low = g_ref[...].astype(bf16)
        total = jnp.zeros((rows, D), f32)
        back = jnp.zeros((rows, D), f32)
        for j in range(0, FF, 512):
            gate = dot(x, up[:, j : j + 512]) + up_b[layer : layer + 1, j : j + 512]
            cdf = 0.5 * (1.0 + lax.erf(gate * math.sqrt(0.5)))
            pdf = jnp.exp(-0.5 * gate * gate) * (1.0 / math.sqrt(2.0 * math.pi))
            total += dot((gate * cdf).astype(bf16), down[j : j + 512])
            grad_gate = (dot_nt(g_low, down[j : j + 512]) * (cdf + gate * pdf)).astype(bf16)
            back += dot_nt(grad_gate, up[:, j : j + 512])
        out_ref[...] = total + down_b[layer : layer + 1]
        back_ref[...] = back

    return call(
        kernel,
        [
            hidden,
            grad,
            params["mlp_gain"],
            params["mlp_shift"],
            (params["up_weight"], layer),
            params["up_bias"],
            (params["down_weight"], layer),
            params["down_bias"],
        ],
        [sds((rows, D), f32), sds((rows, D), f32)],
    )


class Place:
    def __init__(self, n_dp, n_ctx, n_head, rows):
        self.n_ctx, self.n_head, self.rows = n_ctx, n_head, rows
        self.halves = n_dp == 2
        self.blocks = n_ctx * n_head
        self.group = self.blocks * rows
        self.units = FF // self.blocks
        self.packed_rows = 3 * D // self.blocks
        self.mixed_rows = D // self.blocks

    def position(self, scal, slot):
        shift, flip = slot // self.n_head, slot % self.n_head
        ctx = lax.rem(scal[0] - shift + self.n_ctx, self.n_ctx)
        return ctx * self.n_head + (scal[1] ^ flip)

    def ends(self, scal):
        return [scal[3 + k] for k in range(4)]


def delta_rows(grad_mixed_t, mixed_t):
    return jnp.concatenate(
        [
            jnp.sum(grad_mixed_t[n * HD : (n + 1) * HD].astype(f32) * mixed_t[n * HD : (n + 1) * HD], axis=0, keepdims=True)
            for n in range(NH)
        ],
        axis=0,
    )


def stat_payload(logs, deltas):
    parts = [*split_low(logs), *split_low(deltas)]
    top = jnp.concatenate(parts, axis=1)
    return jnp.concatenate([top, jnp.zeros_like(top)], axis=0)


def attention_forward(place, scalars, blocks, tables, params, layer, hidden, mlp_out, last_grad):
    rows, group = place.rows, place.group
    first_layer = layer == 0
    last = last_grad is not None
    tile = min(512, group)

    def kernel(scal, *refs):
        refs = list(refs)
        xs = [refs.pop(0) for _ in range(place.blocks)]
        cos_t, left_t, right_t, gain, shift, w, b, out_w, out_b, h_ref, mlp_ref = refs[:11]
        refs = refs[11:]
        g_ref, below_ref = (refs.pop(0), refs.pop(0)) if last else (None, None)
        (normal_out, k_out, v_out, q_own, kv_own, mixed_ref, mixed_low_ref, log_ref, delta_ref, dmix_ref, h_out, stats_ref, low_ref) = refs[:13]
        a_all = refs[13]
        normal_all, k_all, v_all = normal_out.ref, k_out.ref, v_out.ref
        own_at = pl.multiple_of(scal[2] * rows, rows)
        ends = place.ends(scal)
        gain_l, shift_l = gain[layer : layer + 1], shift[layer : layer + 1]
        for slot in range(place.blocks):
            at = pl.multiple_of(place.position(scal, slot) * rows, rows)
            x = xs[slot][...].astype(f32)
            normal = norm_parts(x)[0] if first_layer else x
            normal_all[pl.ds(at, rows)] = normal.astype(bf16)
            a_all[pl.ds(at, rows)] = (normal * gain_l + shift_l).astype(bf16)
        normal_out.send()
        w, cos_t, left_t, right_t = (x.get() for x in (w, cos_t, left_t, right_t))

        def project(i, _):
            at = pl.multiple_of(i * tile, tile)
            k = dot(a_all[pl.ds(at, tile)], w[:, D : 2 * D]) + b[layer : layer + 1, D : 2 * D]
            tabs = [t[pl.ds(at, tile)] for t in (cos_t, left_t, right_t)]
            for p in range(PAIRS):
                k_all[pl.ds(at, tile), 128 * p : 128 * p + 128] = rope(k[:, 128 * p : 128 * p + 128], *tabs).astype(bf16)
            v = dot(a_all[pl.ds(at, tile)], w[:, 2 * D :]) + b[layer : layer + 1, 2 * D :]
            v_all[pl.ds(at, tile)] = v.astype(bf16)
            return 0

        first_key = start_of(own_at, ends)
        low, high = first_key // STEP, (own_at + rows - 1) // STEP + 1
        lax.fori_loop(low * (STEP // tile), high * (STEP // tile), project, 0)
        k_out.send()
        v_out.send()
        kv_own[0:rows], kv_own[rows : 2 * rows] = k_all[pl.ds(own_at, rows)], v_all[pl.ds(own_at, rows)]
        q = dot(a_all[pl.ds(own_at, rows)], w[:, :D]) + b[layer : layer + 1, :D]
        tabs = [t[pl.ds(own_at, rows)] for t in (cos_t, left_t, right_t)]
        for p in range(PAIRS):
            turned = rope(q[:, 128 * p : 128 * p + 128], *tabs).astype(bf16)
            q_own[:, 128 * p : 128 * p + 128] = turned * jnp.asarray(score_scale, bf16)
        t = own_at + lax.broadcasted_iota(jnp.int32, (1, rows), 1)
        start = start_of(t, ends)
        doubled = [two_heads(q_own[:, 128 * p : 128 * p + 128]) for p in range(PAIRS)]

        def attend(i, carry):
            at = pl.multiple_of(i * STEP, STEP)
            s_at = at + lax.broadcasted_iota(jnp.int32, (STEP, 1), 0)
            bias = jnp.where((s_at >= start) & (s_at <= t), 0.0, masked_value)
            bias = jnp.concatenate([bias, bias], axis=1)
            new = []
            for p in range(PAIRS):
                most, total, acc = carry[p]
                scores = dot_nt(k_all[pl.ds(at, STEP), 128 * p : 128 * p + 128], doubled[p]) + bias
                newest = jnp.maximum(most, jnp.max(scores, axis=0, keepdims=True))
                chance = jnp.exp(scores - newest)
                scale = jnp.exp(most - newest)
                total = total * scale + jnp.sum(chance, axis=0, keepdims=True)
                acc = acc * scale + dot_tn(v_all[pl.ds(at, STEP), 128 * p : 128 * p + 128], chance.astype(bf16))
                new.append((newest, total, acc))
            return tuple(new)

        begin = tuple(
            (jnp.full((1, 2 * rows), masked_value, f32), jnp.zeros((1, 2 * rows), f32), jnp.zeros((128, 2 * rows), f32))
            for _ in range(PAIRS)
        )
        done = lax.fori_loop(low, high, attend, begin)
        logs = []
        for p in range(PAIRS):
            most, total, acc = done[p]
            mixed_ref[128 * p : 128 * p + 128] = one_pair_t(acc / total)
            log = most + jnp.log(total)
            logs += [log[:, :rows], log[:, rows:]]
        log_rows = jnp.concatenate(logs, axis=0)
        log_ref[...] = log_rows
        mixed_low = mixed_ref[...].astype(bf16)
        if last:
            size = place.mixed_rows
            for p in range(place.n_head):
                for c in range(place.n_ctx):
                    at = 128 * p + size * c
                    mixed_low_ref[c * place.n_head + p, 0:size] = below_ref[at : at + size]
                    mixed_low_ref[c * place.n_head + p, size : 2 * size] = mixed_low[at : at + size]
        else:
            mixed_low_ref[...] = mixed_low
        out_w = out_w.get()
        attn_out = dot_tn(mixed_low, out_w[...]) + out_b[layer : layer + 1]
        h = h_ref.get()[...].astype(f32)
        mlp = mlp_ref.get()[...]
        result = h + attn_out + mlp
        lane = lane_of(8)
        sums = [jnp.sum(jnp.sum(v * v, axis=1, keepdims=True), axis=0, keepdims=True) for v in (h, attn_out, mlp)]
        stats_ref[...] = jnp.where(lane == 0, sums[0], jnp.where(lane == 1, sums[1], jnp.where(lane == 2, sums[2], 0.0)))
        if last:
            h_out[...] = result.astype(bf16)
            dmix = dot_nt(out_w[...], g_ref[...]).astype(bf16)
            dmix_ref[...] = dmix
            deltas = delta_rows(dmix, mixed_ref[...])
            delta_ref[...] = deltas
            low_ref[...] = stat_payload(log_rows, deltas)
        else:
            h_out[...] = result
            low_ref[...] = norm_parts(result)[0].astype(bf16)
            dmix_ref[...] = jnp.zeros_like(dmix_ref)
            delta_ref[...] = jnp.zeros_like(delta_ref)

    ins = [
        *blocks,
        *[Lazy(x) for x in tables],
        params["attn_gain"],
        params["attn_shift"],
        lazy_layer(params["qkv_sorted"], layer),
        params["qkv_bias_sorted"],
        lazy_layer(params["out_weight"], layer),
        params["out_bias"],
        Lazy(hidden),
        Lazy(mlp_out),
    ]
    if last:
        ins += last_grad
    outs = [
        Out((group, D), bf16),
        Out((group, D), bf16),
        Out((group, D), bf16),
        sds((rows, D), bf16),
        sds((2 * rows, D), bf16),
        sds((D, rows), f32),
        sds((place.blocks, 2 * place.mixed_rows, rows) if last else (D, rows), bf16),
        sds((NH, rows), f32),
        sds((NH, rows), f32),
        sds((D, rows), bf16),
        sds((rows, D), bf16 if last else f32),
        sds((8, 128), f32),
        sds((16, D) if last else (rows, D), bf16),
    ]
    return call(kernel, ins, outs, [VMEM((group, D), bf16)], scalars, flops=60 * 10**9)


def mlp_backward(grad, factor, hidden, params, layer):
    rows = grad.shape[0]

    def kernel(g_ref, factor_ref, down, up, out_ref):
        g_low = g_ref[...].astype(bf16)
        total = jnp.zeros((rows, D), f32)
        for j in range(0, FF, 512):
            grad_gate = (dot_nt(g_low, down[j : j + 512]) * factor_ref[:, j : j + 512]).astype(bf16)
            total += dot_nt(grad_gate, up[:, j : j + 512])
        out_ref[...] = total

    return call(
        kernel,
        [grad, factor, (params["down_weight"], layer), (params["up_weight"], layer)],
        [sds((rows, D), f32)],
        flops=2 * 2 * rows * D * FF,
    )[0]


def query_backward(place, scalars, tables, own_tables, params, layer, kept):
    rows, group = place.rows, place.group
    tile = min(512, group)

    def kernel(scal, cos_t, left_t, right_t, own_tabs, gain, shift, w, b, normal_all, k_all, v_all, q_own, dmix_ref, log_ref, delta_ref, q_out, grad_ref, grad_t_ref):
        q_all = q_out.ref
        own_at = pl.multiple_of(scal[2] * rows, rows)
        ends = place.ends(scal)
        gain_l, shift_l = gain[layer : layer + 1], shift[layer : layer + 1]

        def project(i, _):
            at = pl.multiple_of(i * tile, tile)
            a = (normal_all[pl.ds(at, tile)].astype(f32) * gain_l + shift_l).astype(bf16)
            q = dot(a, w[...]) + b[layer : layer + 1, :D]
            tabs = [t[pl.ds(at, tile)] for t in (cos_t, left_t, right_t)]
            for p in range(PAIRS):
                turned = rope(q[:, 128 * p : 128 * p + 128], *tabs).astype(bf16)
                q_all[pl.ds(at, tile), 128 * p : 128 * p + 128] = turned * jnp.asarray(score_scale, bf16)
            return 0

        last_end = end_of(own_at + rows - 1, ends, group)
        low, high = own_at // STEP, (last_end + STEP - 1) // STEP
        lax.fori_loop(low * (STEP // tile), high * (STEP // tile), project, 0)
        q_out.send()
        k_all, v_all = k_all.get(), v_all.get()
        t = own_at + lax.broadcasted_iota(jnp.int32, (1, rows), 1)
        start = start_of(t, ends)
        q2 = [two_heads(q_own[:, 128 * p : 128 * p + 128]) for p in range(PAIRS)]
        d2 = [two_heads_t(dmix_ref[128 * p : 128 * p + 128]) for p in range(PAIRS)]
        log2 = [jnp.concatenate([log_ref[2 * p : 2 * p + 1], log_ref[2 * p + 1 : 2 * p + 2]], axis=1) for p in range(PAIRS)]
        delta2 = [
            jnp.concatenate([delta_ref[2 * p : 2 * p + 1], delta_ref[2 * p + 1 : 2 * p + 2]], axis=1) for p in range(PAIRS)
        ]

        def queries(i, carry):
            at = pl.multiple_of(i * STEP, STEP)
            s = at + lax.broadcasted_iota(jnp.int32, (STEP, 1), 0)
            bias = jnp.where((s >= start) & (s <= t), 0.0, masked_value)
            bias = jnp.concatenate([bias, bias], axis=1)
            new = []
            for p in range(PAIRS):
                ks = k_all[pl.ds(at, STEP), 128 * p : 128 * p + 128]
                vs = v_all[pl.ds(at, STEP), 128 * p : 128 * p + 128]
                chance = jnp.exp(dot_nt(ks, q2[p]) + bias - log2[p])
                grad_s = (chance * (dot(vs, d2[p]) - delta2[p])).astype(bf16)
                new.append(carry[p] + dot_tn(ks, grad_s))
            return tuple(new)

        zero = jnp.zeros((128, 2 * rows), f32)
        done = lax.fori_loop(
            start_of(own_at, ends) // STEP, (own_at + rows - 1) // STEP + 1, queries, tuple(zero for _ in range(PAIRS))
        )
        tabs = [own_tabs[0:rows].T, -own_tabs[rows : 2 * rows].T, -own_tabs[2 * rows : 3 * rows].T]
        for p in range(PAIRS):
            grad_t = rope_t(one_pair_t(done[p]) * score_scale, *tabs)
            grad_t_ref[128 * p : 128 * p + 128] = grad_t.astype(bf16)
            grad_ref[:, 128 * p : 128 * p + 128] = grad_t.T.astype(bf16)

    return call(
        kernel,
        [
            *tables,
            own_tables,
            params["attn_gain"],
            params["attn_shift"],
            (params["qkv_sorted"], layer, D),
            params["qkv_bias_sorted"],
            kept["normal_all"],
            Lazy(kept["k_all"]),
            Lazy(kept["v_all"]),
            kept["q_own"],
            kept["dmix"],
            kept["log"],
            kept["delta"],
        ],
        [Out((group, D), bf16), sds((rows, D), bf16), sds((D, rows), bf16)],
        (),
        scalars,
        flops=30 * 10**9,
    )


def key_backward(place, scalars, g_whole, stats, own_tables, params, layer, kept, queries, grad, grad_mlp_in, mixed_below):
    rows, group = place.rows, place.group
    below = layer > 0
    n_stats = len(stats)
    tile = min(512, group)
    part = place.packed_rows

    def kernel(scal, *refs):
        refs = list(refs)
        ss = [refs.pop(0) for _ in range(n_stats)]
        (g_all, own_tabs, gain, mlp_gain, w, out_w, q_all, gq_ref, gq_t_ref, kv_own, h_ref, g_ref, gmlp_ref, stats_ref) = refs[:14]
        refs = refs[14:]
        if below:
            below_mixed, below_log, below_w = refs[:3]
            refs = refs[3:]
        pieces_out, g_out, payload_ref, dmix_out, delta_out = refs[:5]
        dm_all, log_all, delta_all, packed_t = refs[5:]
        own_at = pl.multiple_of(scal[2] * rows, rows)
        ends = place.ends(scal)
        gain_l = gain[layer : layer + 1]
        for slot in range(place.blocks):
            at = pl.multiple_of(place.position(scal, slot) * rows, rows)
            if below:
                flip = slot % place.n_head
                info = ss[slot // place.n_head][16 * flip : 16 * flip + 16].astype(f32)[:NH]
            else:
                info = ss[slot][rows : rows + 16].astype(f32)[:NH]
            log_all[:, pl.ds(at, rows)] = info[:, 0:128] + info[:, 128:256]
            delta_all[:, pl.ds(at, rows)] = info[:, 256:384] + info[:, 384:512]
        last_end = end_of(own_at + rows - 1, ends, group)

        def project(i, _):
            at = pl.multiple_of(i * tile, tile)
            dm_all[pl.ds(at, tile)] = dot_nt(g_all[pl.ds(at, tile)], out_w[...]).astype(bf16)
            return 0

        low, high = own_at // STEP, (last_end + STEP - 1) // STEP
        lax.fori_loop(low * (STEP // tile), high * (STEP // tile), project, 0)
        q_all = q_all.get()
        s_at = own_at + lax.broadcasted_iota(jnp.int32, (rows, 1), 0)
        k2 = [two_heads(kv_own[0:rows, 128 * p : 128 * p + 128]) for p in range(PAIRS)]
        v2 = [two_heads(kv_own[rows : 2 * rows, 128 * p : 128 * p + 128]) for p in range(PAIRS)]

        def keys(i, carry):
            at = pl.multiple_of(i * STEP, STEP)
            t = at + lax.broadcasted_iota(jnp.int32, (1, STEP), 1)
            start = start_of(t, ends)
            bias = jnp.where((s_at >= start) & (s_at <= t), 0.0, masked_value)
            new = []
            for p in range(PAIRS):
                dk, dv = carry[p]
                qs = q_all[pl.ds(at, STEP), 128 * p : 128 * p + 128]
                dms = dm_all[pl.ds(at, STEP), 128 * p : 128 * p + 128]
                scores = dot_nt(k2[p], qs)
                pulled = dot_nt(v2[p], dms)
                chances, grads = [], []
                for half in range(2):
                    n = 2 * p + half
                    part = slice(half * rows, half * rows + rows)
                    chance = jnp.exp(scores[part] + bias - log_all[n : n + 1, pl.ds(at, STEP)])
                    grads.append(chance * (pulled[part] - delta_all[n : n + 1, pl.ds(at, STEP)]))
                    chances.append(chance)
                chance = jnp.concatenate(chances, axis=0).astype(bf16)
                grad_s = jnp.concatenate(grads, axis=0).astype(bf16)
                new.append((dk + dot(grad_s, qs), dv + dot(chance, dms)))
            return tuple(new)

        zero = jnp.zeros((2 * rows, 128), f32)
        done = lax.fori_loop(low, high, keys, tuple((zero, zero) for _ in range(PAIRS)))
        tabs = [own_tabs[0:rows], -own_tabs[rows : 2 * rows], -own_tabs[2 * rows : 3 * rows]]
        grad_k = [rope(one_pair(done[p][0]), *tabs).astype(bf16) for p in range(PAIRS)]
        grad_v = [one_pair(done[p][1]).astype(bf16) for p in range(PAIRS)]
        w = w.get()
        grad_in = dot_nt(gq_ref.get()[...], w[:, 0:D])
        for j, parts in ((1, grad_k), (2, grad_v)):
            grad_in += dot_nt(jnp.concatenate(parts, axis=1), w[:, j * D : j * D + D])

        normal, inverse = norm_parts(h_ref.get()[...].astype(f32))
        grad_mlp = gmlp_ref.get()[...]
        grad_normal = grad_in * gain_l + grad_mlp * mlp_gain[layer : layer + 1]
        back = inverse * (
            grad_normal
            - jnp.mean(grad_normal, axis=-1, keepdims=True)
            - normal * jnp.mean(grad_normal * normal, axis=-1, keepdims=True)
        )
        g_new = g_ref.get()[...].astype(f32) + back
        g_out[...] = g_new

        sums = [
            jnp.sum(v, axis=0, keepdims=True)
            for v in (grad_in * normal, grad_in, grad_mlp * normal, grad_mlp)
        ]
        for j in range(3):
            for p in range(PAIRS):
                if j == 0:
                    turned = gq_t_ref.get()[128 * p : 128 * p + 128]
                else:
                    turned = (grad_k, grad_v)[j - 1][p].astype(f32).T.astype(bf16)
                for half in range(2):
                    at = (2 * p + half) * 3 * HD + j * HD
                    packed_t[at : at + HD] = turned[half * HD : half * HD + HD]
        layer_sums = jnp.where(lane_of(8) < 4, stats_ref[...], 0.0)
        layer_sums = jnp.broadcast_to(pltpu.roll(layer_sums, scal[2] * 4, 1)[0:1], (16, 128))
        row16 = lax.broadcasted_iota(jnp.int32, (16, 128), 0)
        for p in range(place.n_head):
            extra = jnp.concatenate([x[:, 128 * p : 128 * p + 128] for x in sums] + [jnp.zeros((4, 128), f32)], axis=0)
            extra = jnp.concatenate([extra, extra], axis=0)
            extra = jnp.where((row16 & 7) == 4, layer_sums, extra)
            high, rest = split_low(extra)
            extra = jnp.where(row16 < 8, high, rest)
            for c in range(place.n_ctx):
                at = (p * place.n_ctx + c) * part
                pieces_out[c * place.n_head + p, 0:part] = packed_t[at : at + part]
                pieces_out[c * place.n_head + p, part : part + 16] = extra

        g_low = g_new.astype(bf16)
        if below:
            payload_ref[0:rows] = g_low
            dmix = dot_nt(below_w.get()[...], g_low).astype(bf16)
            dmix_out[...] = dmix
            deltas = delta_rows(dmix, below_mixed.get()[...])
            delta_out[...] = deltas
            payload_ref[rows : rows + 16] = stat_payload(below_log[...], deltas)
        else:
            payload_ref[...] = jnp.zeros_like(payload_ref)
            dmix_out[...] = jnp.zeros_like(dmix_out)
            delta_out[...] = jnp.zeros_like(delta_out)

    ins = [
        *stats,
        g_whole,
        own_tables,
        params["attn_gain"],
        params["mlp_gain"],
        lazy_layer(params["qkv_sorted"], layer),
        (params["out_weight"], layer),
        *[Lazy(x) for x in queries],
        kept["kv_own"],
        Lazy(kept["hidden"]),
        Lazy(grad),
        Lazy(grad_mlp_in),
        kept["stats"],
    ]
    if below:
        ins += [Lazy(mixed_below["mixed"]), mixed_below["log"], lazy_layer(params["out_weight"], layer - 1)]
    outs = [
        sds((place.blocks, part + 16, rows), bf16),
        sds((rows, D), f32),
        sds((rows + 16, D) if below else (16, D), bf16),
        sds((D, rows) if below else (16, rows), bf16),
        sds((NH, rows), f32),
    ]
    scratch = [VMEM((group, D), bf16), VMEM((NH, group), f32), VMEM((NH, group), f32), VMEM((3 * D, rows), bf16)]
    return call(kernel, ins, outs, scratch, scalars, flops=60 * 10**9)


def mlp_weight_grads(place, scalars, blocks, normal_all, params, layer, mixed=None):
    group, rows, units = place.group, place.rows, place.units
    tile = min(512, group)
    size = 0 if mixed is None else place.mixed_rows

    def kernel(scal, *refs):
        gs = refs[: place.blocks]
        refs = list(refs[place.blocks :])
        mixed_ref, other_ref = (refs.pop(0), refs.pop(0)) if size else (None, None)
        normal_ref, gain, shift, up, up_b, down, g_out, up_out, down_out = refs[:9]
        g_ref = g_out.ref
        mixed_t = refs[9] if size else None
        gain_l, shift_l = gain[layer : layer + 1], shift[layer : layer + 1]
        for slot in range(place.blocks):
            at = pl.multiple_of(place.position(scal, slot) * rows, rows)
            g_ref[pl.ds(at, rows)] = gs[slot][0:rows]
            if size:
                mixed_t[:, slot * rows : (slot + 1) * rows] = mixed_ref[slot]

        g_out.send()

        def step(i, carry):
            up_t, down_g, bias, g_sum = carry
            at = pl.multiple_of(i * tile, tile)
            x = (normal_ref[pl.ds(at, tile)].astype(f32) * gain_l + shift_l).astype(bf16)
            g = g_ref[pl.ds(at, tile)]
            gate = dot(x, up[...]) + up_b[...]
            cdf = 0.5 * (1.0 + lax.erf(gate * math.sqrt(0.5)))
            pdf = jnp.exp(-0.5 * gate * gate) * (1.0 / math.sqrt(2.0 * math.pi))
            acted = (gate * cdf).astype(bf16)
            grad_gate = (dot_nt(g, down[...]) * (cdf + gate * pdf)).astype(bf16)
            up_t += dot(grad_gate.T, x)
            down_g += dot(acted.T, g)
            bias += jnp.sum(grad_gate.astype(f32), axis=0, keepdims=True)
            g_sum += jnp.sum(g.astype(f32), axis=0, keepdims=True)
            return up_t, down_g, bias, g_sum

        zero = jnp.zeros((units, D), f32)
        up_t, down_g, bias, g_sum = lax.fori_loop(
            0, group // tile, step, (zero, zero, jnp.zeros((1, units), f32), jnp.zeros((1, D), f32))
        )
        up_out[0:units] = up_t.astype(bf16)
        if units < 128:
            bias = jnp.concatenate([bias, jnp.zeros((1, 128 - units), f32)], axis=1)
        wide = jnp.concatenate([bias, jnp.zeros((1, D - 128), f32)], axis=1)
        row = lax.broadcasted_iota(jnp.int32, (32, D), 0)
        extra = jnp.where((row & 7) == 0, wide, jnp.where((row & 7) == 1, g_sum, 0.0))
        high, rest = split_low(extra)
        up_out[units : units + 32] = jnp.where(row < 8, high, jnp.where(row < 16, rest, jnp.zeros_like(rest)))
        if size:
            out_g = [dot(mixed_t[k * size : (k + 1) * size], g[...]) for k, g in enumerate((g_ref, other_ref))]
        for p in range(place.n_head):
            cols = slice(128 * p, 128 * p + 128)
            down_out[p, 0:units] = down_g[:, cols].astype(bf16)
            for k in range(2 if size else 0):
                down_out[p, units + k * size : units + (k + 1) * size] = out_g[k][:, cols].astype(bf16)

    up, up_b, down = params["units"][layer]
    made = call(
        kernel,
        [*blocks, *([] if mixed is None else mixed), normal_all, params["mlp_gain"], params["mlp_shift"], up, up_b, down],
        [Out((group, D), bf16), sds((units + 32, D), bf16), sds((place.n_head, units + 2 * size, 128), bf16)],
        [VMEM((2 * size, group), bf16)] if size else [],
        scalars,
        flops=4 * 2 * group * D * units,
    )
    return made


def attention_weight_grads(place, scalars, received, normal_all, params, layer):
    group, rows, part = place.group, place.rows, place.packed_rows
    tile = min(512, group)

    def kernel(received_ref, normal_ref, gain, shift, out_ref, chunk_t):
        gain_l, shift_l = gain[layer : layer + 1], shift[layer : layer + 1]
        extra = jnp.zeros((16, 128), f32)
        for j in range(place.blocks):
            chunk_t[:, j * rows : (j + 1) * rows] = received_ref[j, 0:part]
            extra += received_ref[j, part : part + 16].astype(f32)
        total = jnp.zeros((part, D), f32)
        for at in range(0, group, tile):
            x = (normal_ref[at : at + tile].astype(f32) * gain_l + shift_l).astype(bf16)
            total += dot(chunk_t[:, at : at + tile], x)
        out_ref[0:part] = total.astype(bf16)
        bias = dot_nt(jnp.ones((16, group), bf16), chunk_t[...])
        bias = jnp.concatenate([bias, jnp.zeros((16, 128 - part), f32)], axis=1)
        extra = extra[0:8] + extra[8:16]
        wide = jnp.concatenate([extra[k : k + 1] for k in range(4)], axis=1)
        none = jnp.zeros((1, D - 256), f32)
        second = jnp.concatenate([bias[0:1], extra[4:5], none], axis=1)
        row = lax.broadcasted_iota(jnp.int32, (16, D), 0)
        high, rest = split_low(jnp.where((row & 7) == 0, wide, jnp.where((row & 7) == 1, second, 0.0)))
        out_ref[part : part + 16] = jnp.where(row < 8, high, rest)

    return call(
        kernel,
        [received, normal_all, params["attn_gain"], params["attn_shift"]],
        [sds((part + 16, D), bf16)],
        [VMEM((part, group), bf16)],
        flops=2 * group * D * part,
    )[0]


def pack_mlp(place, scalars, up_share, pieces, halves):
    rows = place.units + 32 + pieces.shape[1]
    half = rows // 2

    def kernel(scal, up_ref, pieces_ref, *refs):
        if halves:
            mine, other, full = refs
        else:
            (full,) = refs
        full[0 : place.units + 32] = up_ref[...]
        for p in range(place.n_head):
            full[place.units + 32 :, 128 * p : 128 * p + 128] = pieces_ref[p]
        if halves:
            at = pl.multiple_of(scal[7] * half, half)
            mine[...] = full[pl.ds(at, half)]
            other[...] = full[pl.ds(pl.multiple_of(half - at, half), half)]

    outs = [sds((half, D), bf16)] * 2 if halves else [sds((rows, D), bf16)]
    scratch = [VMEM((rows, D), bf16)] if halves else []
    return call(kernel, [up_share, pieces], outs, scratch, scalars, flops=10**7)


def along_lanes(rows, width):
    if width == 128:
        return jnp.concatenate(rows, axis=1)
    full = len(rows) * width
    out = jnp.zeros((8, full), f32)
    for k, row in enumerate(rows):
        lane = lax.broadcasted_iota(jnp.int32, (8, full), 1)
        row = jnp.concatenate([row, jnp.zeros((1, full - 128), f32)], axis=1)
        row = jnp.where(lane < width, jnp.broadcast_to(row, (8, full)), 0.0)
        out += pltpu.roll(row, k * width, 1) if k else row
    return out[0:1]


def whole_shares(place, scal, refs, at, size, full, halves):
    if not halves:
        return [x.at[at : at + size] for x in refs]
    half = size // 2
    for s in range(place.n_ctx):
        full[s, pl.ds(pl.multiple_of(scal[7] * half, half), half)] = refs[s][at : at + half]
        start = s * half
        full[s, pl.ds(pl.multiple_of((1 - scal[7]) * half, half), half)] = refs[-1][start : start + half]
    return [full.at[s] for s in range(place.n_ctx)]


def place_mlp(place, scalars, shares, layer, into):
    n_ctx, units = place.n_ctx, place.units
    taken = 0 if into is None else 2
    halves = len(shares) > n_ctx
    size = place.mixed_rows if layer == 0 else 0
    rows = 2 * units + 32 + 2 * size

    def kernel(scal, *refs):
        up_out, down_out, small_out, *out_outs, up_t, bias_rows, full = refs[len(shares) + taken :]
        ordered = len(shares) == 1
        if ordered:
            srcs = [refs[0].at[c * rows : (c + 1) * rows] for c in range(n_ctx)]
        else:
            srcs = whole_shares(place, scal, refs[: len(shares)], 0, rows, full, halves)
        for s in range(n_ctx):
            c = s if ordered else lax.rem(scal[0] - s + n_ctx, n_ctx)
            at = pl.multiple_of(c * units, units)
            up_t[pl.ds(at, units)] = srcs[s][0:units].astype(f32)
            extra = srcs[s][units : units + 16].astype(f32)
            extra = extra[0:8] + extra[8:16]
            bias_rows[c] = jnp.broadcast_to(extra[0:1, :128], (8, 128))
            if s == 0:
                small_out[...] = jnp.zeros_like(small_out)
                for q in range(place.n_head):

                    @pl.when(scal[1] == q)
                    def _():
                        small_out[1:2, 0:128] = extra[1:2, 128 * q : 128 * q + 128]

            for p in range(place.n_head):
                at = pl.multiple_of(p * (FF // place.n_head) + c * units, units)
                base = units + 32
                down_out[pl.ds(at, units)] = srcs[s][base : base + units, 128 * p : 128 * p + 128].astype(f32)
                at = pl.multiple_of(p * 128 + c * place.mixed_rows, place.mixed_rows)
                for k in range(2 if size else 0):
                    start = base + units + k * size
                    out_outs[0][k, pl.ds(at, size)] = srcs[s][start : start + size, 128 * p : 128 * p + 128].astype(f32)
        up_out[...] = up_t[...].T
        small_out[0:1] = along_lanes([bias_rows[c][0:1] for c in range(n_ctx)], units)

    wide = FF // place.n_head
    return call(
        kernel,
        shares,
        [
            (sds((LAYERS, D, wide), f32), layer),
            (sds((LAYERS, FF, 128), f32), layer),
            sds((8, wide), f32),
            *([sds((LAYERS, D, 128), f32)] if size else []),
        ],
        [VMEM((wide, D), f32), VMEM((n_ctx, 8, 128), f32), VMEM((n_ctx, rows, D) if halves else (1, 16, D), bf16)],
        scalars,
        flops=10**7,
        into=into,
    )


def place_attention(place, scalars, shares, layer, into, smalls=None, count=1):
    n_ctx, part = place.n_ctx, place.packed_rows
    taken = 0 if into is None else 1
    wide = 3 * D // place.n_head
    wide_up = FF // place.n_head
    given = [] if smalls is None else smalls

    def kernel(scal, *refs):
        shares_in, given_in = refs[: len(shares)], refs[len(shares) : len(shares) + len(given)]
        qkv_out, *small_outs, qkv_t, info, small = refs[len(shares) + len(given) + taken :]
        small[...] = jnp.zeros_like(small)
        for s in range(n_ctx):
            c = lax.rem(scal[0] - s + n_ctx, n_ctx)
            at = pl.multiple_of(c * part, part)
            qkv_t[pl.ds(at, part)] = shares_in[s][0:part].astype(f32)
            extra = shares_in[s][part : part + 16].astype(f32)
            extra = extra[0:8] + extra[8:16]
            info[c] = extra
            if s == 0:
                for k in range(4):
                    small[k : k + 1, 0:128] = extra[0:1, 128 * k : 128 * k + 128]
                small[4:5, 0:128] = extra[1:2, 128:256]
        qkv_out[...] = qkv_t[...].T
        small[5:6] = along_lanes([info[c, 1:2, 0:128] for c in range(n_ctx)], part)
        if smalls is None:
            small_outs[0][...] = small[...]
            return
        attn_1, mlp_0, mlp_1 = given_in
        lane = lane_of(1)
        for spot, attn, mlp in ((0, small, mlp_0), (1, attn_1, mlp_1)):
            row = slice(spot, spot + 1)
            for k in range(4):
                small_outs[k][row] = attn[k : k + 1, 0:128]
            small_outs[4][row] = attn[5:6]
            small_outs[5][row] = mlp[0:1]
            small_outs[6][row] = mlp[1:2, 0:128]
            small_outs[7][row] = mlp[1:2, 0:128]
            for k in range(3):
                picked = jnp.where((lane & 3) == k, attn[4:5, 0:128], 0.0)
                small_outs[8][row, k : k + 1] = jnp.sqrt(jnp.sum(picked, axis=1, keepdims=True) * (1.0 / count))

    if smalls is None:
        outs = [sds((8, wide), f32)]
    else:
        widths = [128, 128, 128, 128, wide, wide_up, 128, 128, 3]
        outs = [sds((LAYERS, width), f32) for width in widths]
    return call(
        kernel,
        [*shares, *given],
        [(sds((LAYERS, D, wide), f32), layer), *outs],
        [
            VMEM((wide, D), f32),
            VMEM((n_ctx, 8, D), f32),
            VMEM((8, wide), f32),
        ],
        scalars,
        flops=10**7,
        into=into,
    )


def prepare(place, lengths, qkv_weight, qkv_bias):
    group = place.group
    blocks = group // 128
    dim = jnp.arange(128, dtype=jnp.int32)[None, :] % HD
    freq = rope_base ** (-2.0 * (dim % (ROT // 2)).astype(f32) / ROT)
    starts = jnp.concatenate([jnp.zeros((1,), jnp.int32), lengths[0, :3]])
    starts = jnp.stack([starts[0], starts[1], starts[1] + starts[2], starts[1] + starts[2] + starts[3]])
    first = (jnp.arange(blocks, dtype=jnp.int32)[:, None] * 128 - starts[None, :]).reshape(-1, 1)
    whole = jnp.concatenate([first, jnp.arange(128, dtype=jnp.int32)[:, None]], axis=0).astype(f32) * freq
    cosines, sines = jnp.cos(whole), jnp.sin(whole)
    base = 4 * blocks

    def kernel(scal, w_ref, b_ref, cos_ref, sin_ref, w_out, b_out, cos_t, left_t, right_t, own_t):
        def sort(read, write):
            for p in range(PAIRS):
                a, b, c = (read(slice(128 * (3 * p + i), 128 * (3 * p + i) + 128)).astype(f32) for i in range(3))
                first = lane_of(a.shape[0]) < HD
                made = (jnp.where(first, a, b), pltpu.roll(jnp.where(first, c, a), HD, 1), jnp.where(first, b, c))
                for j in range(3):
                    write(slice(j * D + 128 * p, j * D + 128 * p + 128), made[j])

        for layer in range(LAYERS):

            def store(to, x, layer=layer):
                w_out[layer, :, to] = x.astype(bf16)

            sort(lambda at, layer=layer: w_ref[layer, :, at], store)

        def store_bias(to, x):
            b_out[:, to] = x

        sort(lambda at: b_ref[:, at], store_bias)
        ends = place.ends(scal)
        dim = lane_of(128) & (HD - 1)
        cos_b, sin_b = cos_ref[base : base + 128], sin_ref[base : base + 128]

        def table(i, _):
            at = pl.multiple_of(i * 128, 128)
            t = at + lax.broadcasted_iota(jnp.int32, (128, 1), 0)
            cos_a, sin_a = cos_ref[pl.ds(4 * i, 1)], sin_ref[pl.ds(4 * i, 1)]
            for k in range(1, 4):
                later = t >= ends[k - 1]
                cos_a = jnp.where(later, cos_ref[pl.ds(4 * i + k, 1)], cos_a)
                sin_a = jnp.where(later, sin_ref[pl.ds(4 * i + k, 1)], sin_a)
            cosine = cos_a * cos_b - sin_a * sin_b
            sine = sin_a * cos_b + cos_a * sin_b
            cos_t[pl.ds(at, 128)] = jnp.where(dim < ROT, cosine, 1.0)
            left_t[pl.ds(at, 128)] = jnp.where(dim < ROT // 2, -sine, 0.0)
            right_t[pl.ds(at, 128)] = jnp.where((dim >= ROT // 2) & (dim < ROT), sine, 0.0)
            return 0

        lax.fori_loop(0, blocks, table, 0)
        own_at = pl.multiple_of(scal[2] * place.rows, place.rows)
        for k, ref in enumerate((cos_t, left_t, right_t)):
            own_t[k * place.rows : (k + 1) * place.rows] = ref[pl.ds(own_at, place.rows)]

    bias = jnp.concatenate([qkv_bias, jnp.zeros((8 - LAYERS, 3 * D), f32)], axis=0)
    made = call(
        kernel,
        [qkv_weight, bias, cosines, sines],
        [sds(qkv_weight.shape, bf16), sds((8, 3 * D), f32), *[sds((group, 128), f32)] * 3, sds((3 * place.rows, 128), f32)],
        (),
        lengths,
        flops=10**7,
    )
    return made[0], made[1], made[2:5], made[5]


def tie(x, *after):
    return lax.optimization_barrier((x, *after))[0] if after else x


def flip_heads(x, flip):
    return lax.ppermute(x, "head", [(i, i ^ flip) for i in range(lax.axis_size("head"))])


def turn_ctx(x, shift):
    n = lax.axis_size("ctx")
    return lax.ppermute(x, "ctx", [(i, (i + shift) % n) for i in range(n)])


def gather_rings(own):
    return [own] + [turn_ctx(own, s) for s in range(1, lax.axis_size("ctx"))]


def gather_flips(rings, flip, *after):
    return [flip_heads(tie(x, *after), flip) for x in rings]


def by_slot(rings, far, near, far_near):
    return [x for four in zip(rings, near, far, far_near) for x in four]


def with_flip(own, flip):
    return jnp.concatenate([own, flip_heads(own, flip)], axis=0)


def swap_dp(x):
    return lax.ppermute(x, "dp", [(0, 1), (1, 0)])


def per_device(
    hidden_in,
    lengths,
    attn_gain,
    attn_shift,
    mlp_gain,
    mlp_shift,
    qkv_weight,
    qkv_bias,
    out_weight,
    out_bias,
    up_weight,
    up_bias,
    down_weight,
    down_bias,
    cotangent,
):
    rows = hidden_in.shape[0]
    n_dp, n_ctx, n_head = (lax.axis_size(a) for a in ("dp", "ctx", "head"))
    place = Place(n_dp, n_ctx, n_head, rows)
    group = place.group
    scalars = lengths
    qkv_sorted, qkv_bias_sorted, tables, own_tables = prepare(place, lengths, qkv_weight, qkv_bias)
    params = {
        "attn_gain": attn_gain,
        "attn_shift": attn_shift,
        "mlp_gain": mlp_gain,
        "mlp_shift": mlp_shift,
        "qkv_sorted": qkv_sorted,
        "qkv_bias_sorted": qkv_bias_sorted,
        "out_weight": out_weight,
        "out_bias": out_bias,
        "up_weight": up_weight,
        "up_bias": up_bias,
        "down_weight": down_weight,
        "down_bias": down_bias,
    }
    def attention(layer, blocks, hidden, mlp_out, last_grad):
        names = ("normal_all", "k_all", "v_all", "q_own", "kv_own", "mixed", "mixed_low", "log", "delta", "dmix", "h_out", "stats", "low")
        made = attention_forward(place, scalars, blocks, tables, params, layer, hidden, mlp_out, last_grad)
        return dict(zip(names, made), hidden=hidden)

    def backward_queries(layer, kept):
        return query_backward(place, scalars, tables, own_tables, params, layer, kept)

    def backward_keys(layer, g_all, stats, kept, queries, grad, grad_mlp_in, below):
        return key_backward(
            place, scalars, g_all, stats, own_tables, params, layer, kept, queries, grad, grad_mlp_in, below
        )

    def head_swap(pieces):
        return lax.all_to_all(pieces, "head", 0, 0, tiled=True)

    def group_swap(pieces):
        return lax.all_to_all(pieces, ("ctx", "head"), 0, 0, tiled=True)

    def reduce_mlp(up_share, pieces, halves):
        made = pack_mlp(place, scalars, up_share, pieces, halves)
        if n_dp == 2:
            return (made[0].astype(f32) + swap_dp(made[-1]).astype(f32)).astype(bf16)
        return lax.psum(made[0], "dp")

    def sum_dp(x):
        if n_dp == 2:
            return (x.astype(f32) + swap_dp(x).astype(f32)).astype(bf16)
        return lax.psum(x, "dp")

    def finish(rings):
        return [*rings, swap_dp(jnp.concatenate(rings, axis=0))] if n_dp == 2 else rings

    together = lax.optimization_barrier

    mlp_0, factor_0, _ = mlp_forward(hidden_in, params, 0)
    rings, mlp_0, factor_0 = together((gather_rings(hidden_in), mlp_0, factor_0))
    far = gather_flips(rings, 2)
    far, rings, params["qkv_sorted"], tables, own_tables = together((far, rings, qkv_sorted, tables, own_tables))
    near, far_near = together((gather_flips(rings, 1), gather_flips(far, 1)))
    first, cot_rings = together(
        (attention(0, by_slot(rings, far, near, far_near), hidden_in, mlp_0, None), gather_rings(tie(cotangent, near)))
    )
    hidden, low = first["h_out"], first["low"]
    units = place.units
    at = lax.axis_index("head") * (FF // n_head) + lax.axis_index("ctx") * units
    params["units"] = [
        (
            lax.dynamic_slice(tie(up_weight, first["low"]), (layer, 0, at), (1, D, units))[0],
            lax.dynamic_slice(tie(up_bias, first["low"]), (layer, at), (1, units)),
            lax.dynamic_slice(tie(down_weight, first["low"]), (layer, at, 0), (1, units, D))[0],
        )
        for layer in range(LAYERS)
    ]
    mlp_1, back_1 = mlp_both(hidden, cotangent, params, 1)
    rings, mlp_1, back_1 = together((gather_rings(low), mlp_1, back_1))
    far, rings, params["units"] = together((gather_flips(rings, 2), rings, params["units"]))
    near, far_near = together((gather_flips(rings, 1), gather_flips(far, 1)))
    second = attention(1, by_slot(rings, far, near, far_near), hidden, mlp_1, [cotangent, first["mixed_low"]])
    second, cot_far, cot_rings = together((second, gather_flips(cot_rings, 2, near), cot_rings))
    output_rows, low = second["h_out"], second["low"]

    pair, cot_near, cot_far_near = together((with_flip(low, 1), gather_flips(cot_rings, 1), gather_flips(cot_far, 1)))
    made = mlp_weight_grads(
        place, scalars, by_slot(cot_rings, cot_far, cot_near, cot_far_near), second["normal_all"], params, 1
    )
    (cot_all, up_share_1, pieces_1), four = together((made, with_flip(pair, 2)))
    queries_1, stats = together((backward_queries(1, second), gather_rings(four)))
    made = backward_keys(1, cot_all, stats, second, queries_1, cotangent, back_1, first)
    (packed_1, grad, payload, dmix, delta), mixed = together((made, group_swap(second["mixed_low"])))
    first["dmix"], first["delta"] = dmix, delta
    back_0 = mlp_backward(grad, factor_0, hidden_in, params, 0)
    rings, back_0, pieces_1 = together((gather_rings(payload), back_0, head_swap(tie(pieces_1, payload))))
    half_1 = reduce_mlp(up_share_1, pieces_1, n_dp == 2)
    far, rings, queries_0, half_1, received_1 = together(
        (
            gather_flips(rings, 2),
            rings,
            backward_queries(0, dict(first, delta=tie(delta, back_0))),
            half_1,
            group_swap(tie(packed_1, back_0)),
        )
    )
    near, far_near = together((gather_flips(rings, 1), gather_flips(far, 1)))
    blocks = by_slot(rings, far, near, far_near)
    mlp_rings_1 = gather_rings(tie(half_1, near))
    g_all, up_share_0, pieces_0 = mlp_weight_grads(
        place, scalars, blocks, first["normal_all"], params, 0, [mixed, cot_all]
    )
    made = backward_keys(0, g_all, blocks, first, queries_0, grad, back_0, None)
    (packed_0, grad, _, _, _), pieces_0, mlp_rings_1, up_share_0, received_1 = together(
        (made, head_swap(pieces_0), mlp_rings_1, up_share_0, received_1)
    )
    half_0 = reduce_mlp(up_share_0, pieces_0, n_dp == 2)
    mlp_rings_0 = gather_rings(half_0)
    share_1 = attention_weight_grads(place, scalars, tie(received_1, half_0), second["normal_all"], params, 1)
    sum_1 = sum_dp(share_1)
    received_0, sum_1, mlp_rings_0, mlp_shares_1 = together(
        (group_swap(packed_0), sum_1, mlp_rings_0, finish([tie(x, half_0) for x in mlp_rings_1]))
    )
    share_0 = attention_weight_grads(place, scalars, received_0, first["normal_all"], params, 0)
    *big, mlp_small_1 = place_mlp(place, scalars, [tie(mlp_shares_1[0], share_0), *mlp_shares_1[1:]], 1, None)
    sum_0 = sum_dp(share_0)
    mlp_shares_0 = finish([tie(x, sum_0) for x in mlp_rings_0])
    sum_0, attn_rings_1, big, mlp_small_1 = together((sum_0, gather_rings(sum_1), big, mlp_small_1))
    *attn_big, attn_small_1 = place_attention(place, scalars, attn_rings_1, 1, None)
    up_grad, down_grad, mlp_small_0, out_grad = place_mlp(place, scalars, mlp_shares_0, 0, big)
    attn_rings_0, mlp_small_0, attn_big, attn_small_1 = together(
        (gather_rings(sum_0), mlp_small_0, attn_big, attn_small_1)
    )
    qkv_grad, gain, shift, mlp_g, mlp_s, qkv_b, up_b, down_b, out_b, layer_stats = place_attention(
        place, scalars, attn_rings_0, 0, attn_big, [attn_small_1, mlp_small_0, mlp_small_1], group * n_dp * D
    )
    return (
        output_rows, grad, gain, shift, mlp_g, mlp_s, qkv_grad, qkv_b, out_grad, out_b, up_grad, up_b, down_grad, down_b, layer_stats
    )


def solution(mesh):
    rows = P(("dp", "ctx", "head"), None)
    return jax.shard_map(
        per_device,
        mesh=mesh,
        in_specs=(rows, P("dp", None), *([P()] * 12), rows),
        out_specs=(
            rows,
            rows,
            P(None, "head"),
            P(None, "head"),
            P(None, "head"),
            P(None, "head"),
            P(None, None, "head"),
            P(None, "head"),
            P(None, None, "head"),
            P(None, "head"),
            P(None, None, "head"),
            P(None, "head"),
            P(None, None, "head"),
            P(None, "head"),
            P(),
        ),
        check_vma=False,
    )
```

```python
import math

import jax
import jax.numpy as jnp
from jax import lax
from jax.experimental import pallas as pl
from jax.experimental.pallas import tpu as pltpu
from jax.sharding import PartitionSpec as P

D = 512
FF = 2048
NH = 8
HD = 64
ROT = 16
LAYERS = 2
PAIRS = NH // 2
epsilon = 1e-05
masked_value = -1e30
score_scale = 0.125
rope_base = 10000.0
f32 = jnp.float32
bf16 = jnp.bfloat16
STEP = 1024
VMEM = pltpu.VMEM


def dot(a, b):
    return lax.dot_general(a, b, (((1,), (0,)), ((), ())), preferred_element_type=f32)


def dot_nt(a, b):
    return lax.dot_general(a, b, (((1,), (1,)), ((), ())), preferred_element_type=f32)


def norm_parts(hidden):
    centred = hidden - jnp.mean(hidden, axis=-1, keepdims=True)
    inverse = lax.rsqrt(jnp.mean(centred * centred, axis=-1, keepdims=True) + epsilon)
    return centred * inverse, inverse


def rope(x, cos_t, left_t, right_t):
    return x * cos_t + pltpu.roll(x, 128 - 8, 1) * left_t + pltpu.roll(x, 8, 1) * right_t


def start_of(place, ends):
    start = jnp.zeros_like(place)
    for end in ends:
        start = jnp.where(end <= place, end, start)
    return start


def end_of(place, ends, size):
    found = jnp.int32(size)
    for end in reversed(ends):
        found = jnp.where(place < end, end, found)
    return found


def split_low(x):
    high = x.astype(bf16)
    return high, (x - high.astype(f32)).astype(bf16)


def lane_of(rows):
    return lax.broadcasted_iota(jnp.int32, (rows, 128), 1)


def two_heads(x):
    first = lane_of(x.shape[0]) < HD
    zero = jnp.zeros_like(x)
    return jnp.concatenate([jnp.where(first, x, zero), jnp.where(first, zero, x)], axis=0)


def one_pair(x):
    rows = x.shape[0] // 2
    return jnp.where(lane_of(rows) < HD, x[:rows], x[rows:])


def dot_tn(a, b):
    return lax.dot_general(a, b, (((0,), (0,)), ((), ())), preferred_element_type=f32)


def two_heads_t(x):
    first = lax.broadcasted_iota(jnp.int32, x.shape, 0) < HD
    zero = jnp.zeros_like(x)
    return jnp.concatenate([jnp.where(first, x, zero), jnp.where(first, zero, x)], axis=1)


def one_pair_t(x):
    rows = x.shape[1] // 2
    return jnp.where(lax.broadcasted_iota(jnp.int32, (128, rows), 0) < HD, x[:, :rows], x[:, rows:])


def rope_t(x, cos_t, left_t, right_t):
    return x * cos_t + pltpu.roll(x, 128 - 8, 0) * left_t + pltpu.roll(x, 8, 0) * right_t


class Far:
    def __init__(self, array):
        self.array = array


class Lazy:
    def __init__(self, array, at=None, shape=None):
        self.array, self.at = array, at or (lambda ref: ref)
        self.shape = shape or array.shape


class Out:
    def __init__(self, shape, dtype):
        self.shape, self.dtype = shape, dtype


class Coming:
    def __init__(self, ref, copy):
        self.ref, self.copy, self.there = ref, copy, False

    def get(self):
        if not self.there:
            self.copy.wait()
            self.there = True
        return self.ref


class Going:
    def __init__(self, ref, copy):
        self.ref, self.copy, self.gone = ref, copy, False

    def send(self):
        self.copy.start()
        self.gone = True


def call(kernel, ins, outs, scratch=(), scalars=None, vmem=60 << 20, flops=10**9, into=None):
    specs, arrays = [], []

    def block(shape, layer, cols=None):
        place = (layer, *([0] * (len(shape) - 1)))
        return pl.BlockSpec((None, *shape[1:-1], cols or shape[-1]), lambda i: place)

    def whole(shape):
        return pl.BlockSpec(shape, lambda i: (0,) * len(shape))

    n_ins, n_outs = len(ins), len(outs)
    lead = 0
    if scalars is not None:
        specs.append(pl.BlockSpec(memory_space=pltpu.SMEM))
        arrays.append(scalars)
        lead = 1
    for item in ins:
        if isinstance(item, (Far, Lazy)):
            specs.append(pl.BlockSpec(memory_space=pl.ANY))
            arrays.append(item.array)
            continue
        array = item[0] if isinstance(item, tuple) else item
        specs.append(block(array.shape, *item[1:]) if isinstance(item, tuple) else whole(array.shape))
        arrays.append(array)
    aliases = {}
    if into is not None:
        spots = [k for k, o in enumerate(outs) if isinstance(o, tuple)]
        for spot, array in zip(spots, into):
            aliases[len(arrays)] = spot
            specs.append(pl.BlockSpec(memory_space=pl.ANY))
            arrays.append(array)
    shapes, out_specs = [], []
    for o in outs:
        if isinstance(o, tuple):
            shapes.append(o[0])
            out_specs.append(block(o[0].shape, o[1]))
        elif isinstance(o, Out):
            shapes.append(sds(o.shape, o.dtype))
            out_specs.append(pl.BlockSpec(memory_space=pl.ANY))
        else:
            shapes.append(o)
            out_specs.append(whole(o.shape))
    coming = [k for k, item in enumerate(ins) if isinstance(item, Lazy)]
    going = [k for k, o in enumerate(outs) if isinstance(o, Out)]
    slow = [VMEM(ins[k].shape, ins[k].array.dtype) for k in coming] + [VMEM(outs[k].shape, outs[k].dtype) for k in going]
    if slow:
        slow.append(pltpu.SemaphoreType.DMA((len(slow),)))

    def body(*refs):
        refs = list(refs)
        given = []
        if scalars is not None:
            lengths_ref = refs.pop(0)
            ctx, head = lax.axis_index("ctx"), lax.axis_index("head")
            ends = [lengths_ref[0, 0]]
            for k in range(1, 4):
                ends.append(ends[-1] + lengths_ref[0, k])
            given = [[ctx, head, ctx * lax.axis_size("head") + head, *ends, lax.axis_index("dp")]]
        finals = []
        if slow:
            extra = refs[len(refs) - len(slow) :]
            refs = refs[: len(refs) - len(slow)]
            sems = extra[-1]
            for j, k in enumerate(coming):
                copy = pltpu.make_async_copy(ins[k].at(refs[k]), extra[j], sems.at[j])
                copy.start()
                refs[k] = Coming(extra[j], copy)
            first_out = len(arrays) - lead
            for j, k in enumerate(going):
                j += len(coming)
                refs[first_out + k] = Going(extra[j], pltpu.make_async_copy(extra[j], refs[first_out + k], sems.at[j]))
                finals.append(refs[first_out + k])
        kernel(*given, *refs)
        for item in finals:
            if not item.gone:
                item.send()
        for item in finals:
            item.copy.wait()

    moved = sum(x.size * x.dtype.itemsize for x in arrays)
    return pl.pallas_call(
        body,
        grid=(1,),
        in_specs=specs,
        out_specs=out_specs,
        out_shape=shapes,
        scratch_shapes=[*scratch, *slow],
        input_output_aliases=aliases,
        compiler_params=pltpu.CompilerParams(vmem_limit_bytes=vmem),
        cost_estimate=pl.CostEstimate(flops=flops, bytes_accessed=moved, transcendentals=0),
    )(*arrays)


def lazy_layer(array, layer, cols=None):
    if cols is None:
        return Lazy(array, lambda ref: ref.at[layer], array.shape[1:])
    return Lazy(array, lambda ref: ref.at[layer, :, 0:cols], (*array.shape[1:-1], cols))


def sds(shape, dtype):
    return jax.ShapeDtypeStruct(shape, dtype)


def mlp_forward(hidden, params, layer):
    rows = hidden.shape[0]

    def kernel(h_ref, gain, shift, up, up_b, down, down_b, out_ref, factor_ref, normal_ref):
        normal, _ = norm_parts(h_ref[...].astype(f32))
        normal_ref[...] = normal.astype(bf16)
        x = (normal * gain[layer : layer + 1] + shift[layer : layer + 1]).astype(bf16)
        total = jnp.zeros((rows, D), f32)
        for j in range(0, FF, 512):
            gate = dot(x, up[:, j : j + 512]) + up_b[layer : layer + 1, j : j + 512]
            cdf = 0.5 * (1.0 + lax.erf(gate * math.sqrt(0.5)))
            pdf = jnp.exp(-0.5 * gate * gate) * (1.0 / math.sqrt(2.0 * math.pi))
            factor_ref[:, j : j + 512] = cdf + gate * pdf
            total += dot((gate * cdf).astype(bf16), down[j : j + 512])
        out_ref[...] = total + down_b[layer : layer + 1]

    return call(
        kernel,
        [
            hidden,
            params["mlp_gain"],
            params["mlp_shift"],
            (params["up_weight"], layer),
            params["up_bias"],
            (params["down_weight"], layer),
            params["down_bias"],
        ],
        [sds((rows, D), f32), sds((rows, FF), f32), sds((rows, D), bf16)],
        flops=2 * 2 * rows * D * FF,
    )


def mlp_both(hidden, grad, params, layer):
    rows = hidden.shape[0]

    def kernel(h_ref, g_ref, gain, shift, up, up_b, down, down_b, out_ref, back_ref):
        normal, _ = norm_parts(h_ref[...].astype(f32))
        x = (normal * gain[layer : layer + 1] + shift[layer : layer + 1]).astype(bf16)
        g_low = g_ref[...].astype(bf16)
        total = jnp.zeros((rows, D), f32)
        back = jnp.zeros((rows, D), f32)
        for j in range(0, FF, 512):
            gate = dot(x, up[:, j : j + 512]) + up_b[layer : layer + 1, j : j + 512]
            cdf = 0.5 * (1.0 + lax.erf(gate * math.sqrt(0.5)))
            pdf = jnp.exp(-0.5 * gate * gate) * (1.0 / math.sqrt(2.0 * math.pi))
            total += dot((gate * cdf).astype(bf16), down[j : j + 512])
            grad_gate = (dot_nt(g_low, down[j : j + 512]) * (cdf + gate * pdf)).astype(bf16)
            back += dot_nt(grad_gate, up[:, j : j + 512])
        out_ref[...] = total + down_b[layer : layer + 1]
        back_ref[...] = back

    return call(
        kernel,
        [
            hidden,
            grad,
            params["mlp_gain"],
            params["mlp_shift"],
            (params["up_weight"], layer),
            params["up_bias"],
            (params["down_weight"], layer),
            params["down_bias"],
        ],
        [sds((rows, D), f32), sds((rows, D), f32)],
    )


class Place:
    def __init__(self, n_dp, n_ctx, n_head, rows):
        self.n_ctx, self.n_head, self.rows = n_ctx, n_head, rows
        self.halves = n_dp == 2
        self.blocks = n_ctx * n_head
        self.group = self.blocks * rows
        self.units = FF // self.blocks
        self.packed_rows = 3 * D // self.blocks
        self.mixed_rows = D // self.blocks

    def position(self, scal, slot):
        shift, flip = slot // self.n_head, slot % self.n_head
        ctx = lax.rem(scal[0] - shift + self.n_ctx, self.n_ctx)
        return ctx * self.n_head + (scal[1] ^ flip)

    def ends(self, scal):
        return [scal[3 + k] for k in range(4)]


def delta_rows(grad_mixed_t, mixed_t):
    return jnp.concatenate(
        [
            jnp.sum(grad_mixed_t[n * HD : (n + 1) * HD].astype(f32) * mixed_t[n * HD : (n + 1) * HD], axis=0, keepdims=True)
            for n in range(NH)
        ],
        axis=0,
    )


def stat_payload(logs, deltas):
    parts = [*split_low(logs), *split_low(deltas)]
    top = jnp.concatenate(parts, axis=1)
    return jnp.concatenate([top, jnp.zeros_like(top)], axis=0)


def attention_forward(place, scalars, blocks, tables, params, layer, hidden, mlp_out, last_grad):
    rows, group = place.rows, place.group
    first_layer = layer == 0
    last = last_grad is not None
    tile = min(512, group)

    def kernel(scal, *refs):
        refs = list(refs)
        xs = [refs.pop(0) for _ in range(place.blocks)]
        cos_t, left_t, right_t, gain, shift, w, b, out_w, out_b, h_ref, mlp_ref = refs[:11]
        refs = refs[11:]
        g_ref, below_ref = (refs.pop(0), refs.pop(0)) if last else (None, None)
        (normal_out, k_out, v_out, q_own, kv_own, mixed_ref, mixed_low_ref, log_ref, delta_ref, dmix_ref, h_out, stats_ref, low_ref) = refs[:13]
        a_all = refs[13]
        normal_all, k_all, v_all = normal_out.ref, k_out.ref, v_out.ref
        own_at = pl.multiple_of(scal[2] * rows, rows)
        ends = place.ends(scal)
        gain_l, shift_l = gain[layer : layer + 1], shift[layer : layer + 1]
        for slot in range(place.blocks):
            at = pl.multiple_of(place.position(scal, slot) * rows, rows)
            x = xs[slot][...].astype(f32)
            normal = norm_parts(x)[0] if first_layer else x
            normal_all[pl.ds(at, rows)] = normal.astype(bf16)
            a_all[pl.ds(at, rows)] = (normal * gain_l + shift_l).astype(bf16)
        normal_out.send()
        w, cos_t, left_t, right_t = (x.get() for x in (w, cos_t, left_t, right_t))

        def project(i, _):
            at = pl.multiple_of(i * tile, tile)
            k = dot(a_all[pl.ds(at, tile)], w[:, D : 2 * D]) + b[layer : layer + 1, D : 2 * D]
            tabs = [t[pl.ds(at, tile)] for t in (cos_t, left_t, right_t)]
            for p in range(PAIRS):
                k_all[pl.ds(at, tile), 128 * p : 128 * p + 128] = rope(k[:, 128 * p : 128 * p + 128], *tabs).astype(bf16)
            v = dot(a_all[pl.ds(at, tile)], w[:, 2 * D :]) + b[layer : layer + 1, 2 * D :]
            v_all[pl.ds(at, tile)] = v.astype(bf16)
            return 0

        first_key = start_of(own_at, ends)
        low, high = first_key // STEP, (own_at + rows - 1) // STEP + 1
        lax.fori_loop(low * (STEP // tile), high * (STEP // tile), project, 0)
        k_out.send()
        v_out.send()
        kv_own[0:rows], kv_own[rows : 2 * rows] = k_all[pl.ds(own_at, rows)], v_all[pl.ds(own_at, rows)]
        q = dot(a_all[pl.ds(own_at, rows)], w[:, :D]) + b[layer : layer + 1, :D]
        tabs = [t[pl.ds(own_at, rows)] for t in (cos_t, left_t, right_t)]
        for p in range(PAIRS):
            turned = rope(q[:, 128 * p : 128 * p + 128], *tabs).astype(bf16)
            q_own[:, 128 * p : 128 * p + 128] = turned * jnp.asarray(score_scale, bf16)
        t = own_at + lax.broadcasted_iota(jnp.int32, (1, rows), 1)
        start = start_of(t, ends)
        doubled = [two_heads(q_own[:, 128 * p : 128 * p + 128]) for p in range(PAIRS)]

        def attend(i, carry):
            at = pl.multiple_of(i * STEP, STEP)
            s_at = at + lax.broadcasted_iota(jnp.int32, (STEP, 1), 0)
            bias = jnp.where((s_at >= start) & (s_at <= t), 0.0, masked_value)
            bias = jnp.concatenate([bias, bias], axis=1)
            new = []
            for p in range(PAIRS):
                most, total, acc = carry[p]
                scores = dot_nt(k_all[pl.ds(at, STEP), 128 * p : 128 * p + 128], doubled[p]) + bias
                newest = jnp.maximum(most, jnp.max(scores, axis=0, keepdims=True))
                chance = jnp.exp(scores - newest)
                scale = jnp.exp(most - newest)
                total = total * scale + jnp.sum(chance, axis=0, keepdims=True)
                acc = acc * scale + dot_tn(v_all[pl.ds(at, STEP), 128 * p : 128 * p + 128], chance.astype(bf16))
                new.append((newest, total, acc))
            return tuple(new)

        begin = tuple(
            (jnp.full((1, 2 * rows), masked_value, f32), jnp.zeros((1, 2 * rows), f32), jnp.zeros((128, 2 * rows), f32))
            for _ in range(PAIRS)
        )
        done = lax.fori_loop(low, high, attend, begin)
        logs = []
        for p in range(PAIRS):
            most, total, acc = done[p]
            mixed_ref[128 * p : 128 * p + 128] = one_pair_t(acc / total)
            log = most + jnp.log(total)
            logs += [log[:, :rows], log[:, rows:]]
        log_rows = jnp.concatenate(logs, axis=0)
        log_ref[...] = log_rows
        mixed_low = mixed_ref[...].astype(bf16)
        if last:
            size = place.mixed_rows
            for p in range(place.n_head):
                for c in range(place.n_ctx):
                    at = 128 * p + size * c
                    mixed_low_ref[c * place.n_head + p, 0:size] = below_ref[at : at + size]
                    mixed_low_ref[c * place.n_head + p, size : 2 * size] = mixed_low[at : at + size]
        else:
            mixed_low_ref[...] = mixed_low
        out_w = out_w.get()
        attn_out = dot_tn(mixed_low, out_w[...]) + out_b[layer : layer + 1]
        h = h_ref.get()[...].astype(f32)
        mlp = mlp_ref.get()[...]
        result = h + attn_out + mlp
        lane = lane_of(8)
        sums = [jnp.sum(jnp.sum(v * v, axis=1, keepdims=True), axis=0, keepdims=True) for v in (h, attn_out, mlp)]
        stats_ref[...] = jnp.where(lane == 0, sums[0], jnp.where(lane == 1, sums[1], jnp.where(lane == 2, sums[2], 0.0)))
        if last:
            h_out[...] = result.astype(bf16)
            dmix = dot_nt(out_w[...], g_ref[...]).astype(bf16)
            dmix_ref[...] = dmix
            deltas = delta_rows(dmix, mixed_ref[...])
            delta_ref[...] = deltas
            low_ref[...] = stat_payload(log_rows, deltas)
        else:
            h_out[...] = result
            low_ref[...] = norm_parts(result)[0].astype(bf16)
            dmix_ref[...] = jnp.zeros_like(dmix_ref)
            delta_ref[...] = jnp.zeros_like(delta_ref)

    ins = [
        *blocks,
        *[Lazy(x) for x in tables],
        params["attn_gain"],
        params["attn_shift"],
        lazy_layer(params["qkv_sorted"], layer),
        params["qkv_bias_sorted"],
        lazy_layer(params["out_weight"], layer),
        params["out_bias"],
        Lazy(hidden),
        Lazy(mlp_out),
    ]
    if last:
        ins += last_grad
    outs = [
        Out((group, D), bf16),
        Out((group, D), bf16),
        Out((group, D), bf16),
        sds((rows, D), bf16),
        sds((2 * rows, D), bf16),
        sds((D, rows), f32),
        sds((place.blocks, 2 * place.mixed_rows, rows) if last else (D, rows), bf16),
        sds((NH, rows), f32),
        sds((NH, rows), f32),
        sds((D, rows), bf16),
        sds((rows, D), bf16 if last else f32),
        sds((8, 128), f32),
        sds((16, D) if last else (rows, D), bf16),
    ]
    return call(kernel, ins, outs, [VMEM((group, D), bf16)], scalars, flops=60 * 10**9)


def mlp_backward(grad, factor, hidden, params, layer):
    rows = grad.shape[0]

    def kernel(g_ref, factor_ref, down, up, out_ref):
        g_low = g_ref[...].astype(bf16)
        total = jnp.zeros((rows, D), f32)
        for j in range(0, FF, 512):
            grad_gate = (dot_nt(g_low, down[j : j + 512]) * factor_ref[:, j : j + 512]).astype(bf16)
            total += dot_nt(grad_gate, up[:, j : j + 512])
        out_ref[...] = total

    return call(
        kernel,
        [grad, factor, (params["down_weight"], layer), (params["up_weight"], layer)],
        [sds((rows, D), f32)],
        flops=2 * 2 * rows * D * FF,
    )[0]


def query_backward(place, scalars, tables, own_tables, params, layer, kept):
    rows, group = place.rows, place.group
    tile = min(512, group)

    def kernel(scal, cos_t, left_t, right_t, own_tabs, gain, shift, w, b, normal_all, k_all, v_all, q_own, dmix_ref, log_ref, delta_ref, q_out, grad_ref, grad_t_ref):
        q_all = q_out.ref
        own_at = pl.multiple_of(scal[2] * rows, rows)
        ends = place.ends(scal)
        gain_l, shift_l = gain[layer : layer + 1], shift[layer : layer + 1]

        def project(i, _):
            at = pl.multiple_of(i * tile, tile)
            a = (normal_all[pl.ds(at, tile)].astype(f32) * gain_l + shift_l).astype(bf16)
            q = dot(a, w[...]) + b[layer : layer + 1, :D]
            tabs = [t[pl.ds(at, tile)] for t in (cos_t, left_t, right_t)]
            for p in range(PAIRS):
                turned = rope(q[:, 128 * p : 128 * p + 128], *tabs).astype(bf16)
                q_all[pl.ds(at, tile), 128 * p : 128 * p + 128] = turned * jnp.asarray(score_scale, bf16)
            return 0

        last_end = end_of(own_at + rows - 1, ends, group)
        low, high = own_at // STEP, (last_end + STEP - 1) // STEP
        lax.fori_loop(low * (STEP // tile), high * (STEP // tile), project, 0)
        q_out.send()
        k_all, v_all = k_all.get(), v_all.get()
        t = own_at + lax.broadcasted_iota(jnp.int32, (1, rows), 1)
        start = start_of(t, ends)
        q2 = [two_heads(q_own[:, 128 * p : 128 * p + 128]) for p in range(PAIRS)]
        d2 = [two_heads_t(dmix_ref[128 * p : 128 * p + 128]) for p in range(PAIRS)]
        log2 = [jnp.concatenate([log_ref[2 * p : 2 * p + 1], log_ref[2 * p + 1 : 2 * p + 2]], axis=1) for p in range(PAIRS)]
        delta2 = [
            jnp.concatenate([delta_ref[2 * p : 2 * p + 1], delta_ref[2 * p + 1 : 2 * p + 2]], axis=1) for p in range(PAIRS)
        ]

        def queries(i, carry):
            at = pl.multiple_of(i * STEP, STEP)
            s = at + lax.broadcasted_iota(jnp.int32, (STEP, 1), 0)
            bias = jnp.where((s >= start) & (s <= t), 0.0, masked_value)
            bias = jnp.concatenate([bias, bias], axis=1)
            new = []
            for p in range(PAIRS):
                ks = k_all[pl.ds(at, STEP), 128 * p : 128 * p + 128]
                vs = v_all[pl.ds(at, STEP), 128 * p : 128 * p + 128]
                chance = jnp.exp(dot_nt(ks, q2[p]) + bias - log2[p])
                grad_s = (chance * (dot(vs, d2[p]) - delta2[p])).astype(bf16)
                new.append(carry[p] + dot_tn(ks, grad_s))
            return tuple(new)

        zero = jnp.zeros((128, 2 * rows), f32)
        done = lax.fori_loop(
            start_of(own_at, ends) // STEP, (own_at + rows - 1) // STEP + 1, queries, tuple(zero for _ in range(PAIRS))
        )
        tabs = [own_tabs[0:rows].T, -own_tabs[rows : 2 * rows].T, -own_tabs[2 * rows : 3 * rows].T]
        for p in range(PAIRS):
            grad_t = rope_t(one_pair_t(done[p]) * score_scale, *tabs)
            grad_t_ref[128 * p : 128 * p + 128] = grad_t.astype(bf16)
            grad_ref[:, 128 * p : 128 * p + 128] = grad_t.T.astype(bf16)

    return call(
        kernel,
        [
            *tables,
            own_tables,
            params["attn_gain"],
            params["attn_shift"],
            (params["qkv_sorted"], layer, D),
            params["qkv_bias_sorted"],
            kept["normal_all"],
            Lazy(kept["k_all"]),
            Lazy(kept["v_all"]),
            kept["q_own"],
            kept["dmix"],
            kept["log"],
            kept["delta"],
        ],
        [Out((group, D), bf16), sds((rows, D), bf16), sds((D, rows), bf16)],
        (),
        scalars,
        flops=30 * 10**9,
    )


def key_backward(place, scalars, g_whole, stats, own_tables, params, layer, kept, queries, grad, grad_mlp_in, mixed_below):
    rows, group = place.rows, place.group
    below = layer > 0
    n_stats = len(stats)
    tile = min(512, group)
    part = place.packed_rows

    def kernel(scal, *refs):
        refs = list(refs)
        ss = [refs.pop(0) for _ in range(n_stats)]
        (g_all, own_tabs, gain, mlp_gain, w, out_w, q_all, gq_ref, gq_t_ref, kv_own, h_ref, g_ref, gmlp_ref, stats_ref) = refs[:14]
        refs = refs[14:]
        if below:
            below_mixed, below_log, below_w, carried = refs[:4]
            refs = refs[4:]
        pieces_out, g_out, payload_ref, dmix_out, delta_out = refs[:5]
        dm_all, log_all, delta_all, packed_t = refs[5:]
        own_at = pl.multiple_of(scal[2] * rows, rows)
        ends = place.ends(scal)
        gain_l = gain[layer : layer + 1]
        for slot in range(place.blocks):
            at = pl.multiple_of(place.position(scal, slot) * rows, rows)
            if below:
                flip = slot % place.n_head
                info = ss[slot // place.n_head][16 * flip : 16 * flip + 16].astype(f32)[:NH]
            else:
                info = ss[slot][rows : rows + 16].astype(f32)[:NH]
            log_all[:, pl.ds(at, rows)] = info[:, 0:128] + info[:, 128:256]
            delta_all[:, pl.ds(at, rows)] = info[:, 256:384] + info[:, 384:512]
        last_end = end_of(own_at + rows - 1, ends, group)

        def project(i, _):
            at = pl.multiple_of(i * tile, tile)
            dm_all[pl.ds(at, tile)] = dot_nt(g_all[pl.ds(at, tile)], out_w[...]).astype(bf16)
            return 0

        low, high = own_at // STEP, (last_end + STEP - 1) // STEP
        lax.fori_loop(low * (STEP // tile), high * (STEP // tile), project, 0)
        q_all = q_all.get()
        s_at = own_at + lax.broadcasted_iota(jnp.int32, (rows, 1), 0)
        k2 = [two_heads(kv_own[0:rows, 128 * p : 128 * p + 128]) for p in range(PAIRS)]
        v2 = [two_heads(kv_own[rows : 2 * rows, 128 * p : 128 * p + 128]) for p in range(PAIRS)]

        def keys(i, carry):
            at = pl.multiple_of(i * STEP, STEP)
            t = at + lax.broadcasted_iota(jnp.int32, (1, STEP), 1)
            start = start_of(t, ends)
            bias = jnp.where((s_at >= start) & (s_at <= t), 0.0, masked_value)
            new = []
            for p in range(PAIRS):
                dk, dv = carry[p]
                qs = q_all[pl.ds(at, STEP), 128 * p : 128 * p + 128]
                dms = dm_all[pl.ds(at, STEP), 128 * p : 128 * p + 128]
                scores = dot_nt(k2[p], qs)
                pulled = dot_nt(v2[p], dms)
                chances, grads = [], []
                for half in range(2):
                    n = 2 * p + half
                    part = slice(half * rows, half * rows + rows)
                    chance = jnp.exp(scores[part] + bias - log_all[n : n + 1, pl.ds(at, STEP)])
                    grads.append(chance * (pulled[part] - delta_all[n : n + 1, pl.ds(at, STEP)]))
                    chances.append(chance)
                chance = jnp.concatenate(chances, axis=0).astype(bf16)
                grad_s = jnp.concatenate(grads, axis=0).astype(bf16)
                new.append((dk + dot(grad_s, qs), dv + dot(chance, dms)))
            return tuple(new)

        zero = jnp.zeros((2 * rows, 128), f32)
        done = lax.fori_loop(low, high, keys, tuple((zero, zero) for _ in range(PAIRS)))
        tabs = [own_tabs[0:rows], -own_tabs[rows : 2 * rows], -own_tabs[2 * rows : 3 * rows]]
        grad_k = [rope(one_pair(done[p][0]), *tabs).astype(bf16) for p in range(PAIRS)]
        grad_v = [one_pair(done[p][1]).astype(bf16) for p in range(PAIRS)]
        w = w.get()
        grad_in = dot_nt(gq_ref.get()[...], w[:, 0:D])
        for j, parts in ((1, grad_k), (2, grad_v)):
            grad_in += dot_nt(jnp.concatenate(parts, axis=1), w[:, j * D : j * D + D])

        normal, inverse = norm_parts(h_ref.get()[...].astype(f32))
        grad_mlp = gmlp_ref.get()[...]
        grad_normal = grad_in * gain_l + grad_mlp * mlp_gain[layer : layer + 1]
        back = inverse * (
            grad_normal
            - jnp.mean(grad_normal, axis=-1, keepdims=True)
            - normal * jnp.mean(grad_normal * normal, axis=-1, keepdims=True)
        )
        g_new = g_ref.get()[...].astype(f32) + back
        g_out[...] = g_new

        sums = [
            jnp.sum(v, axis=0, keepdims=True)
            for v in (grad_in * normal, grad_in, grad_mlp * normal, grad_mlp)
        ]
        for j in range(3):
            for p in range(PAIRS):
                if j == 0:
                    turned = gq_t_ref.get()[128 * p : 128 * p + 128]
                else:
                    turned = (grad_k, grad_v)[j - 1][p].astype(f32).T.astype(bf16)
                for half in range(2):
                    at = (2 * p + half) * 3 * HD + j * HD
                    packed_t[at : at + HD] = turned[half * HD : half * HD + HD]
        layer_sums = jnp.where(lane_of(8) < 4, stats_ref[...], 0.0)
        layer_sums = jnp.broadcast_to(pltpu.roll(layer_sums, scal[2] * 4, 1)[0:1], (16, 128))
        row16 = lax.broadcasted_iota(jnp.int32, (16, 128), 0)
        for p in range(place.n_head):
            extra = jnp.concatenate([x[:, 128 * p : 128 * p + 128] for x in sums] + [jnp.zeros((4, 128), f32)], axis=0)
            extra = jnp.concatenate([extra, extra], axis=0)
            extra = jnp.where((row16 & 7) == 4, layer_sums, extra)
            high, rest = split_low(extra)
            extra = jnp.where(row16 < 8, high, rest)
            for c in range(place.n_ctx):
                at = (p * place.n_ctx + c) * part
                pieces_out[c * place.n_head + p, 0:part] = packed_t[at : at + part]
                pieces_out[c * place.n_head + p, part : part + 16] = extra
        if below:
            pieces_out[:, part + 16 :] = carried[...]

        g_low = g_new.astype(bf16)
        if below:
            payload_ref[0:rows] = g_low
            dmix = dot_nt(below_w.get()[...], g_low).astype(bf16)
            dmix_out[...] = dmix
            deltas = delta_rows(dmix, below_mixed.get()[...])
            delta_out[...] = deltas
            payload_ref[rows : rows + 16] = stat_payload(below_log[...], deltas)
        else:
            payload_ref[...] = jnp.zeros_like(payload_ref)
            dmix_out[...] = jnp.zeros_like(dmix_out)
            delta_out[...] = jnp.zeros_like(delta_out)

    ins = [
        *stats,
        g_whole,
        own_tables,
        params["attn_gain"],
        params["mlp_gain"],
        lazy_layer(params["qkv_sorted"], layer),
        (params["out_weight"], layer),
        *[Lazy(x) for x in queries],
        kept["kv_own"],
        Lazy(kept["hidden"]),
        Lazy(grad),
        Lazy(grad_mlp_in),
        kept["stats"],
    ]
    if below:
        ins += [Lazy(mixed_below["mixed"]), mixed_below["log"], lazy_layer(params["out_weight"], layer - 1)]
        ins.append(kept["mixed_low"])
    outs = [
        sds((place.blocks, part + 16 + (2 * place.mixed_rows if below else 0), rows), bf16),
        sds((rows, D), f32),
        sds((rows + 16, D) if below else (16, D), bf16),
        sds((D, rows) if below else (16, rows), bf16),
        sds((NH, rows), f32),
    ]
    scratch = [VMEM((group, D), bf16), VMEM((NH, group), f32), VMEM((NH, group), f32), VMEM((3 * D, rows), bf16)]
    return call(kernel, ins, outs, scratch, scalars, flops=60 * 10**9)


def mlp_weight_grads(place, scalars, blocks, normal_all, params, layer, mixed=None):
    group, rows, units = place.group, place.rows, place.units
    tile = min(512, group)
    size = 0 if mixed is None else place.mixed_rows

    def kernel(scal, *refs):
        gs = refs[: place.blocks]
        refs = list(refs[place.blocks :])
        mixed_ref, other_ref = (refs.pop(0), refs.pop(0)) if size else (None, None)
        normal_ref, gain, shift, up, up_b, down, g_out, up_out, down_out = refs[:9]
        g_ref = g_out.ref
        mixed_t = refs[9] if size else None
        gain_l, shift_l = gain[layer : layer + 1], shift[layer : layer + 1]
        for slot in range(place.blocks):
            at = pl.multiple_of(place.position(scal, slot) * rows, rows)
            g_ref[pl.ds(at, rows)] = gs[slot][0:rows]
            if size:
                mixed_t[:, slot * rows : (slot + 1) * rows] = mixed_ref[slot, place.packed_rows + 16 :]

        g_out.send()

        def step(i, carry):
            up_t, down_g, bias, g_sum = carry
            at = pl.multiple_of(i * tile, tile)
            x = (normal_ref[pl.ds(at, tile)].astype(f32) * gain_l + shift_l).astype(bf16)
            g = g_ref[pl.ds(at, tile)]
            gate = dot(x, up[...]) + up_b[...]
            cdf = 0.5 * (1.0 + lax.erf(gate * math.sqrt(0.5)))
            pdf = jnp.exp(-0.5 * gate * gate) * (1.0 / math.sqrt(2.0 * math.pi))
            acted = (gate * cdf).astype(bf16)
            grad_gate = (dot_nt(g, down[...]) * (cdf + gate * pdf)).astype(bf16)
            up_t += dot(grad_gate.T, x)
            down_g += dot(acted.T, g)
            bias += jnp.sum(grad_gate.astype(f32), axis=0, keepdims=True)
            g_sum += jnp.sum(g.astype(f32), axis=0, keepdims=True)
            return up_t, down_g, bias, g_sum

        zero = jnp.zeros((units, D), f32)
        up_t, down_g, bias, g_sum = lax.fori_loop(
            0, group // tile, step, (zero, zero, jnp.zeros((1, units), f32), jnp.zeros((1, D), f32))
        )
        up_out[0:units] = up_t.astype(bf16)
        if units < 128:
            bias = jnp.concatenate([bias, jnp.zeros((1, 128 - units), f32)], axis=1)
        wide = jnp.concatenate([bias, jnp.zeros((1, D - 128), f32)], axis=1)
        row = lax.broadcasted_iota(jnp.int32, (32, D), 0)
        extra = jnp.where((row & 7) == 0, wide, jnp.where((row & 7) == 1, g_sum, 0.0))
        high, rest = split_low(extra)
        up_out[units : units + 32] = jnp.where(row < 8, high, jnp.where(row < 16, rest, jnp.zeros_like(rest)))
        if size:
            out_g = [dot(mixed_t[k * size : (k + 1) * size], g[...]) for k, g in enumerate((g_ref, other_ref))]
        for p in range(place.n_head):
            cols = slice(128 * p, 128 * p + 128)
            down_out[p, 0:units] = down_g[:, cols].astype(bf16)
            for k in range(2 if size else 0):
                down_out[p, units + k * size : units + (k + 1) * size] = out_g[k][:, cols].astype(bf16)

    up, up_b, down = params["units"][layer]
    made = call(
        kernel,
        [*blocks, *([] if mixed is None else mixed), normal_all, params["mlp_gain"], params["mlp_shift"], up, up_b, down],
        [Out((group, D), bf16), sds((units + 32, D), bf16), sds((place.n_head, units + 2 * size, 128), bf16)],
        [VMEM((2 * size, group), bf16)] if size else [],
        scalars,
        flops=4 * 2 * group * D * units,
    )
    return made


def attention_weight_grads(place, scalars, received, normal_all, params, layer):
    group, rows, part = place.group, place.rows, place.packed_rows
    tile = min(512, group)

    def kernel(received_ref, normal_ref, gain, shift, out_ref, chunk_t):
        gain_l, shift_l = gain[layer : layer + 1], shift[layer : layer + 1]
        extra = jnp.zeros((16, 128), f32)
        for j in range(place.blocks):
            chunk_t[:, j * rows : (j + 1) * rows] = received_ref[j, 0:part]
            extra += received_ref[j, part : part + 16].astype(f32)
        total = jnp.zeros((part, D), f32)
        for at in range(0, group, tile):
            x = (normal_ref[at : at + tile].astype(f32) * gain_l + shift_l).astype(bf16)
            total += dot(chunk_t[:, at : at + tile], x)
        out_ref[0:part] = total.astype(bf16)
        bias = dot_nt(jnp.ones((16, group), bf16), chunk_t[...])
        bias = jnp.concatenate([bias, jnp.zeros((16, 128 - part), f32)], axis=1)
        extra = extra[0:8] + extra[8:16]
        wide = jnp.concatenate([extra[k : k + 1] for k in range(4)], axis=1)
        none = jnp.zeros((1, D - 256), f32)
        second = jnp.concatenate([bias[0:1], extra[4:5], none], axis=1)
        row = lax.broadcasted_iota(jnp.int32, (16, D), 0)
        high, rest = split_low(jnp.where((row & 7) == 0, wide, jnp.where((row & 7) == 1, second, 0.0)))
        out_ref[part : part + 16] = jnp.where(row < 8, high, rest)

    return call(
        kernel,
        [received, normal_all, params["attn_gain"], params["attn_shift"]],
        [sds((part + 16, D), bf16)],
        [VMEM((part, group), bf16)],
        flops=2 * group * D * part,
    )[0]


def pack_mlp(place, scalars, up_share, pieces, halves):
    rows = place.units + 32 + pieces.shape[1]
    half = rows // 2

    def kernel(scal, up_ref, pieces_ref, *refs):
        if halves:
            mine, other, full = refs
        else:
            (full,) = refs
        full[0 : place.units + 32] = up_ref[...]
        for p in range(place.n_head):
            full[place.units + 32 :, 128 * p : 128 * p + 128] = pieces_ref[p]
        if halves:
            at = pl.multiple_of(scal[7] * half, half)
            mine[...] = full[pl.ds(at, half)]
            other[...] = full[pl.ds(pl.multiple_of(half - at, half), half)]

    outs = [sds((half, D), bf16)] * 2 if halves else [sds((rows, D), bf16)]
    scratch = [VMEM((rows, D), bf16)] if halves else []
    return call(kernel, [up_share, pieces], outs, scratch, scalars, flops=10**7)


def along_lanes(rows, width):
    if width == 128:
        return jnp.concatenate(rows, axis=1)
    full = len(rows) * width
    out = jnp.zeros((8, full), f32)
    for k, row in enumerate(rows):
        lane = lax.broadcasted_iota(jnp.int32, (8, full), 1)
        row = jnp.concatenate([row, jnp.zeros((1, full - 128), f32)], axis=1)
        row = jnp.where(lane < width, jnp.broadcast_to(row, (8, full)), 0.0)
        out += pltpu.roll(row, k * width, 1) if k else row
    return out[0:1]


def whole_shares(place, scal, refs, at, size, full, halves):
    if not halves:
        return [x.at[at : at + size] for x in refs]
    half = size // 2
    for s in range(place.n_ctx):
        full[s, pl.ds(pl.multiple_of(scal[7] * half, half), half)] = refs[s][at : at + half]
        start = s * half
        full[s, pl.ds(pl.multiple_of((1 - scal[7]) * half, half), half)] = refs[-1][start : start + half]
    return [full.at[s] for s in range(place.n_ctx)]


def place_mlp(place, scalars, shares, layer, into):
    n_ctx, units = place.n_ctx, place.units
    taken = 0 if into is None else 2
    halves = len(shares) > n_ctx
    size = place.mixed_rows if layer == 0 else 0
    rows = 2 * units + 32 + 2 * size

    def kernel(scal, *refs):
        up_out, down_out, small_out, *out_outs, up_t, bias_rows, full = refs[len(shares) + taken :]
        ordered = len(shares) == 1
        if ordered:
            srcs = [refs[0].at[c * rows : (c + 1) * rows] for c in range(n_ctx)]
        else:
            srcs = whole_shares(place, scal, refs[: len(shares)], 0, rows, full, halves)
        for s in range(n_ctx):
            c = s if ordered else lax.rem(scal[0] - s + n_ctx, n_ctx)
            at = pl.multiple_of(c * units, units)
            up_t[pl.ds(at, units)] = srcs[s][0:units].astype(f32)
            extra = srcs[s][units : units + 16].astype(f32)
            extra = extra[0:8] + extra[8:16]
            bias_rows[c] = jnp.broadcast_to(extra[0:1, :128], (8, 128))
            if s == 0:
                small_out[...] = jnp.zeros_like(small_out)
                for q in range(place.n_head):

                    @pl.when(scal[1] == q)
                    def _():
                        small_out[1:2, 0:128] = extra[1:2, 128 * q : 128 * q + 128]

            for p in range(place.n_head):
                at = pl.multiple_of(p * (FF // place.n_head) + c * units, units)
                base = units + 32
                down_out[pl.ds(at, units)] = srcs[s][base : base + units, 128 * p : 128 * p + 128].astype(f32)
                at = pl.multiple_of(p * 128 + c * place.mixed_rows, place.mixed_rows)
                for k in range(2 if size else 0):
                    start = base + units + k * size
                    out_outs[0][k, pl.ds(at, size)] = srcs[s][start : start + size, 128 * p : 128 * p + 128].astype(f32)
        up_out[...] = up_t[...].T
        small_out[0:1] = along_lanes([bias_rows[c][0:1] for c in range(n_ctx)], units)

    wide = FF // place.n_head
    return call(
        kernel,
        shares,
        [
            (sds((LAYERS, D, wide), f32), layer),
            (sds((LAYERS, FF, 128), f32), layer),
            sds((8, wide), f32),
            *([sds((LAYERS, D, 128), f32)] if size else []),
        ],
        [VMEM((wide, D), f32), VMEM((n_ctx, 8, 128), f32), VMEM((n_ctx, rows, D) if halves else (1, 16, D), bf16)],
        scalars,
        flops=10**7,
        into=into,
    )


def place_attention(place, scalars, shares, layer, into, smalls=None, count=1):
    n_ctx, part = place.n_ctx, place.packed_rows
    taken = 0 if into is None else 1
    wide = 3 * D // place.n_head
    wide_up = FF // place.n_head
    given = [] if smalls is None else smalls

    def kernel(scal, *refs):
        shares_in, given_in = refs[: len(shares)], refs[len(shares) : len(shares) + len(given)]
        qkv_out, *small_outs, qkv_t, info, small = refs[len(shares) + len(given) + taken :]
        small[...] = jnp.zeros_like(small)
        for s in range(n_ctx):
            c = lax.rem(scal[0] - s + n_ctx, n_ctx)
            at = pl.multiple_of(c * part, part)
            qkv_t[pl.ds(at, part)] = shares_in[s][0:part].astype(f32)
            extra = shares_in[s][part : part + 16].astype(f32)
            extra = extra[0:8] + extra[8:16]
            info[c] = extra
            if s == 0:
                for k in range(4):
                    small[k : k + 1, 0:128] = extra[0:1, 128 * k : 128 * k + 128]
                small[4:5, 0:128] = extra[1:2, 128:256]
        qkv_out[...] = qkv_t[...].T
        small[5:6] = along_lanes([info[c, 1:2, 0:128] for c in range(n_ctx)], part)
        if smalls is None:
            small_outs[0][...] = small[...]
            return
        attn_1, mlp_0, mlp_1 = given_in
        lane = lane_of(1)
        for spot, attn, mlp in ((0, small, mlp_0), (1, attn_1, mlp_1)):
            row = slice(spot, spot + 1)
            for k in range(4):
                small_outs[k][row] = attn[k : k + 1, 0:128]
            small_outs[4][row] = attn[5:6]
            small_outs[5][row] = mlp[0:1]
            small_outs[6][row] = mlp[1:2, 0:128]
            small_outs[7][row] = mlp[1:2, 0:128]
            for k in range(3):
                picked = jnp.where((lane & 3) == k, attn[4:5, 0:128], 0.0)
                small_outs[8][row, k : k + 1] = jnp.sqrt(jnp.sum(picked, axis=1, keepdims=True) * (1.0 / count))

    if smalls is None:
        outs = [sds((8, wide), f32)]
    else:
        widths = [128, 128, 128, 128, wide, wide_up, 128, 128, 3]
        outs = [sds((LAYERS, width), f32) for width in widths]
    return call(
        kernel,
        [*shares, *given],
        [(sds((LAYERS, D, wide), f32), layer), *outs],
        [
            VMEM((wide, D), f32),
            VMEM((n_ctx, 8, D), f32),
            VMEM((8, wide), f32),
        ],
        scalars,
        flops=10**7,
        into=into,
    )


def prepare(place, lengths, qkv_weight, qkv_bias):
    group = place.group
    blocks = group // 128
    dim = jnp.arange(128, dtype=jnp.int32)[None, :] % HD
    freq = rope_base ** (-2.0 * (dim % (ROT // 2)).astype(f32) / ROT)
    starts = jnp.concatenate([jnp.zeros((1,), jnp.int32), lengths[0, :3]])
    starts = jnp.stack([starts[0], starts[1], starts[1] + starts[2], starts[1] + starts[2] + starts[3]])
    first = (jnp.arange(blocks, dtype=jnp.int32)[:, None] * 128 - starts[None, :]).reshape(-1, 1)
    whole = jnp.concatenate([first, jnp.arange(128, dtype=jnp.int32)[:, None]], axis=0).astype(f32) * freq
    cosines, sines = jnp.cos(whole), jnp.sin(whole)
    base = 4 * blocks

    def kernel(scal, w_ref, b_ref, cos_ref, sin_ref, w_out, b_out, cos_t, left_t, right_t, own_t):
        def sort(read, write):
            for p in range(PAIRS):
                a, b, c = (read(slice(128 * (3 * p + i), 128 * (3 * p + i) + 128)).astype(f32) for i in range(3))
                first = lane_of(a.shape[0]) < HD
                made = (jnp.where(first, a, b), pltpu.roll(jnp.where(first, c, a), HD, 1), jnp.where(first, b, c))
                for j in range(3):
                    write(slice(j * D + 128 * p, j * D + 128 * p + 128), made[j])

        for layer in range(LAYERS):

            def store(to, x, layer=layer):
                w_out[layer, :, to] = x.astype(bf16)

            sort(lambda at, layer=layer: w_ref[layer, :, at], store)

        def store_bias(to, x):
            b_out[:, to] = x

        sort(lambda at: b_ref[:, at], store_bias)
        ends = place.ends(scal)
        dim = lane_of(128) & (HD - 1)
        cos_b, sin_b = cos_ref[base : base + 128], sin_ref[base : base + 128]

        def table(i, _):
            at = pl.multiple_of(i * 128, 128)
            t = at + lax.broadcasted_iota(jnp.int32, (128, 1), 0)
            cos_a, sin_a = cos_ref[pl.ds(4 * i, 1)], sin_ref[pl.ds(4 * i, 1)]
            for k in range(1, 4):
                later = t >= ends[k - 1]
                cos_a = jnp.where(later, cos_ref[pl.ds(4 * i + k, 1)], cos_a)
                sin_a = jnp.where(later, sin_ref[pl.ds(4 * i + k, 1)], sin_a)
            cosine = cos_a * cos_b - sin_a * sin_b
            sine = sin_a * cos_b + cos_a * sin_b
            cos_t[pl.ds(at, 128)] = jnp.where(dim < ROT, cosine, 1.0)
            left_t[pl.ds(at, 128)] = jnp.where(dim < ROT // 2, -sine, 0.0)
            right_t[pl.ds(at, 128)] = jnp.where((dim >= ROT // 2) & (dim < ROT), sine, 0.0)
            return 0

        lax.fori_loop(0, blocks, table, 0)
        own_at = pl.multiple_of(scal[2] * place.rows, place.rows)
        for k, ref in enumerate((cos_t, left_t, right_t)):
            own_t[k * place.rows : (k + 1) * place.rows] = ref[pl.ds(own_at, place.rows)]

    bias = jnp.concatenate([qkv_bias, jnp.zeros((8 - LAYERS, 3 * D), f32)], axis=0)
    made = call(
        kernel,
        [qkv_weight, bias, cosines, sines],
        [sds(qkv_weight.shape, bf16), sds((8, 3 * D), f32), *[sds((group, 128), f32)] * 3, sds((3 * place.rows, 128), f32)],
        (),
        lengths,
        flops=10**7,
    )
    return made[0], made[1], made[2:5], made[5]


def tie(x, *after):
    return lax.optimization_barrier((x, *after))[0] if after else x


def flip_heads(x, flip):
    return lax.ppermute(x, "head", [(i, i ^ flip) for i in range(lax.axis_size("head"))])


def turn_ctx(x, shift):
    n = lax.axis_size("ctx")
    return lax.ppermute(x, "ctx", [(i, (i + shift) % n) for i in range(n)])


def gather_rings(own):
    return [own] + [turn_ctx(own, s) for s in range(1, lax.axis_size("ctx"))]


def gather_flips(rings, flip, *after):
    return [flip_heads(tie(x, *after), flip) for x in rings]


def by_slot(rings, far, near, far_near):
    return [x for four in zip(rings, near, far, far_near) for x in four]


def with_flip(own, flip):
    return jnp.concatenate([own, flip_heads(own, flip)], axis=0)


def swap_dp(x):
    return lax.ppermute(x, "dp", [(0, 1), (1, 0)])


def per_device(
    hidden_in,
    lengths,
    attn_gain,
    attn_shift,
    mlp_gain,
    mlp_shift,
    qkv_weight,
    qkv_bias,
    out_weight,
    out_bias,
    up_weight,
    up_bias,
    down_weight,
    down_bias,
    cotangent,
):
    rows = hidden_in.shape[0]
    n_dp, n_ctx, n_head = (lax.axis_size(a) for a in ("dp", "ctx", "head"))
    place = Place(n_dp, n_ctx, n_head, rows)
    group = place.group
    scalars = lengths
    qkv_sorted, qkv_bias_sorted, tables, own_tables = prepare(place, lengths, qkv_weight, qkv_bias)
    params = {
        "attn_gain": attn_gain,
        "attn_shift": attn_shift,
        "mlp_gain": mlp_gain,
        "mlp_shift": mlp_shift,
        "qkv_sorted": qkv_sorted,
        "qkv_bias_sorted": qkv_bias_sorted,
        "out_weight": out_weight,
        "out_bias": out_bias,
        "up_weight": up_weight,
        "up_bias": up_bias,
        "down_weight": down_weight,
        "down_bias": down_bias,
    }
    def attention(layer, blocks, hidden, mlp_out, last_grad):
        names = ("normal_all", "k_all", "v_all", "q_own", "kv_own", "mixed", "mixed_low", "log", "delta", "dmix", "h_out", "stats", "low")
        made = attention_forward(place, scalars, blocks, tables, params, layer, hidden, mlp_out, last_grad)
        return dict(zip(names, made), hidden=hidden)

    def backward_queries(layer, kept):
        return query_backward(place, scalars, tables, own_tables, params, layer, kept)

    def backward_keys(layer, g_all, stats, kept, queries, grad, grad_mlp_in, below):
        return key_backward(
            place, scalars, g_all, stats, own_tables, params, layer, kept, queries, grad, grad_mlp_in, below
        )

    def head_swap(pieces):
        return lax.all_to_all(pieces, "head", 0, 0, tiled=True)

    def group_swap(pieces):
        return lax.all_to_all(pieces, ("ctx", "head"), 0, 0, tiled=True)

    def reduce_mlp(up_share, pieces, halves):
        made = pack_mlp(place, scalars, up_share, pieces, halves)
        if n_dp == 2:
            return (made[0].astype(f32) + swap_dp(made[-1]).astype(f32)).astype(bf16)
        return lax.psum(made[0], "dp")

    def sum_dp(x):
        if n_dp == 2:
            return (x.astype(f32) + swap_dp(x).astype(f32)).astype(bf16)
        return lax.psum(x, "dp")

    def finish(rings):
        return [*rings, swap_dp(jnp.concatenate(rings, axis=0))] if n_dp == 2 else rings

    together = lax.optimization_barrier

    mlp_0, factor_0, _ = mlp_forward(hidden_in, params, 0)
    rings, mlp_0, factor_0 = together((gather_rings(hidden_in), mlp_0, factor_0))
    far = gather_flips(rings, 2)
    far, rings, params["qkv_sorted"], tables, own_tables = together((far, rings, qkv_sorted, tables, own_tables))
    near, far_near = together((gather_flips(rings, 1), gather_flips(far, 1)))
    first, cot_rings = together(
        (attention(0, by_slot(rings, far, near, far_near), hidden_in, mlp_0, None), gather_rings(tie(cotangent, near)))
    )
    hidden, low = first["h_out"], first["low"]
    units = place.units
    at = lax.axis_index("head") * (FF // n_head) + lax.axis_index("ctx") * units
    params["units"] = [
        (
            lax.dynamic_slice(tie(up_weight, first["low"]), (layer, 0, at), (1, D, units))[0],
            lax.dynamic_slice(tie(up_bias, first["low"]), (layer, at), (1, units)),
            lax.dynamic_slice(tie(down_weight, first["low"]), (layer, at, 0), (1, units, D))[0],
        )
        for layer in range(LAYERS)
    ]
    mlp_1, back_1 = mlp_both(hidden, cotangent, params, 1)
    rings, mlp_1, back_1 = together((gather_rings(low), mlp_1, back_1))
    far, rings, params["units"] = together((gather_flips(rings, 2), rings, params["units"]))
    near, far_near = together((gather_flips(rings, 1), gather_flips(far, 1)))
    second = attention(1, by_slot(rings, far, near, far_near), hidden, mlp_1, [cotangent, first["mixed_low"]])
    second, cot_far, cot_rings = together((second, gather_flips(cot_rings, 2, near), cot_rings))
    output_rows, low = second["h_out"], second["low"]

    pair, cot_near, cot_far_near = together((with_flip(low, 1), gather_flips(cot_rings, 1), gather_flips(cot_far, 1)))
    made = mlp_weight_grads(
        place, scalars, by_slot(cot_rings, cot_far, cot_near, cot_far_near), second["normal_all"], params, 1
    )
    (cot_all, up_share_1, pieces_1), four = together((made, with_flip(pair, 2)))
    queries_1, stats = together((backward_queries(1, second), gather_rings(four)))
    made = backward_keys(1, cot_all, stats, second, queries_1, cotangent, back_1, first)
    packed_1, grad, payload, dmix, delta = made
    first["dmix"], first["delta"] = dmix, delta
    back_0 = mlp_backward(grad, factor_0, hidden_in, params, 0)
    rings, back_0, pieces_1 = together((gather_rings(payload), back_0, head_swap(tie(pieces_1, payload))))
    received_1 = group_swap(tie(packed_1, back_0))
    far, rings, queries_0 = together(
        (gather_flips(rings, 2), rings, backward_queries(0, dict(first, delta=tie(delta, back_0))))
    )
    half_1 = reduce_mlp(tie(up_share_1, far), pieces_1, n_dp == 2)
    near, far_near = together((gather_flips(rings, 1), gather_flips(far, 1)))
    blocks = by_slot(rings, far, near, far_near)
    mlp_rings_1 = gather_rings(tie(half_1, near))
    g_all, up_share_0, pieces_0 = mlp_weight_grads(
        place, scalars, blocks, first["normal_all"], params, 0, [received_1, cot_all]
    )
    made = backward_keys(0, g_all, blocks, first, queries_0, grad, back_0, None)
    (packed_0, grad, _, _, _), pieces_0, mlp_rings_1, up_share_0, received_1 = together(
        (made, head_swap(pieces_0), mlp_rings_1, up_share_0, received_1)
    )
    half_0 = reduce_mlp(up_share_0, pieces_0, n_dp == 2)
    mlp_rings_0 = gather_rings(half_0)
    share_1 = attention_weight_grads(place, scalars, tie(received_1, half_0), second["normal_all"], params, 1)
    sum_1 = sum_dp(share_1)
    received_0, sum_1, mlp_rings_0, mlp_shares_1 = together(
        (group_swap(packed_0), sum_1, mlp_rings_0, finish([tie(x, half_0) for x in mlp_rings_1]))
    )
    share_0 = attention_weight_grads(place, scalars, received_0, first["normal_all"], params, 0)
    *big, mlp_small_1 = place_mlp(place, scalars, [tie(mlp_shares_1[0], share_0), *mlp_shares_1[1:]], 1, None)
    other_0 = swap_dp(share_0) if n_dp == 2 else lax.psum(share_0, "dp")
    attn_rings_1 = gather_rings(tie(sum_1, share_0))
    mlp_shares_0 = finish([tie(x, other_0) for x in mlp_rings_0])
    other_0, attn_rings_1 = together((other_0, attn_rings_1))
    sum_0 = (share_0.astype(f32) + other_0.astype(f32)).astype(bf16) if n_dp == 2 else other_0
    sum_0, big, mlp_small_1 = together((sum_0, big, mlp_small_1))
    *attn_big, attn_small_1 = place_attention(place, scalars, attn_rings_1, 1, None)
    up_grad, down_grad, mlp_small_0, out_grad = place_mlp(place, scalars, mlp_shares_0, 0, big)
    attn_rings_0, mlp_small_0, attn_big, attn_small_1 = together(
        (gather_rings(sum_0), mlp_small_0, attn_big, attn_small_1)
    )
    qkv_grad, gain, shift, mlp_g, mlp_s, qkv_b, up_b, down_b, out_b, layer_stats = place_attention(
        place, scalars, attn_rings_0, 0, attn_big, [attn_small_1, mlp_small_0, mlp_small_1], group * n_dp * D
    )
    return (
        output_rows, grad, gain, shift, mlp_g, mlp_s, qkv_grad, qkv_b, out_grad, out_b, up_grad, up_b, down_grad, down_b, layer_stats
    )


def solution(mesh):
    rows = P(("dp", "ctx", "head"), None)
    return jax.shard_map(
        per_device,
        mesh=mesh,
        in_specs=(rows, P("dp", None), *([P()] * 12), rows),
        out_specs=(
            rows,
            rows,
            P(None, "head"),
            P(None, "head"),
            P(None, "head"),
            P(None, "head"),
            P(None, None, "head"),
            P(None, "head"),
            P(None, None, "head"),
            P(None, "head"),
            P(None, None, "head"),
            P(None, "head"),
            P(None, None, "head"),
            P(None, "head"),
            P(),
        ),
        check_vma=False,
    )
```

```python
import math

import jax
import jax.numpy as jnp
from jax import lax
from jax.experimental import pallas as pl
from jax.experimental.pallas import tpu as pltpu
from jax.sharding import PartitionSpec as P

D = 512
FF = 2048
NH = 8
HD = 64
ROT = 16
LAYERS = 2
PAIRS = NH // 2
epsilon = 1e-05
masked_value = -1e30
score_scale = 0.125
rope_base = 10000.0
f32 = jnp.float32
bf16 = jnp.bfloat16
STEP = 1024
VMEM = pltpu.VMEM


def dot(a, b):
    return lax.dot_general(a, b, (((1,), (0,)), ((), ())), preferred_element_type=f32)


def dot_nt(a, b):
    return lax.dot_general(a, b, (((1,), (1,)), ((), ())), preferred_element_type=f32)


def norm_parts(hidden):
    centred = hidden - jnp.mean(hidden, axis=-1, keepdims=True)
    inverse = lax.rsqrt(jnp.mean(centred * centred, axis=-1, keepdims=True) + epsilon)
    return centred * inverse, inverse


def rope(x, cos_t, left_t, right_t):
    return x * cos_t + pltpu.roll(x, 128 - 8, 1) * left_t + pltpu.roll(x, 8, 1) * right_t


def start_of(place, ends):
    start = jnp.zeros_like(place)
    for end in ends:
        start = jnp.where(end <= place, end, start)
    return start


def end_of(place, ends, size):
    found = jnp.int32(size)
    for end in reversed(ends):
        found = jnp.where(place < end, end, found)
    return found


def split_low(x):
    high = x.astype(bf16)
    return high, (x - high.astype(f32)).astype(bf16)


def lane_of(rows):
    return lax.broadcasted_iota(jnp.int32, (rows, 128), 1)


def two_heads(x):
    first = lane_of(x.shape[0]) < HD
    zero = jnp.zeros_like(x)
    return jnp.concatenate([jnp.where(first, x, zero), jnp.where(first, zero, x)], axis=0)


def one_pair(x):
    rows = x.shape[0] // 2
    return jnp.where(lane_of(rows) < HD, x[:rows], x[rows:])


def dot_tn(a, b):
    return lax.dot_general(a, b, (((0,), (0,)), ((), ())), preferred_element_type=f32)


def two_heads_t(x):
    first = lax.broadcasted_iota(jnp.int32, x.shape, 0) < HD
    zero = jnp.zeros_like(x)
    return jnp.concatenate([jnp.where(first, x, zero), jnp.where(first, zero, x)], axis=1)


def one_pair_t(x):
    rows = x.shape[1] // 2
    return jnp.where(lax.broadcasted_iota(jnp.int32, (128, rows), 0) < HD, x[:, :rows], x[:, rows:])


def rope_t(x, cos_t, left_t, right_t):
    return x * cos_t + pltpu.roll(x, 128 - 8, 0) * left_t + pltpu.roll(x, 8, 0) * right_t


class Far:
    def __init__(self, array):
        self.array = array


class Lazy:
    def __init__(self, array, at=None, shape=None):
        self.array, self.at = array, at or (lambda ref: ref)
        self.shape = shape or array.shape


class Out:
    def __init__(self, shape, dtype):
        self.shape, self.dtype = shape, dtype


class Coming:
    def __init__(self, ref, copy):
        self.ref, self.copy, self.there = ref, copy, False

    def get(self):
        if not self.there:
            self.copy.wait()
            self.there = True
        return self.ref


class Going:
    def __init__(self, ref, copy):
        self.ref, self.copy, self.gone = ref, copy, False

    def send(self):
        self.copy.start()
        self.gone = True


def call(kernel, ins, outs, scratch=(), scalars=None, vmem=60 << 20, flops=10**9, into=None):
    specs, arrays = [], []

    def block(shape, layer, cols=None):
        place = (layer, *([0] * (len(shape) - 1)))
        return pl.BlockSpec((None, *shape[1:-1], cols or shape[-1]), lambda i: place)

    def whole(shape):
        return pl.BlockSpec(shape, lambda i: (0,) * len(shape))

    n_ins, n_outs = len(ins), len(outs)
    lead = 0
    if scalars is not None:
        specs.append(pl.BlockSpec(memory_space=pltpu.SMEM))
        arrays.append(scalars)
        lead = 1
    for item in ins:
        if isinstance(item, (Far, Lazy)):
            specs.append(pl.BlockSpec(memory_space=pl.ANY))
            arrays.append(item.array)
            continue
        array = item[0] if isinstance(item, tuple) else item
        specs.append(block(array.shape, *item[1:]) if isinstance(item, tuple) else whole(array.shape))
        arrays.append(array)
    aliases = {}
    if into is not None:
        spots = [k for k, o in enumerate(outs) if isinstance(o, tuple)]
        for spot, array in zip(spots, into):
            aliases[len(arrays)] = spot
            specs.append(pl.BlockSpec(memory_space=pl.ANY))
            arrays.append(array)
    shapes, out_specs = [], []
    for o in outs:
        if isinstance(o, tuple):
            shapes.append(o[0])
            out_specs.append(block(o[0].shape, o[1]))
        elif isinstance(o, Out):
            shapes.append(sds(o.shape, o.dtype))
            out_specs.append(pl.BlockSpec(memory_space=pl.ANY))
        else:
            shapes.append(o)
            out_specs.append(whole(o.shape))
    coming = [k for k, item in enumerate(ins) if isinstance(item, Lazy)]
    going = [k for k, o in enumerate(outs) if isinstance(o, Out)]
    slow = [VMEM(ins[k].shape, ins[k].array.dtype) for k in coming] + [VMEM(outs[k].shape, outs[k].dtype) for k in going]
    if slow:
        slow.append(pltpu.SemaphoreType.DMA((len(slow),)))

    def body(*refs):
        refs = list(refs)
        given = []
        if scalars is not None:
            lengths_ref = refs.pop(0)
            ctx, head = lax.axis_index("ctx"), lax.axis_index("head")
            ends = [lengths_ref[0, 0]]
            for k in range(1, 4):
                ends.append(ends[-1] + lengths_ref[0, k])
            given = [[ctx, head, ctx * lax.axis_size("head") + head, *ends, lax.axis_index("dp")]]
        finals = []
        if slow:
            extra = refs[len(refs) - len(slow) :]
            refs = refs[: len(refs) - len(slow)]
            sems = extra[-1]
            for j, k in enumerate(coming):
                copy = pltpu.make_async_copy(ins[k].at(refs[k]), extra[j], sems.at[j])
                copy.start()
                refs[k] = Coming(extra[j], copy)
            first_out = len(arrays) - lead
            for j, k in enumerate(going):
                j += len(coming)
                refs[first_out + k] = Going(extra[j], pltpu.make_async_copy(extra[j], refs[first_out + k], sems.at[j]))
                finals.append(refs[first_out + k])
        kernel(*given, *refs)
        for item in finals:
            if not item.gone:
                item.send()
        for item in finals:
            item.copy.wait()

    moved = sum(x.size * x.dtype.itemsize for x in arrays)
    return pl.pallas_call(
        body,
        grid=(1,),
        in_specs=specs,
        out_specs=out_specs,
        out_shape=shapes,
        scratch_shapes=[*scratch, *slow],
        input_output_aliases=aliases,
        compiler_params=pltpu.CompilerParams(vmem_limit_bytes=vmem),
        cost_estimate=pl.CostEstimate(flops=flops, bytes_accessed=moved, transcendentals=0),
    )(*arrays)


def lazy_layer(array, layer, cols=None):
    if cols is None:
        return Lazy(array, lambda ref: ref.at[layer], array.shape[1:])
    return Lazy(array, lambda ref: ref.at[layer, :, 0:cols], (*array.shape[1:-1], cols))


def sds(shape, dtype):
    return jax.ShapeDtypeStruct(shape, dtype)


def mlp_forward(hidden, params, layer):
    rows = hidden.shape[0]

    def kernel(h_ref, gain, shift, up, up_b, down, down_b, out_ref, factor_ref, normal_ref):
        normal, _ = norm_parts(h_ref[...].astype(f32))
        normal_ref[...] = normal.astype(bf16)
        x = (normal * gain[layer : layer + 1] + shift[layer : layer + 1]).astype(bf16)
        total = jnp.zeros((rows, D), f32)
        for j in range(0, FF, 512):
            gate = dot(x, up[:, j : j + 512]) + up_b[layer : layer + 1, j : j + 512]
            cdf = 0.5 * (1.0 + lax.erf(gate * math.sqrt(0.5)))
            pdf = jnp.exp(-0.5 * gate * gate) * (1.0 / math.sqrt(2.0 * math.pi))
            factor_ref[:, j : j + 512] = cdf + gate * pdf
            total += dot((gate * cdf).astype(bf16), down[j : j + 512])
        out_ref[...] = total + down_b[layer : layer + 1]

    return call(
        kernel,
        [
            hidden,
            params["mlp_gain"],
            params["mlp_shift"],
            (params["up_weight"], layer),
            params["up_bias"],
            (params["down_weight"], layer),
            params["down_bias"],
        ],
        [sds((rows, D), f32), sds((rows, FF), f32), sds((rows, D), bf16)],
        flops=2 * 2 * rows * D * FF,
    )


def mlp_both(hidden, grad, params, layer):
    rows = hidden.shape[0]

    def kernel(h_ref, g_ref, gain, shift, up, up_b, down, down_b, out_ref, back_ref):
        normal, _ = norm_parts(h_ref[...].astype(f32))
        x = (normal * gain[layer : layer + 1] + shift[layer : layer + 1]).astype(bf16)
        g_low = g_ref[...].astype(bf16)
        total = jnp.zeros((rows, D), f32)
        back = jnp.zeros((rows, D), f32)
        for j in range(0, FF, 512):
            gate = dot(x, up[:, j : j + 512]) + up_b[layer : layer + 1, j : j + 512]
            cdf = 0.5 * (1.0 + lax.erf(gate * math.sqrt(0.5)))
            pdf = jnp.exp(-0.5 * gate * gate) * (1.0 / math.sqrt(2.0 * math.pi))
            total += dot((gate * cdf).astype(bf16), down[j : j + 512])
            grad_gate = (dot_nt(g_low, down[j : j + 512]) * (cdf + gate * pdf)).astype(bf16)
            back += dot_nt(grad_gate, up[:, j : j + 512])
        out_ref[...] = total + down_b[layer : layer + 1]
        back_ref[...] = back

    return call(
        kernel,
        [
            hidden,
            grad,
            params["mlp_gain"],
            params["mlp_shift"],
            (params["up_weight"], layer),
            params["up_bias"],
            (params["down_weight"], layer),
            params["down_bias"],
        ],
        [sds((rows, D), f32), sds((rows, D), f32)],
    )


class Place:
    def __init__(self, n_dp, n_ctx, n_head, rows):
        self.n_ctx, self.n_head, self.rows = n_ctx, n_head, rows
        self.halves = n_dp == 2
        self.blocks = n_ctx * n_head
        self.group = self.blocks * rows
        self.units = FF // self.blocks
        self.packed_rows = 3 * D // self.blocks
        self.mixed_rows = D // self.blocks

    def position(self, scal, slot):
        shift, flip = slot // self.n_head, slot % self.n_head
        ctx = lax.rem(scal[0] - shift + self.n_ctx, self.n_ctx)
        return ctx * self.n_head + (scal[1] ^ flip)

    def ends(self, scal):
        return [scal[3 + k] for k in range(4)]


def delta_rows(grad_mixed_t, mixed_t):
    return jnp.concatenate(
        [
            jnp.sum(grad_mixed_t[n * HD : (n + 1) * HD].astype(f32) * mixed_t[n * HD : (n + 1) * HD], axis=0, keepdims=True)
            for n in range(NH)
        ],
        axis=0,
    )


def stat_payload(logs, deltas):
    parts = [*split_low(logs), *split_low(deltas)]
    top = jnp.concatenate(parts, axis=1)
    return jnp.concatenate([top, jnp.zeros_like(top)], axis=0)


def attention_forward(place, scalars, blocks, tables, params, layer, hidden, mlp_out, last_grad):
    rows, group = place.rows, place.group
    first_layer = layer == 0
    last = last_grad is not None
    tile = min(1024, group)

    def kernel(scal, *refs):
        refs = list(refs)
        xs = [refs.pop(0) for _ in range(place.blocks)]
        cos_t, left_t, right_t, gain, shift, w, b, out_w, out_b, h_ref, mlp_ref = refs[:11]
        refs = refs[11:]
        g_ref, below_ref = (refs.pop(0), refs.pop(0)) if last else (None, None)
        (normal_out, k_out, v_out, q_own, kv_own, mixed_ref, mixed_low_ref, log_ref, delta_ref, dmix_ref, h_out, stats_ref, low_ref) = refs[:13]
        a_all = refs[13]
        normal_all, k_all, v_all = normal_out.ref, k_out.ref, v_out.ref
        own_at = pl.multiple_of(scal[2] * rows, rows)
        ends = place.ends(scal)
        gain_l, shift_l = gain[layer : layer + 1], shift[layer : layer + 1]
        for slot in range(place.blocks):
            at = pl.multiple_of(place.position(scal, slot) * rows, rows)
            x = xs[slot][...].astype(f32)
            normal = norm_parts(x)[0] if first_layer else x
            normal_all[pl.ds(at, rows)] = normal.astype(bf16)
            a_all[pl.ds(at, rows)] = (normal * gain_l + shift_l).astype(bf16)
        normal_out.send()
        w, cos_t, left_t, right_t = (x.get() for x in (w, cos_t, left_t, right_t))

        def project(i, _):
            at = pl.multiple_of(i * tile, tile)
            k = dot(a_all[pl.ds(at, tile)], w[:, D : 2 * D]) + b[layer : layer + 1, D : 2 * D]
            tabs = [t[pl.ds(at, tile)] for t in (cos_t, left_t, right_t)]
            for p in range(PAIRS):
                k_all[pl.ds(at, tile), 128 * p : 128 * p + 128] = rope(k[:, 128 * p : 128 * p + 128], *tabs).astype(bf16)
            v = dot(a_all[pl.ds(at, tile)], w[:, 2 * D :]) + b[layer : layer + 1, 2 * D :]
            v_all[pl.ds(at, tile)] = v.astype(bf16)
            return 0

        first_key = start_of(own_at, ends)
        low, high = first_key // STEP, (own_at + rows - 1) // STEP + 1
        lax.fori_loop(low * (STEP // tile), high * (STEP // tile), project, 0)
        k_out.send()
        v_out.send()
        kv_own[0:rows], kv_own[rows : 2 * rows] = k_all[pl.ds(own_at, rows)], v_all[pl.ds(own_at, rows)]
        q = dot(a_all[pl.ds(own_at, rows)], w[:, :D]) + b[layer : layer + 1, :D]
        tabs = [t[pl.ds(own_at, rows)] for t in (cos_t, left_t, right_t)]
        for p in range(PAIRS):
            turned = rope(q[:, 128 * p : 128 * p + 128], *tabs).astype(bf16)
            q_own[:, 128 * p : 128 * p + 128] = turned * jnp.asarray(score_scale, bf16)
        t = own_at + lax.broadcasted_iota(jnp.int32, (1, rows), 1)
        start = start_of(t, ends)
        doubled = [two_heads(q_own[:, 128 * p : 128 * p + 128]) for p in range(PAIRS)]

        def attend(i, carry):
            at = pl.multiple_of(i * STEP, STEP)
            s_at = at + lax.broadcasted_iota(jnp.int32, (STEP, 1), 0)
            bias = jnp.where((s_at >= start) & (s_at <= t), 0.0, masked_value)
            bias = jnp.concatenate([bias, bias], axis=1)
            new = []
            for p in range(PAIRS):
                most, total, acc = carry[p]
                scores = dot_nt(k_all[pl.ds(at, STEP), 128 * p : 128 * p + 128], doubled[p]) + bias
                newest = jnp.maximum(most, jnp.max(scores, axis=0, keepdims=True))
                chance = jnp.exp(scores - newest)
                scale = jnp.exp(most - newest)
                total = total * scale + jnp.sum(chance, axis=0, keepdims=True)
                acc = acc * scale + dot_tn(v_all[pl.ds(at, STEP), 128 * p : 128 * p + 128], chance.astype(bf16))
                new.append((newest, total, acc))
            return tuple(new)

        begin = tuple(
            (jnp.full((1, 2 * rows), masked_value, f32), jnp.zeros((1, 2 * rows), f32), jnp.zeros((128, 2 * rows), f32))
            for _ in range(PAIRS)
        )
        done = lax.fori_loop(low, high, attend, begin)
        logs = []
        for p in range(PAIRS):
            most, total, acc = done[p]
            mixed_ref[128 * p : 128 * p + 128] = one_pair_t(acc / total)
            log = most + jnp.log(total)
            logs += [log[:, :rows], log[:, rows:]]
        log_rows = jnp.concatenate(logs, axis=0)
        log_ref[...] = log_rows
        mixed_low = mixed_ref[...].astype(bf16)
        if last:
            size = place.mixed_rows
            for p in range(place.n_head):
                for c in range(place.n_ctx):
                    at = 128 * p + size * c
                    mixed_low_ref[c * place.n_head + p, 0:size] = below_ref[at : at + size]
                    mixed_low_ref[c * place.n_head + p, size : 2 * size] = mixed_low[at : at + size]
        else:
            mixed_low_ref[...] = mixed_low
        out_w = out_w.get()
        attn_out = dot_tn(mixed_low, out_w[...]) + out_b[layer : layer + 1]
        h = h_ref.get()[...].astype(f32)
        mlp = mlp_ref.get()[...]
        result = h + attn_out + mlp
        lane = lane_of(8)
        sums = [jnp.sum(jnp.sum(v * v, axis=1, keepdims=True), axis=0, keepdims=True) for v in (h, attn_out, mlp)]
        stats_ref[...] = jnp.where(lane == 0, sums[0], jnp.where(lane == 1, sums[1], jnp.where(lane == 2, sums[2], 0.0)))
        if last:
            h_out[...] = result.astype(bf16)
            dmix = dot_nt(out_w[...], g_ref[...]).astype(bf16)
            dmix_ref[...] = dmix
            deltas = delta_rows(dmix, mixed_ref[...])
            delta_ref[...] = deltas
            low_ref[...] = stat_payload(log_rows, deltas)
        else:
            h_out[...] = result
            low_ref[...] = norm_parts(result)[0].astype(bf16)
            dmix_ref[...] = jnp.zeros_like(dmix_ref)
            delta_ref[...] = jnp.zeros_like(delta_ref)

    ins = [
        *blocks,
        *[Lazy(x) for x in tables],
        params["attn_gain"],
        params["attn_shift"],
        lazy_layer(params["qkv_sorted"], layer),
        params["qkv_bias_sorted"],
        lazy_layer(params["out_weight"], layer),
        params["out_bias"],
        Lazy(hidden),
        Lazy(mlp_out),
    ]
    if last:
        ins += last_grad
    outs = [
        Out((group, D), bf16),
        Out((group, D), bf16),
        Out((group, D), bf16),
        sds((rows, D), bf16),
        sds((2 * rows, D), bf16),
        sds((D, rows), f32),
        sds((place.blocks, 2 * place.mixed_rows, rows) if last else (D, rows), bf16),
        sds((NH, rows), f32),
        sds((NH, rows), f32),
        sds((D, rows), bf16),
        sds((rows, D), bf16 if last else f32),
        sds((8, 128), f32),
        sds((16, D) if last else (rows, D), bf16),
    ]
    return call(kernel, ins, outs, [VMEM((group, D), bf16)], scalars, flops=60 * 10**9)


def mlp_backward(grad, factor, hidden, params, layer):
    rows = grad.shape[0]

    def kernel(g_ref, factor_ref, down, up, out_ref):
        g_low = g_ref[...].astype(bf16)
        total = jnp.zeros((rows, D), f32)
        for j in range(0, FF, 512):
            grad_gate = (dot_nt(g_low, down[j : j + 512]) * factor_ref[:, j : j + 512]).astype(bf16)
            total += dot_nt(grad_gate, up[:, j : j + 512])
        out_ref[...] = total

    return call(
        kernel,
        [grad, factor, (params["down_weight"], layer), (params["up_weight"], layer)],
        [sds((rows, D), f32)],
        flops=2 * 2 * rows * D * FF,
    )[0]


def query_backward(place, scalars, tables, own_tables, params, layer, kept):
    rows, group = place.rows, place.group
    tile = min(1024, group)

    def kernel(scal, cos_t, left_t, right_t, own_tabs, gain, shift, w, b, normal_all, k_all, v_all, q_own, dmix_ref, log_ref, delta_ref, q_out, grad_ref, grad_t_ref):
        q_all = q_out.ref
        own_at = pl.multiple_of(scal[2] * rows, rows)
        ends = place.ends(scal)
        gain_l, shift_l = gain[layer : layer + 1], shift[layer : layer + 1]

        def project(i, _):
            at = pl.multiple_of(i * tile, tile)
            a = (normal_all[pl.ds(at, tile)].astype(f32) * gain_l + shift_l).astype(bf16)
            q = dot(a, w[...]) + b[layer : layer + 1, :D]
            tabs = [t[pl.ds(at, tile)] for t in (cos_t, left_t, right_t)]
            for p in range(PAIRS):
                turned = rope(q[:, 128 * p : 128 * p + 128], *tabs).astype(bf16)
                q_all[pl.ds(at, tile), 128 * p : 128 * p + 128] = turned * jnp.asarray(score_scale, bf16)
            return 0

        last_end = end_of(own_at + rows - 1, ends, group)
        low, high = own_at // STEP, (last_end + STEP - 1) // STEP
        lax.fori_loop(low * (STEP // tile), high * (STEP // tile), project, 0)
        q_out.send()
        k_all, v_all = k_all.get(), v_all.get()
        t = own_at + lax.broadcasted_iota(jnp.int32, (1, rows), 1)
        start = start_of(t, ends)
        q2 = [two_heads(q_own[:, 128 * p : 128 * p + 128]) for p in range(PAIRS)]
        d2 = [two_heads_t(dmix_ref[128 * p : 128 * p + 128]) for p in range(PAIRS)]
        log2 = [jnp.concatenate([log_ref[2 * p : 2 * p + 1], log_ref[2 * p + 1 : 2 * p + 2]], axis=1) for p in range(PAIRS)]
        delta2 = [
            jnp.concatenate([delta_ref[2 * p : 2 * p + 1], delta_ref[2 * p + 1 : 2 * p + 2]], axis=1) for p in range(PAIRS)
        ]

        def queries(i, carry):
            at = pl.multiple_of(i * STEP, STEP)
            s = at + lax.broadcasted_iota(jnp.int32, (STEP, 1), 0)
            bias = jnp.where((s >= start) & (s <= t), 0.0, masked_value)
            bias = jnp.concatenate([bias, bias], axis=1)
            new = []
            for p in range(PAIRS):
                ks = k_all[pl.ds(at, STEP), 128 * p : 128 * p + 128]
                vs = v_all[pl.ds(at, STEP), 128 * p : 128 * p + 128]
                chance = jnp.exp(dot_nt(ks, q2[p]) + bias - log2[p])
                grad_s = (chance * (dot(vs, d2[p]) - delta2[p])).astype(bf16)
                new.append(carry[p] + dot_tn(ks, grad_s))
            return tuple(new)

        zero = jnp.zeros((128, 2 * rows), f32)
        done = lax.fori_loop(
            start_of(own_at, ends) // STEP, (own_at + rows - 1) // STEP + 1, queries, tuple(zero for _ in range(PAIRS))
        )
        tabs = [own_tabs[0:rows].T, -own_tabs[rows : 2 * rows].T, -own_tabs[2 * rows : 3 * rows].T]
        for p in range(PAIRS):
            grad_t = rope_t(one_pair_t(done[p]) * score_scale, *tabs)
            grad_t_ref[128 * p : 128 * p + 128] = grad_t.astype(bf16)
            grad_ref[:, 128 * p : 128 * p + 128] = grad_t.T.astype(bf16)

    return call(
        kernel,
        [
            *tables,
            own_tables,
            params["attn_gain"],
            params["attn_shift"],
            (params["qkv_sorted"], layer, D),
            params["qkv_bias_sorted"],
            kept["normal_all"],
            Lazy(kept["k_all"]),
            Lazy(kept["v_all"]),
            kept["q_own"],
            kept["dmix"],
            kept["log"],
            kept["delta"],
        ],
        [Out((group, D), bf16), sds((rows, D), bf16), sds((D, rows), bf16)],
        (),
        scalars,
        flops=30 * 10**9,
    )


def key_backward(place, scalars, g_whole, stats, own_tables, params, layer, kept, queries, grad, grad_mlp_in, mixed_below):
    rows, group = place.rows, place.group
    below = layer > 0
    n_stats = len(stats)
    tile = min(1024, group)
    part = place.packed_rows

    def kernel(scal, *refs):
        refs = list(refs)
        ss = [refs.pop(0) for _ in range(n_stats)]
        (g_all, own_tabs, gain, mlp_gain, w, out_w, q_all, gq_ref, gq_t_ref, kv_own, h_ref, g_ref, gmlp_ref, stats_ref) = refs[:14]
        refs = refs[14:]
        if below:
            below_mixed, below_log, below_w, carried = refs[:4]
            refs = refs[4:]
        pieces_out, g_out, payload_ref, dmix_out, delta_out = refs[:5]
        dm_all, log_all, delta_all, packed_t = refs[5:]
        own_at = pl.multiple_of(scal[2] * rows, rows)
        ends = place.ends(scal)
        gain_l = gain[layer : layer + 1]
        for slot in range(place.blocks):
            at = pl.multiple_of(place.position(scal, slot) * rows, rows)
            if below:
                flip = slot % place.n_head
                info = ss[slot // place.n_head][16 * flip : 16 * flip + 16].astype(f32)[:NH]
            else:
                info = ss[slot][rows : rows + 16].astype(f32)[:NH]
            log_all[:, pl.ds(at, rows)] = info[:, 0:128] + info[:, 128:256]
            delta_all[:, pl.ds(at, rows)] = info[:, 256:384] + info[:, 384:512]
        last_end = end_of(own_at + rows - 1, ends, group)

        def project(i, _):
            at = pl.multiple_of(i * tile, tile)
            dm_all[pl.ds(at, tile)] = dot_nt(g_all[pl.ds(at, tile)], out_w[...]).astype(bf16)
            return 0

        low, high = own_at // STEP, (last_end + STEP - 1) // STEP
        lax.fori_loop(low * (STEP // tile), high * (STEP // tile), project, 0)
        q_all = q_all.get()
        s_at = own_at + lax.broadcasted_iota(jnp.int32, (rows, 1), 0)
        k2 = [two_heads(kv_own[0:rows, 128 * p : 128 * p + 128]) for p in range(PAIRS)]
        v2 = [two_heads(kv_own[rows : 2 * rows, 128 * p : 128 * p + 128]) for p in range(PAIRS)]

        def keys(i, carry):
            at = pl.multiple_of(i * STEP, STEP)
            t = at + lax.broadcasted_iota(jnp.int32, (1, STEP), 1)
            start = start_of(t, ends)
            bias = jnp.where((s_at >= start) & (s_at <= t), 0.0, masked_value)
            new = []
            for p in range(PAIRS):
                dk, dv = carry[p]
                qs = q_all[pl.ds(at, STEP), 128 * p : 128 * p + 128]
                dms = dm_all[pl.ds(at, STEP), 128 * p : 128 * p + 128]
                scores = dot_nt(k2[p], qs)
                pulled = dot_nt(v2[p], dms)
                chances, grads = [], []
                for half in range(2):
                    n = 2 * p + half
                    part = slice(half * rows, half * rows + rows)
                    chance = jnp.exp(scores[part] + bias - log_all[n : n + 1, pl.ds(at, STEP)])
                    grads.append(chance * (pulled[part] - delta_all[n : n + 1, pl.ds(at, STEP)]))
                    chances.append(chance)
                chance = jnp.concatenate(chances, axis=0).astype(bf16)
                grad_s = jnp.concatenate(grads, axis=0).astype(bf16)
                new.append((dk + dot(grad_s, qs), dv + dot(chance, dms)))
            return tuple(new)

        zero = jnp.zeros((2 * rows, 128), f32)
        done = lax.fori_loop(low, high, keys, tuple((zero, zero) for _ in range(PAIRS)))
        tabs = [own_tabs[0:rows], -own_tabs[rows : 2 * rows], -own_tabs[2 * rows : 3 * rows]]
        grad_k = [rope(one_pair(done[p][0]), *tabs).astype(bf16) for p in range(PAIRS)]
        grad_v = [one_pair(done[p][1]).astype(bf16) for p in range(PAIRS)]
        w = w.get()
        grad_in = dot_nt(gq_ref.get()[...], w[:, 0:D])
        for j, parts in ((1, grad_k), (2, grad_v)):
            grad_in += dot_nt(jnp.concatenate(parts, axis=1), w[:, j * D : j * D + D])

        normal, inverse = norm_parts(h_ref.get()[...].astype(f32))
        grad_mlp = gmlp_ref.get()[...]
        grad_normal = grad_in * gain_l + grad_mlp * mlp_gain[layer : layer + 1]
        back = inverse * (
            grad_normal
            - jnp.mean(grad_normal, axis=-1, keepdims=True)
            - normal * jnp.mean(grad_normal * normal, axis=-1, keepdims=True)
        )
        g_new = g_ref.get()[...].astype(f32) + back
        g_out[...] = g_new

        sums = [
            jnp.sum(v, axis=0, keepdims=True)
            for v in (grad_in * normal, grad_in, grad_mlp * normal, grad_mlp)
        ]
        for j in range(3):
            for p in range(PAIRS):
                if j == 0:
                    turned = gq_t_ref.get()[128 * p : 128 * p + 128]
                else:
                    turned = (grad_k, grad_v)[j - 1][p].astype(f32).T.astype(bf16)
                for half in range(2):
                    at = (2 * p + half) * 3 * HD + j * HD
                    packed_t[at : at + HD] = turned[half * HD : half * HD + HD]
        layer_sums = jnp.where(lane_of(8) < 4, stats_ref[...], 0.0)
        layer_sums = jnp.broadcast_to(pltpu.roll(layer_sums, scal[2] * 4, 1)[0:1], (16, 128))
        row16 = lax.broadcasted_iota(jnp.int32, (16, 128), 0)
        for p in range(place.n_head):
            extra = jnp.concatenate([x[:, 128 * p : 128 * p + 128] for x in sums] + [jnp.zeros((4, 128), f32)], axis=0)
            extra = jnp.concatenate([extra, extra], axis=0)
            extra = jnp.where((row16 & 7) == 4, layer_sums, extra)
            high, rest = split_low(extra)
            extra = jnp.where(row16 < 8, high, rest)
            for c in range(place.n_ctx):
                at = (p * place.n_ctx + c) * part
                pieces_out[c * place.n_head + p, 0:part] = packed_t[at : at + part]
                pieces_out[c * place.n_head + p, part : part + 16] = extra
        if below:
            pieces_out[:, part + 16 :] = carried[...]

        g_low = g_new.astype(bf16)
        if below:
            payload_ref[0:rows] = g_low
            dmix = dot_nt(below_w.get()[...], g_low).astype(bf16)
            dmix_out[...] = dmix
            deltas = delta_rows(dmix, below_mixed.get()[...])
            delta_out[...] = deltas
            payload_ref[rows : rows + 16] = stat_payload(below_log[...], deltas)
        else:
            payload_ref[...] = jnp.zeros_like(payload_ref)
            dmix_out[...] = jnp.zeros_like(dmix_out)
            delta_out[...] = jnp.zeros_like(delta_out)

    ins = [
        *stats,
        g_whole,
        own_tables,
        params["attn_gain"],
        params["mlp_gain"],
        lazy_layer(params["qkv_sorted"], layer),
        (params["out_weight"], layer),
        *[Lazy(x) for x in queries],
        kept["kv_own"],
        Lazy(kept["hidden"]),
        Lazy(grad),
        Lazy(grad_mlp_in),
        kept["stats"],
    ]
    if below:
        ins += [Lazy(mixed_below["mixed"]), mixed_below["log"], lazy_layer(params["out_weight"], layer - 1)]
        ins.append(kept["mixed_low"])
    outs = [
        sds((place.blocks, part + 16 + (2 * place.mixed_rows if below else 0), rows), bf16),
        sds((rows, D), f32),
        sds((rows + 16, D) if below else (16, D), bf16),
        sds((D, rows) if below else (16, rows), bf16),
        sds((NH, rows), f32),
    ]
    scratch = [VMEM((group, D), bf16), VMEM((NH, group), f32), VMEM((NH, group), f32), VMEM((3 * D, rows), bf16)]
    return call(kernel, ins, outs, scratch, scalars, flops=60 * 10**9)


def mlp_weight_grads(place, scalars, blocks, normal_all, params, layer, mixed=None):
    group, rows, units = place.group, place.rows, place.units
    tile = min(2048, group)
    size = 0 if mixed is None else place.mixed_rows

    def kernel(scal, *refs):
        gs = refs[: place.blocks]
        refs = list(refs[place.blocks :])
        mixed_ref, other_ref = (refs.pop(0), refs.pop(0)) if size else (None, None)
        normal_ref, gain, shift, up, up_b, down, g_out, up_out, down_out = refs[:9]
        g_ref = g_out.ref
        mixed_t = refs[9] if size else None
        gain_l, shift_l = gain[layer : layer + 1], shift[layer : layer + 1]
        for slot in range(place.blocks):
            at = pl.multiple_of(place.position(scal, slot) * rows, rows)
            g_ref[pl.ds(at, rows)] = gs[slot][0:rows]
            if size:
                mixed_t[:, slot * rows : (slot + 1) * rows] = mixed_ref[slot, place.packed_rows + 16 :]

        g_out.send()

        def step(i, carry):
            up_t, down_g, bias, g_sum = carry
            at = pl.multiple_of(i * tile, tile)
            x = (normal_ref[pl.ds(at, tile)].astype(f32) * gain_l + shift_l).astype(bf16)
            g = g_ref[pl.ds(at, tile)]
            gate = dot(x, up[...]) + up_b[...]
            cdf = 0.5 * (1.0 + lax.erf(gate * math.sqrt(0.5)))
            pdf = jnp.exp(-0.5 * gate * gate) * (1.0 / math.sqrt(2.0 * math.pi))
            acted = (gate * cdf).astype(bf16)
            grad_gate = (dot_nt(g, down[...]) * (cdf + gate * pdf)).astype(bf16)
            up_t += dot(grad_gate.T, x)
            down_g += dot(acted.T, g)
            bias += jnp.sum(grad_gate.astype(f32), axis=0, keepdims=True)
            g_sum += jnp.sum(g.astype(f32), axis=0, keepdims=True)
            return up_t, down_g, bias, g_sum

        zero = jnp.zeros((units, D), f32)
        up_t, down_g, bias, g_sum = lax.fori_loop(
            0, group // tile, step, (zero, zero, jnp.zeros((1, units), f32), jnp.zeros((1, D), f32))
        )
        up_out[0:units] = up_t.astype(bf16)
        if units < 128:
            bias = jnp.concatenate([bias, jnp.zeros((1, 128 - units), f32)], axis=1)
        wide = jnp.concatenate([bias, jnp.zeros((1, D - 128), f32)], axis=1)
        row = lax.broadcasted_iota(jnp.int32, (32, D), 0)
        extra = jnp.where((row & 7) == 0, wide, jnp.where((row & 7) == 1, g_sum, 0.0))
        high, rest = split_low(extra)
        up_out[units : units + 32] = jnp.where(row < 8, high, jnp.where(row < 16, rest, jnp.zeros_like(rest)))
        if size:
            out_g = [dot(mixed_t[k * size : (k + 1) * size], g[...]) for k, g in enumerate((g_ref, other_ref))]
        for p in range(place.n_head):
            cols = slice(128 * p, 128 * p + 128)
            down_out[p, 0:units] = down_g[:, cols].astype(bf16)
            for k in range(2 if size else 0):
                down_out[p, units + k * size : units + (k + 1) * size] = out_g[k][:, cols].astype(bf16)

    up, up_b, down = params["units"][layer]
    made = call(
        kernel,
        [*blocks, *([] if mixed is None else mixed), normal_all, params["mlp_gain"], params["mlp_shift"], up, up_b, down],
        [Out((group, D), bf16), sds((units + 32, D), bf16), sds((place.n_head, units + 2 * size, 128), bf16)],
        [VMEM((2 * size, group), bf16)] if size else [],
        scalars,
        flops=4 * 2 * group * D * units,
    )
    return made


def attention_weight_grads(place, scalars, received, normal_all, params, layer):
    group, rows, part = place.group, place.rows, place.packed_rows
    tile = min(2048, group)

    def kernel(received_ref, normal_ref, gain, shift, out_ref, chunk_t):
        gain_l, shift_l = gain[layer : layer + 1], shift[layer : layer + 1]
        extra = jnp.zeros((16, 128), f32)
        for j in range(place.blocks):
            chunk_t[:, j * rows : (j + 1) * rows] = received_ref[j, 0:part]
            extra += received_ref[j, part : part + 16].astype(f32)
        total = jnp.zeros((part, D), f32)
        for at in range(0, group, tile):
            x = (normal_ref[at : at + tile].astype(f32) * gain_l + shift_l).astype(bf16)
            total += dot(chunk_t[:, at : at + tile], x)
        out_ref[0:part] = total.astype(bf16)
        bias = dot_nt(jnp.ones((16, group), bf16), chunk_t[...])
        bias = jnp.concatenate([bias, jnp.zeros((16, 128 - part), f32)], axis=1)
        extra = extra[0:8] + extra[8:16]
        wide = jnp.concatenate([extra[k : k + 1] for k in range(4)], axis=1)
        none = jnp.zeros((1, D - 256), f32)
        second = jnp.concatenate([bias[0:1], extra[4:5], none], axis=1)
        row = lax.broadcasted_iota(jnp.int32, (16, D), 0)
        high, rest = split_low(jnp.where((row & 7) == 0, wide, jnp.where((row & 7) == 1, second, 0.0)))
        out_ref[part : part + 16] = jnp.where(row < 8, high, rest)

    return call(
        kernel,
        [received, normal_all, params["attn_gain"], params["attn_shift"]],
        [sds((part + 16, D), bf16)],
        [VMEM((part, group), bf16)],
        flops=2 * group * D * part,
    )[0]


def pack_mlp(place, scalars, up_share, pieces, halves):
    rows = place.units + 32 + pieces.shape[1]
    half = rows // 2

    def kernel(scal, up_ref, pieces_ref, *refs):
        if halves:
            mine, other, full = refs
        else:
            (full,) = refs
        full[0 : place.units + 32] = up_ref[...]
        for p in range(place.n_head):
            full[place.units + 32 :, 128 * p : 128 * p + 128] = pieces_ref[p]
        if halves:
            at = pl.multiple_of(scal[7] * half, half)
            mine[...] = full[pl.ds(at, half)]
            other[...] = full[pl.ds(pl.multiple_of(half - at, half), half)]

    outs = [sds((half, D), bf16)] * 2 if halves else [sds((rows, D), bf16)]
    scratch = [VMEM((rows, D), bf16)] if halves else []
    return call(kernel, [up_share, pieces], outs, scratch, scalars, flops=10**7)


def along_lanes(rows, width):
    if width == 128:
        return jnp.concatenate(rows, axis=1)
    full = len(rows) * width
    out = jnp.zeros((8, full), f32)
    for k, row in enumerate(rows):
        lane = lax.broadcasted_iota(jnp.int32, (8, full), 1)
        row = jnp.concatenate([row, jnp.zeros((1, full - 128), f32)], axis=1)
        row = jnp.where(lane < width, jnp.broadcast_to(row, (8, full)), 0.0)
        out += pltpu.roll(row, k * width, 1) if k else row
    return out[0:1]


def whole_shares(place, scal, refs, at, size, full, halves):
    if not halves:
        return [x.at[at : at + size] for x in refs]
    half = size // 2
    for s in range(place.n_ctx):
        full[s, pl.ds(pl.multiple_of(scal[7] * half, half), half)] = refs[s][at : at + half]
        start = s * half
        full[s, pl.ds(pl.multiple_of((1 - scal[7]) * half, half), half)] = refs[-1][start : start + half]
    return [full.at[s] for s in range(place.n_ctx)]


def place_mlp(place, scalars, shares, layer, into):
    n_ctx, units = place.n_ctx, place.units
    taken = 0 if into is None else 2
    halves = len(shares) > n_ctx
    size = place.mixed_rows if layer == 0 else 0
    rows = 2 * units + 32 + 2 * size

    def kernel(scal, *refs):
        up_out, down_out, small_out, *out_outs, up_t, bias_rows, full = refs[len(shares) + taken :]
        ordered = len(shares) == 1
        if ordered:
            srcs = [refs[0].at[c * rows : (c + 1) * rows] for c in range(n_ctx)]
        else:
            srcs = whole_shares(place, scal, refs[: len(shares)], 0, rows, full, halves)
        for s in range(n_ctx):
            c = s if ordered else lax.rem(scal[0] - s + n_ctx, n_ctx)
            at = pl.multiple_of(c * units, units)
            up_t[pl.ds(at, units)] = srcs[s][0:units].astype(f32)
            extra = srcs[s][units : units + 16].astype(f32)
            extra = extra[0:8] + extra[8:16]
            bias_rows[c] = jnp.broadcast_to(extra[0:1, :128], (8, 128))
            if s == 0:
                small_out[...] = jnp.zeros_like(small_out)
                for q in range(place.n_head):

                    @pl.when(scal[1] == q)
                    def _():
                        small_out[1:2, 0:128] = extra[1:2, 128 * q : 128 * q + 128]

            for p in range(place.n_head):
                at = pl.multiple_of(p * (FF // place.n_head) + c * units, units)
                base = units + 32
                down_out[pl.ds(at, units)] = srcs[s][base : base + units, 128 * p : 128 * p + 128].astype(f32)
                at = pl.multiple_of(p * 128 + c * place.mixed_rows, place.mixed_rows)
                for k in range(2 if size else 0):
                    start = base + units + k * size
                    out_outs[0][k, pl.ds(at, size)] = srcs[s][start : start + size, 128 * p : 128 * p + 128].astype(f32)
        up_out[...] = up_t[...].T
        small_out[0:1] = along_lanes([bias_rows[c][0:1] for c in range(n_ctx)], units)

    wide = FF // place.n_head
    return call(
        kernel,
        shares,
        [
            (sds((LAYERS, D, wide), f32), layer),
            (sds((LAYERS, FF, 128), f32), layer),
            sds((8, wide), f32),
            *([sds((LAYERS, D, 128), f32)] if size else []),
        ],
        [VMEM((wide, D), f32), VMEM((n_ctx, 8, 128), f32), VMEM((n_ctx, rows, D) if halves else (1, 16, D), bf16)],
        scalars,
        flops=10**7,
        into=into,
    )


def place_attention(place, scalars, shares, layer, into, smalls=None, count=1):
    n_ctx, part = place.n_ctx, place.packed_rows
    taken = 0 if into is None else 1
    wide = 3 * D // place.n_head
    wide_up = FF // place.n_head
    given = [] if smalls is None else smalls

    def kernel(scal, *refs):
        shares_in, given_in = refs[: len(shares)], refs[len(shares) : len(shares) + len(given)]
        qkv_out, *small_outs, qkv_t, info, small = refs[len(shares) + len(given) + taken :]
        small[...] = jnp.zeros_like(small)
        for s in range(n_ctx):
            c = lax.rem(scal[0] - s + n_ctx, n_ctx)
            at = pl.multiple_of(c * part, part)
            qkv_t[pl.ds(at, part)] = shares_in[s][0:part].astype(f32)
            extra = shares_in[s][part : part + 16].astype(f32)
            extra = extra[0:8] + extra[8:16]
            info[c] = extra
            if s == 0:
                for k in range(4):
                    small[k : k + 1, 0:128] = extra[0:1, 128 * k : 128 * k + 128]
                small[4:5, 0:128] = extra[1:2, 128:256]
        qkv_out[...] = qkv_t[...].T
        small[5:6] = along_lanes([info[c, 1:2, 0:128] for c in range(n_ctx)], part)
        if smalls is None:
            small_outs[0][...] = small[...]
            return
        attn_1, mlp_0, mlp_1 = given_in
        lane = lane_of(1)
        for spot, attn, mlp in ((0, small, mlp_0), (1, attn_1, mlp_1)):
            row = slice(spot, spot + 1)
            for k in range(4):
                small_outs[k][row] = attn[k : k + 1, 0:128]
            small_outs[4][row] = attn[5:6]
            small_outs[5][row] = mlp[0:1]
            small_outs[6][row] = mlp[1:2, 0:128]
            small_outs[7][row] = mlp[1:2, 0:128]
            for k in range(3):
                picked = jnp.where((lane & 3) == k, attn[4:5, 0:128], 0.0)
                small_outs[8][row, k : k + 1] = jnp.sqrt(jnp.sum(picked, axis=1, keepdims=True) * (1.0 / count))

    if smalls is None:
        outs = [sds((8, wide), f32)]
    else:
        widths = [128, 128, 128, 128, wide, wide_up, 128, 128, 3]
        outs = [sds((LAYERS, width), f32) for width in widths]
    return call(
        kernel,
        [*shares, *given],
        [(sds((LAYERS, D, wide), f32), layer), *outs],
        [
            VMEM((wide, D), f32),
            VMEM((n_ctx, 8, D), f32),
            VMEM((8, wide), f32),
        ],
        scalars,
        flops=10**7,
        into=into,
    )


def prepare(place, lengths, qkv_weight, qkv_bias):
    group = place.group
    blocks = group // 128
    dim = jnp.arange(128, dtype=jnp.int32)[None, :] % HD
    freq = rope_base ** (-2.0 * (dim % (ROT // 2)).astype(f32) / ROT)
    starts = jnp.concatenate([jnp.zeros((1,), jnp.int32), lengths[0, :3]])
    starts = jnp.stack([starts[0], starts[1], starts[1] + starts[2], starts[1] + starts[2] + starts[3]])
    first = (jnp.arange(blocks, dtype=jnp.int32)[:, None] * 128 - starts[None, :]).reshape(-1, 1)
    whole = jnp.concatenate([first, jnp.arange(128, dtype=jnp.int32)[:, None]], axis=0).astype(f32) * freq
    cosines, sines = jnp.cos(whole), jnp.sin(whole)
    base = 4 * blocks

    def kernel(scal, w_ref, b_ref, cos_ref, sin_ref, w_out, b_out, cos_t, left_t, right_t, own_t):
        def sort(read, write):
            for p in range(PAIRS):
                a, b, c = (read(slice(128 * (3 * p + i), 128 * (3 * p + i) + 128)).astype(f32) for i in range(3))
                first = lane_of(a.shape[0]) < HD
                made = (jnp.where(first, a, b), pltpu.roll(jnp.where(first, c, a), HD, 1), jnp.where(first, b, c))
                for j in range(3):
                    write(slice(j * D + 128 * p, j * D + 128 * p + 128), made[j])

        for layer in range(LAYERS):

            def store(to, x, layer=layer):
                w_out[layer, :, to] = x.astype(bf16)

            sort(lambda at, layer=layer: w_ref[layer, :, at], store)

        def store_bias(to, x):
            b_out[:, to] = x

        sort(lambda at: b_ref[:, at], store_bias)
        ends = place.ends(scal)
        dim = lane_of(128) & (HD - 1)
        cos_b, sin_b = cos_ref[base : base + 128], sin_ref[base : base + 128]

        def table(i, _):
            at = pl.multiple_of(i * 128, 128)
            t = at + lax.broadcasted_iota(jnp.int32, (128, 1), 0)
            cos_a, sin_a = cos_ref[pl.ds(4 * i, 1)], sin_ref[pl.ds(4 * i, 1)]
            for k in range(1, 4):
                later = t >= ends[k - 1]
                cos_a = jnp.where(later, cos_ref[pl.ds(4 * i + k, 1)], cos_a)
                sin_a = jnp.where(later, sin_ref[pl.ds(4 * i + k, 1)], sin_a)
            cosine = cos_a * cos_b - sin_a * sin_b
            sine = sin_a * cos_b + cos_a * sin_b
            cos_t[pl.ds(at, 128)] = jnp.where(dim < ROT, cosine, 1.0)
            left_t[pl.ds(at, 128)] = jnp.where(dim < ROT // 2, -sine, 0.0)
            right_t[pl.ds(at, 128)] = jnp.where((dim >= ROT // 2) & (dim < ROT), sine, 0.0)
            return 0

        lax.fori_loop(0, blocks, table, 0)
        own_at = pl.multiple_of(scal[2] * place.rows, place.rows)
        for k, ref in enumerate((cos_t, left_t, right_t)):
            own_t[k * place.rows : (k + 1) * place.rows] = ref[pl.ds(own_at, place.rows)]

    bias = jnp.concatenate([qkv_bias, jnp.zeros((8 - LAYERS, 3 * D), f32)], axis=0)
    made = call(
        kernel,
        [qkv_weight, bias, cosines, sines],
        [sds(qkv_weight.shape, bf16), sds((8, 3 * D), f32), *[sds((group, 128), f32)] * 3, sds((3 * place.rows, 128), f32)],
        (),
        lengths,
        flops=10**7,
    )
    return made[0], made[1], made[2:5], made[5]


def tie(x, *after):
    return lax.optimization_barrier((x, *after))[0] if after else x


def flip_heads(x, flip):
    return lax.ppermute(x, "head", [(i, i ^ flip) for i in range(lax.axis_size("head"))])


def turn_ctx(x, shift):
    n = lax.axis_size("ctx")
    return lax.ppermute(x, "ctx", [(i, (i + shift) % n) for i in range(n)])


def gather_rings(own):
    return [own] + [turn_ctx(own, s) for s in range(1, lax.axis_size("ctx"))]


def gather_flips(rings, flip, *after):
    return [flip_heads(tie(x, *after), flip) for x in rings]


def by_slot(rings, far, near, far_near):
    return [x for four in zip(rings, near, far, far_near) for x in four]


def with_flip(own, flip):
    return jnp.concatenate([own, flip_heads(own, flip)], axis=0)


def swap_dp(x):
    return lax.ppermute(x, "dp", [(0, 1), (1, 0)])


def per_device(
    hidden_in,
    lengths,
    attn_gain,
    attn_shift,
    mlp_gain,
    mlp_shift,
    qkv_weight,
    qkv_bias,
    out_weight,
    out_bias,
    up_weight,
    up_bias,
    down_weight,
    down_bias,
    cotangent,
):
    rows = hidden_in.shape[0]
    n_dp, n_ctx, n_head = (lax.axis_size(a) for a in ("dp", "ctx", "head"))
    place = Place(n_dp, n_ctx, n_head, rows)
    group = place.group
    scalars = lengths
    qkv_sorted, qkv_bias_sorted, tables, own_tables = prepare(place, lengths, qkv_weight, qkv_bias)
    params = {
        "attn_gain": attn_gain,
        "attn_shift": attn_shift,
        "mlp_gain": mlp_gain,
        "mlp_shift": mlp_shift,
        "qkv_sorted": qkv_sorted,
        "qkv_bias_sorted": qkv_bias_sorted,
        "out_weight": out_weight,
        "out_bias": out_bias,
        "up_weight": up_weight,
        "up_bias": up_bias,
        "down_weight": down_weight,
        "down_bias": down_bias,
    }
    def attention(layer, blocks, hidden, mlp_out, last_grad):
        names = ("normal_all", "k_all", "v_all", "q_own", "kv_own", "mixed", "mixed_low", "log", "delta", "dmix", "h_out", "stats", "low")
        made = attention_forward(place, scalars, blocks, tables, params, layer, hidden, mlp_out, last_grad)
        return dict(zip(names, made), hidden=hidden)

    def backward_queries(layer, kept):
        return query_backward(place, scalars, tables, own_tables, params, layer, kept)

    def backward_keys(layer, g_all, stats, kept, queries, grad, grad_mlp_in, below):
        return key_backward(
            place, scalars, g_all, stats, own_tables, params, layer, kept, queries, grad, grad_mlp_in, below
        )

    def head_swap(pieces):
        return lax.all_to_all(pieces, "head", 0, 0, tiled=True)

    def group_swap(pieces):
        return lax.all_to_all(pieces, ("ctx", "head"), 0, 0, tiled=True)

    def reduce_mlp(up_share, pieces, halves):
        made = pack_mlp(place, scalars, up_share, pieces, halves)
        if n_dp == 2:
            return (made[0].astype(f32) + swap_dp(made[-1]).astype(f32)).astype(bf16)
        return lax.psum(made[0], "dp")

    def sum_dp(x):
        if n_dp == 2:
            return (x.astype(f32) + swap_dp(x).astype(f32)).astype(bf16)
        return lax.psum(x, "dp")

    def finish(rings):
        return [*rings, swap_dp(jnp.concatenate(rings, axis=0))] if n_dp == 2 else rings

    together = lax.optimization_barrier

    mlp_0, factor_0, _ = mlp_forward(hidden_in, params, 0)
    rings, mlp_0, factor_0 = together((gather_rings(hidden_in), mlp_0, factor_0))
    far = gather_flips(rings, 2)
    far, rings, params["qkv_sorted"], tables, own_tables = together((far, rings, qkv_sorted, tables, own_tables))
    near, far_near = together((gather_flips(rings, 1), gather_flips(far, 1)))
    first, cot_rings = together(
        (attention(0, by_slot(rings, far, near, far_near), hidden_in, mlp_0, None), gather_rings(tie(cotangent, near)))
    )
    hidden, low = first["h_out"], first["low"]
    units = place.units
    at = lax.axis_index("head") * (FF // n_head) + lax.axis_index("ctx") * units
    params["units"] = [
        (
            lax.dynamic_slice(tie(up_weight, first["low"]), (layer, 0, at), (1, D, units))[0],
            lax.dynamic_slice(tie(up_bias, first["low"]), (layer, at), (1, units)),
            lax.dynamic_slice(tie(down_weight, first["low"]), (layer, at, 0), (1, units, D))[0],
        )
        for layer in range(LAYERS)
    ]
    mlp_1, back_1 = mlp_both(hidden, cotangent, params, 1)
    rings, mlp_1, back_1 = together((gather_rings(low), mlp_1, back_1))
    far, rings, params["units"] = together((gather_flips(rings, 2), rings, params["units"]))
    near, far_near = together((gather_flips(rings, 1), gather_flips(far, 1)))
    second = attention(1, by_slot(rings, far, near, far_near), hidden, mlp_1, [cotangent, first["mixed_low"]])
    second, cot_far, cot_rings = together((second, gather_flips(cot_rings, 2, near), cot_rings))
    output_rows, low = second["h_out"], second["low"]

    pair, cot_near, cot_far_near = together((with_flip(low, 1), gather_flips(cot_rings, 1), gather_flips(cot_far, 1)))
    made = mlp_weight_grads(
        place, scalars, by_slot(cot_rings, cot_far, cot_near, cot_far_near), second["normal_all"], params, 1
    )
    (cot_all, up_share_1, pieces_1), four = together((made, with_flip(pair, 2)))
    queries_1, stats = together((backward_queries(1, second), gather_rings(four)))
    made = backward_keys(1, cot_all, stats, second, queries_1, cotangent, back_1, first)
    packed_1, grad, payload, dmix, delta = made
    first["dmix"], first["delta"] = dmix, delta
    back_0 = mlp_backward(grad, factor_0, hidden_in, params, 0)
    rings, back_0, pieces_1 = together((gather_rings(payload), back_0, head_swap(tie(pieces_1, payload))))
    received_1 = group_swap(tie(packed_1, back_0))
    far, rings, queries_0 = together(
        (gather_flips(rings, 2), rings, backward_queries(0, dict(first, delta=tie(delta, back_0))))
    )
    half_1 = reduce_mlp(tie(up_share_1, far), pieces_1, n_dp == 2)
    near, far_near = together((gather_flips(rings, 1), gather_flips(far, 1)))
    blocks = by_slot(rings, far, near, far_near)
    mlp_rings_1 = gather_rings(tie(half_1, near))
    g_all, up_share_0, pieces_0 = mlp_weight_grads(
        place, scalars, blocks, first["normal_all"], params, 0, [received_1, cot_all]
    )
    made = backward_keys(0, g_all, blocks, first, queries_0, grad, back_0, None)
    (packed_0, grad, _, _, _), pieces_0, mlp_rings_1, up_share_0, received_1 = together(
        (made, head_swap(pieces_0), mlp_rings_1, up_share_0, received_1)
    )
    half_0 = reduce_mlp(up_share_0, pieces_0, n_dp == 2)
    mlp_rings_0 = gather_rings(half_0)
    share_1 = attention_weight_grads(place, scalars, tie(received_1, half_0), second["normal_all"], params, 1)
    sum_1 = sum_dp(share_1)
    received_0, sum_1, mlp_rings_0, mlp_shares_1 = together(
        (group_swap(packed_0), sum_1, mlp_rings_0, finish([tie(x, half_0) for x in mlp_rings_1]))
    )
    share_0 = attention_weight_grads(place, scalars, received_0, first["normal_all"], params, 0)
    *big, mlp_small_1 = place_mlp(place, scalars, [tie(mlp_shares_1[0], share_0), *mlp_shares_1[1:]], 1, None)
    other_0 = swap_dp(share_0) if n_dp == 2 else lax.psum(share_0, "dp")
    attn_rings_1 = gather_rings(tie(sum_1, share_0))
    mlp_shares_0 = finish([tie(x, other_0) for x in mlp_rings_0])
    other_0, attn_rings_1 = together((other_0, attn_rings_1))
    sum_0 = (share_0.astype(f32) + other_0.astype(f32)).astype(bf16) if n_dp == 2 else other_0
    sum_0, big, mlp_small_1 = together((sum_0, big, mlp_small_1))
    *attn_big, attn_small_1 = place_attention(place, scalars, attn_rings_1, 1, None)
    up_grad, down_grad, mlp_small_0, out_grad = place_mlp(place, scalars, mlp_shares_0, 0, big)
    attn_rings_0, mlp_small_0, attn_big, attn_small_1 = together(
        (gather_rings(sum_0), mlp_small_0, attn_big, attn_small_1)
    )
    qkv_grad, gain, shift, mlp_g, mlp_s, qkv_b, up_b, down_b, out_b, layer_stats = place_attention(
        place, scalars, attn_rings_0, 0, attn_big, [attn_small_1, mlp_small_0, mlp_small_1], group * n_dp * D
    )
    return (
        output_rows, grad, gain, shift, mlp_g, mlp_s, qkv_grad, qkv_b, out_grad, out_b, up_grad, up_b, down_grad, down_b, layer_stats
    )


def solution(mesh):
    rows = P(("dp", "ctx", "head"), None)
    return jax.shard_map(
        per_device,
        mesh=mesh,
        in_specs=(rows, P("dp", None), *([P()] * 12), rows),
        out_specs=(
            rows,
            rows,
            P(None, "head"),
            P(None, "head"),
            P(None, "head"),
            P(None, "head"),
            P(None, None, "head"),
            P(None, "head"),
            P(None, None, "head"),
            P(None, "head"),
            P(None, None, "head"),
            P(None, "head"),
            P(None, None, "head"),
            P(None, "head"),
            P(),
        ),
        check_vma=False,
    )
```

```python
import math

import jax
import jax.numpy as jnp
from jax import lax
from jax.experimental import pallas as pl
from jax.experimental.pallas import tpu as pltpu
from jax.sharding import PartitionSpec as P

D = 512
FF = 2048
NH = 8
HD = 64
ROT = 16
LAYERS = 2
PAIRS = NH // 2
epsilon = 1e-05
masked_value = -1e30
score_scale = 0.125
rope_base = 10000.0
f32 = jnp.float32
bf16 = jnp.bfloat16
STEP = 1024
VMEM = pltpu.VMEM


def dot(a, b):
    return lax.dot_general(a, b, (((1,), (0,)), ((), ())), preferred_element_type=f32)


def dot_nt(a, b):
    return lax.dot_general(a, b, (((1,), (1,)), ((), ())), preferred_element_type=f32)


def norm_parts(hidden):
    centred = hidden - jnp.mean(hidden, axis=-1, keepdims=True)
    inverse = lax.rsqrt(jnp.mean(centred * centred, axis=-1, keepdims=True) + epsilon)
    return centred * inverse, inverse


def rope(x, cos_t, left_t, right_t):
    return x * cos_t + pltpu.roll(x, 128 - 8, 1) * left_t + pltpu.roll(x, 8, 1) * right_t


def start_of(place, ends):
    start = jnp.zeros_like(place)
    for end in ends:
        start = jnp.where(end <= place, end, start)
    return start


def end_of(place, ends, size):
    found = jnp.int32(size)
    for end in reversed(ends):
        found = jnp.where(place < end, end, found)
    return found


def split_low(x):
    high = x.astype(bf16)
    return high, (x - high.astype(f32)).astype(bf16)


def lane_of(rows):
    return lax.broadcasted_iota(jnp.int32, (rows, 128), 1)


def two_heads(x):
    first = lane_of(x.shape[0]) < HD
    zero = jnp.zeros_like(x)
    return jnp.concatenate([jnp.where(first, x, zero), jnp.where(first, zero, x)], axis=0)


def one_pair(x):
    rows = x.shape[0] // 2
    return jnp.where(lane_of(rows) < HD, x[:rows], x[rows:])


def dot_tn(a, b):
    return lax.dot_general(a, b, (((0,), (0,)), ((), ())), preferred_element_type=f32)


def two_heads_t(x):
    first = lax.broadcasted_iota(jnp.int32, x.shape, 0) < HD
    zero = jnp.zeros_like(x)
    return jnp.concatenate([jnp.where(first, x, zero), jnp.where(first, zero, x)], axis=1)


def one_pair_t(x):
    rows = x.shape[1] // 2
    return jnp.where(lax.broadcasted_iota(jnp.int32, (128, rows), 0) < HD, x[:, :rows], x[:, rows:])


def rope_t(x, cos_t, left_t, right_t):
    return x * cos_t + pltpu.roll(x, 128 - 8, 0) * left_t + pltpu.roll(x, 8, 0) * right_t


class Far:
    def __init__(self, array):
        self.array = array


class Lazy:
    def __init__(self, array, at=None, shape=None):
        self.array, self.at = array, at or (lambda ref: ref)
        self.shape = shape or array.shape


class Out:
    def __init__(self, shape, dtype):
        self.shape, self.dtype = shape, dtype


class Coming:
    def __init__(self, ref, copy):
        self.ref, self.copy, self.there = ref, copy, False

    def get(self):
        if not self.there:
            self.copy.wait()
            self.there = True
        return self.ref


class Going:
    def __init__(self, ref, copy):
        self.ref, self.copy, self.gone = ref, copy, False

    def send(self):
        self.copy.start()
        self.gone = True


def call(kernel, ins, outs, scratch=(), scalars=None, vmem=60 << 20, flops=10**9, into=None):
    specs, arrays = [], []

    def block(shape, layer, cols=None):
        place = (layer, *([0] * (len(shape) - 1)))
        return pl.BlockSpec((None, *shape[1:-1], cols or shape[-1]), lambda i: place)

    def whole(shape):
        return pl.BlockSpec(shape, lambda i: (0,) * len(shape))

    n_ins, n_outs = len(ins), len(outs)
    lead = 0
    if scalars is not None:
        specs.append(pl.BlockSpec(memory_space=pltpu.SMEM))
        arrays.append(scalars)
        lead = 1
    for item in ins:
        if isinstance(item, (Far, Lazy)):
            specs.append(pl.BlockSpec(memory_space=pl.ANY))
            arrays.append(item.array)
            continue
        array = item[0] if isinstance(item, tuple) else item
        specs.append(block(array.shape, *item[1:]) if isinstance(item, tuple) else whole(array.shape))
        arrays.append(array)
    aliases = {}
    if into is not None:
        spots = [k for k, o in enumerate(outs) if isinstance(o, tuple)]
        for spot, array in zip(spots, into):
            aliases[len(arrays)] = spot
            specs.append(pl.BlockSpec(memory_space=pl.ANY))
            arrays.append(array)
    shapes, out_specs = [], []
    for o in outs:
        if isinstance(o, tuple):
            shapes.append(o[0])
            out_specs.append(block(o[0].shape, o[1]))
        elif isinstance(o, Out):
            shapes.append(sds(o.shape, o.dtype))
            out_specs.append(pl.BlockSpec(memory_space=pl.ANY))
        else:
            shapes.append(o)
            out_specs.append(whole(o.shape))
    coming = [k for k, item in enumerate(ins) if isinstance(item, Lazy)]
    going = [k for k, o in enumerate(outs) if isinstance(o, Out)]
    slow = [VMEM(ins[k].shape, ins[k].array.dtype) for k in coming] + [VMEM(outs[k].shape, outs[k].dtype) for k in going]
    if slow:
        slow.append(pltpu.SemaphoreType.DMA((len(slow),)))

    def body(*refs):
        refs = list(refs)
        given = []
        if scalars is not None:
            lengths_ref = refs.pop(0)
            ctx, head = lax.axis_index("ctx"), lax.axis_index("head")
            ends = [lengths_ref[0, 0]]
            for k in range(1, 4):
                ends.append(ends[-1] + lengths_ref[0, k])
            given = [[ctx, head, ctx * lax.axis_size("head") + head, *ends, lax.axis_index("dp")]]
        finals = []
        if slow:
            extra = refs[len(refs) - len(slow) :]
            refs = refs[: len(refs) - len(slow)]
            sems = extra[-1]
            for j, k in enumerate(coming):
                copy = pltpu.make_async_copy(ins[k].at(refs[k]), extra[j], sems.at[j])
                copy.start()
                refs[k] = Coming(extra[j], copy)
            first_out = len(arrays) - lead
            for j, k in enumerate(going):
                j += len(coming)
                refs[first_out + k] = Going(extra[j], pltpu.make_async_copy(extra[j], refs[first_out + k], sems.at[j]))
                finals.append(refs[first_out + k])
        kernel(*given, *refs)
        for item in finals:
            if not item.gone:
                item.send()
        for item in finals:
            item.copy.wait()

    moved = sum(x.size * x.dtype.itemsize for x in arrays)
    return pl.pallas_call(
        body,
        grid=(1,),
        in_specs=specs,
        out_specs=out_specs,
        out_shape=shapes,
        scratch_shapes=[*scratch, *slow],
        input_output_aliases=aliases,
        compiler_params=pltpu.CompilerParams(vmem_limit_bytes=vmem),
        cost_estimate=pl.CostEstimate(flops=flops, bytes_accessed=moved, transcendentals=0),
    )(*arrays)


def lazy_layer(array, layer, cols=None):
    if cols is None:
        return Lazy(array, lambda ref: ref.at[layer], array.shape[1:])
    return Lazy(array, lambda ref: ref.at[layer, :, 0:cols], (*array.shape[1:-1], cols))


def sds(shape, dtype):
    return jax.ShapeDtypeStruct(shape, dtype)


def mlp_forward(hidden, params, layer):
    rows = hidden.shape[0]

    def kernel(h_ref, gain, shift, up, up_b, down, down_b, out_ref, factor_ref, normal_ref):
        normal, _ = norm_parts(h_ref[...].astype(f32))
        normal_ref[...] = normal.astype(bf16)
        x = (normal * gain[layer : layer + 1] + shift[layer : layer + 1]).astype(bf16)
        total = jnp.zeros((rows, D), f32)
        for j in range(0, FF, 1024):
            gate = dot(x, up[:, j : j + 1024]) + up_b[layer : layer + 1, j : j + 1024]
            cdf = 0.5 * (1.0 + lax.erf(gate * math.sqrt(0.5)))
            pdf = jnp.exp(-0.5 * gate * gate) * (1.0 / math.sqrt(2.0 * math.pi))
            factor_ref[:, j : j + 1024] = cdf + gate * pdf
            total += dot((gate * cdf).astype(bf16), down[j : j + 1024])
        out_ref[...] = total + down_b[layer : layer + 1]

    return call(
        kernel,
        [
            hidden,
            params["mlp_gain"],
            params["mlp_shift"],
            (params["up_weight"], layer),
            params["up_bias"],
            (params["down_weight"], layer),
            params["down_bias"],
        ],
        [sds((rows, D), f32), sds((rows, FF), f32), sds((rows, D), bf16)],
        flops=2 * 2 * rows * D * FF,
    )


def mlp_both(hidden, grad, params, layer):
    rows = hidden.shape[0]

    def kernel(h_ref, g_ref, gain, shift, up, up_b, down, down_b, out_ref, back_ref):
        normal, _ = norm_parts(h_ref[...].astype(f32))
        x = (normal * gain[layer : layer + 1] + shift[layer : layer + 1]).astype(bf16)
        g_low = g_ref[...].astype(bf16)
        total = jnp.zeros((rows, D), f32)
        back = jnp.zeros((rows, D), f32)
        for j in range(0, FF, 1024):
            gate = dot(x, up[:, j : j + 1024]) + up_b[layer : layer + 1, j : j + 1024]
            cdf = 0.5 * (1.0 + lax.erf(gate * math.sqrt(0.5)))
            pdf = jnp.exp(-0.5 * gate * gate) * (1.0 / math.sqrt(2.0 * math.pi))
            total += dot((gate * cdf).astype(bf16), down[j : j + 1024])
            grad_gate = (dot_nt(g_low, down[j : j + 1024]) * (cdf + gate * pdf)).astype(bf16)
            back += dot_nt(grad_gate, up[:, j : j + 1024])
        out_ref[...] = total + down_b[layer : layer + 1]
        back_ref[...] = back

    return call(
        kernel,
        [
            hidden,
            grad,
            params["mlp_gain"],
            params["mlp_shift"],
            (params["up_weight"], layer),
            params["up_bias"],
            (params["down_weight"], layer),
            params["down_bias"],
        ],
        [sds((rows, D), f32), sds((rows, D), f32)],
    )


class Place:
    def __init__(self, n_dp, n_ctx, n_head, rows):
        self.n_ctx, self.n_head, self.rows = n_ctx, n_head, rows
        self.halves = n_dp == 2
        self.blocks = n_ctx * n_head
        self.group = self.blocks * rows
        self.units = FF // self.blocks
        self.packed_rows = 3 * D // self.blocks
        self.mixed_rows = D // self.blocks

    def position(self, scal, slot):
        shift, flip = slot // self.n_head, slot % self.n_head
        ctx = lax.rem(scal[0] - shift + self.n_ctx, self.n_ctx)
        return ctx * self.n_head + (scal[1] ^ flip)

    def ends(self, scal):
        return [scal[3 + k] for k in range(4)]


def delta_rows(grad_mixed_t, mixed_t):
    return jnp.concatenate(
        [
            jnp.sum(grad_mixed_t[n * HD : (n + 1) * HD].astype(f32) * mixed_t[n * HD : (n + 1) * HD], axis=0, keepdims=True)
            for n in range(NH)
        ],
        axis=0,
    )


def stat_payload(logs, deltas):
    parts = [*split_low(logs), *split_low(deltas)]
    top = jnp.concatenate(parts, axis=1)
    return jnp.concatenate([top, jnp.zeros_like(top)], axis=0)


def attention_forward(place, scalars, blocks, tables, params, layer, hidden, mlp_out, last_grad):
    rows, group = place.rows, place.group
    first_layer = layer == 0
    last = last_grad is not None
    tile = min(1024, group)

    def kernel(scal, *refs):
        refs = list(refs)
        xs = [refs.pop(0) for _ in range(place.blocks)]
        cos_t, left_t, right_t, gain, shift, w, b, out_w, out_b, h_ref, mlp_ref = refs[:11]
        refs = refs[11:]
        g_ref, below_ref = (refs.pop(0), refs.pop(0)) if last else (None, None)
        (normal_out, k_out, v_out, q_own, kv_own, mixed_ref, mixed_low_ref, log_ref, delta_ref, dmix_ref, h_out, stats_ref, low_ref) = refs[:13]
        a_all = refs[13]
        normal_all, k_all, v_all = normal_out.ref, k_out.ref, v_out.ref
        own_at = pl.multiple_of(scal[2] * rows, rows)
        ends = place.ends(scal)
        gain_l, shift_l = gain[layer : layer + 1], shift[layer : layer + 1]
        for slot in range(place.blocks):
            at = pl.multiple_of(place.position(scal, slot) * rows, rows)
            x = xs[slot][...].astype(f32)
            normal = norm_parts(x)[0] if first_layer else x
            normal_all[pl.ds(at, rows)] = normal.astype(bf16)
            a_all[pl.ds(at, rows)] = (normal * gain_l + shift_l).astype(bf16)
        normal_out.send()
        w, cos_t, left_t, right_t = (x.get() for x in (w, cos_t, left_t, right_t))

        def project(i, _):
            at = pl.multiple_of(i * tile, tile)
            k = dot(a_all[pl.ds(at, tile)], w[:, D : 2 * D]) + b[layer : layer + 1, D : 2 * D]
            tabs = [t[pl.ds(at, tile)] for t in (cos_t, left_t, right_t)]
            for p in range(PAIRS):
                k_all[pl.ds(at, tile), 128 * p : 128 * p + 128] = rope(k[:, 128 * p : 128 * p + 128], *tabs).astype(bf16)
            v = dot(a_all[pl.ds(at, tile)], w[:, 2 * D :]) + b[layer : layer + 1, 2 * D :]
            v_all[pl.ds(at, tile)] = v.astype(bf16)
            return 0

        first_key = start_of(own_at, ends)
        low, high = first_key // STEP, (own_at + rows - 1) // STEP + 1
        lax.fori_loop(low * (STEP // tile), high * (STEP // tile), project, 0)
        k_out.send()
        v_out.send()
        kv_own[0:rows], kv_own[rows : 2 * rows] = k_all[pl.ds(own_at, rows)], v_all[pl.ds(own_at, rows)]
        q = dot(a_all[pl.ds(own_at, rows)], w[:, :D]) + b[layer : layer + 1, :D]
        tabs = [t[pl.ds(own_at, rows)] for t in (cos_t, left_t, right_t)]
        for p in range(PAIRS):
            turned = rope(q[:, 128 * p : 128 * p + 128], *tabs).astype(bf16)
            q_own[:, 128 * p : 128 * p + 128] = turned * jnp.asarray(score_scale, bf16)
        t = own_at + lax.broadcasted_iota(jnp.int32, (1, rows), 1)
        start = start_of(t, ends)
        doubled = [two_heads(q_own[:, 128 * p : 128 * p + 128]) for p in range(PAIRS)]

        def attend(i, carry):
            at = pl.multiple_of(i * STEP, STEP)
            s_at = at + lax.broadcasted_iota(jnp.int32, (STEP, 1), 0)
            bias = jnp.where((s_at >= start) & (s_at <= t), 0.0, masked_value)
            bias = jnp.concatenate([bias, bias], axis=1)
            new = []
            for p in range(PAIRS):
                most, total, acc = carry[p]
                scores = dot_nt(k_all[pl.ds(at, STEP), 128 * p : 128 * p + 128], doubled[p]) + bias
                newest = jnp.maximum(most, jnp.max(scores, axis=0, keepdims=True))
                chance = jnp.exp(scores - newest)
                scale = jnp.exp(most - newest)
                total = total * scale + jnp.sum(chance, axis=0, keepdims=True)
                acc = acc * scale + dot_tn(v_all[pl.ds(at, STEP), 128 * p : 128 * p + 128], chance.astype(bf16))
                new.append((newest, total, acc))
            return tuple(new)

        begin = tuple(
            (jnp.full((1, 2 * rows), masked_value, f32), jnp.zeros((1, 2 * rows), f32), jnp.zeros((128, 2 * rows), f32))
            for _ in range(PAIRS)
        )
        done = lax.fori_loop(low, high, attend, begin)
        logs = []
        for p in range(PAIRS):
            most, total, acc = done[p]
            mixed_ref[128 * p : 128 * p + 128] = one_pair_t(acc / total)
            log = most + jnp.log(total)
            logs += [log[:, :rows], log[:, rows:]]
        log_rows = jnp.concatenate(logs, axis=0)
        log_ref[...] = log_rows
        mixed_low = mixed_ref[...].astype(bf16)
        if last:
            size = place.mixed_rows
            for p in range(place.n_head):
                for c in range(place.n_ctx):
                    at = 128 * p + size * c
                    mixed_low_ref[c * place.n_head + p, 0:size] = below_ref[at : at + size]
                    mixed_low_ref[c * place.n_head + p, size : 2 * size] = mixed_low[at : at + size]
        else:
            mixed_low_ref[...] = mixed_low
        out_w = out_w.get()
        attn_out = dot_tn(mixed_low, out_w[...]) + out_b[layer : layer + 1]
        h = h_ref.get()[...].astype(f32)
        mlp = mlp_ref.get()[...]
        result = h + attn_out + mlp
        lane = lane_of(8)
        sums = [jnp.sum(jnp.sum(v * v, axis=1, keepdims=True), axis=0, keepdims=True) for v in (h, attn_out, mlp)]
        stats_ref[...] = jnp.where(lane == 0, sums[0], jnp.where(lane == 1, sums[1], jnp.where(lane == 2, sums[2], 0.0)))
        if last:
            h_out[...] = result.astype(bf16)
            dmix = dot_nt(out_w[...], g_ref[...]).astype(bf16)
            dmix_ref[...] = dmix
            deltas = delta_rows(dmix, mixed_ref[...])
            delta_ref[...] = deltas
            low_ref[...] = stat_payload(log_rows, deltas)
        else:
            h_out[...] = result
            low_ref[...] = norm_parts(result)[0].astype(bf16)
            dmix_ref[...] = jnp.zeros_like(dmix_ref)
            delta_ref[...] = jnp.zeros_like(delta_ref)

    ins = [
        *blocks,
        *[Lazy(x) for x in tables],
        params["attn_gain"],
        params["attn_shift"],
        lazy_layer(params["qkv_sorted"], layer),
        params["qkv_bias_sorted"],
        lazy_layer(params["out_weight"], layer),
        params["out_bias"],
        Lazy(hidden),
        Lazy(mlp_out),
    ]
    if last:
        ins += last_grad
    outs = [
        Out((group, D), bf16),
        Out((group, D), bf16),
        Out((group, D), bf16),
        sds((rows, D), bf16),
        sds((2 * rows, D), bf16),
        sds((D, rows), f32),
        sds((place.blocks, 2 * place.mixed_rows, rows) if last else (D, rows), bf16),
        sds((NH, rows), f32),
        sds((NH, rows), f32),
        sds((D, rows), bf16),
        sds((rows, D), bf16 if last else f32),
        sds((8, 128), f32),
        sds((16, D) if last else (rows, D), bf16),
    ]
    return call(kernel, ins, outs, [VMEM((group, D), bf16)], scalars, flops=60 * 10**9)


def mlp_backward(grad, factor, hidden, params, layer):
    rows = grad.shape[0]

    def kernel(g_ref, factor_ref, down, up, out_ref):
        g_low = g_ref[...].astype(bf16)
        total = jnp.zeros((rows, D), f32)
        for j in range(0, FF, 1024):
            grad_gate = (dot_nt(g_low, down[j : j + 1024]) * factor_ref[:, j : j + 1024]).astype(bf16)
            total += dot_nt(grad_gate, up[:, j : j + 1024])
        out_ref[...] = total

    return call(
        kernel,
        [grad, factor, (params["down_weight"], layer), (params["up_weight"], layer)],
        [sds((rows, D), f32)],
        flops=2 * 2 * rows * D * FF,
    )[0]


def query_backward(place, scalars, tables, own_tables, params, layer, kept):
    rows, group = place.rows, place.group
    tile = min(1024, group)

    def kernel(scal, cos_t, left_t, right_t, own_tabs, gain, shift, w, b, normal_all, k_all, v_all, q_own, dmix_ref, log_ref, delta_ref, q_out, grad_ref, grad_t_ref):
        q_all = q_out.ref
        own_at = pl.multiple_of(scal[2] * rows, rows)
        ends = place.ends(scal)
        gain_l, shift_l = gain[layer : layer + 1], shift[layer : layer + 1]

        def project(i, _):
            at = pl.multiple_of(i * tile, tile)
            a = (normal_all[pl.ds(at, tile)].astype(f32) * gain_l + shift_l).astype(bf16)
            q = dot(a, w[...]) + b[layer : layer + 1, :D]
            tabs = [t[pl.ds(at, tile)] for t in (cos_t, left_t, right_t)]
            for p in range(PAIRS):
                turned = rope(q[:, 128 * p : 128 * p + 128], *tabs).astype(bf16)
                q_all[pl.ds(at, tile), 128 * p : 128 * p + 128] = turned * jnp.asarray(score_scale, bf16)
            return 0

        last_end = end_of(own_at + rows - 1, ends, group)
        low, high = own_at // STEP, (last_end + STEP - 1) // STEP
        lax.fori_loop(low * (STEP // tile), high * (STEP // tile), project, 0)
        q_out.send()
        k_all, v_all = k_all.get(), v_all.get()
        t = own_at + lax.broadcasted_iota(jnp.int32, (1, rows), 1)
        start = start_of(t, ends)
        q2 = [two_heads(q_own[:, 128 * p : 128 * p + 128]) for p in range(PAIRS)]
        d2 = [two_heads_t(dmix_ref[128 * p : 128 * p + 128]) for p in range(PAIRS)]
        log2 = [jnp.concatenate([log_ref[2 * p : 2 * p + 1], log_ref[2 * p + 1 : 2 * p + 2]], axis=1) for p in range(PAIRS)]
        delta2 = [
            jnp.concatenate([delta_ref[2 * p : 2 * p + 1], delta_ref[2 * p + 1 : 2 * p + 2]], axis=1) for p in range(PAIRS)
        ]

        def queries(i, carry):
            at = pl.multiple_of(i * STEP, STEP)
            s = at + lax.broadcasted_iota(jnp.int32, (STEP, 1), 0)
            bias = jnp.where((s >= start) & (s <= t), 0.0, masked_value)
            bias = jnp.concatenate([bias, bias], axis=1)
            new = []
            for p in range(PAIRS):
                ks = k_all[pl.ds(at, STEP), 128 * p : 128 * p + 128]
                vs = v_all[pl.ds(at, STEP), 128 * p : 128 * p + 128]
                chance = jnp.exp(dot_nt(ks, q2[p]) + bias - log2[p])
                grad_s = (chance * (dot(vs, d2[p]) - delta2[p])).astype(bf16)
                new.append(carry[p] + dot_tn(ks, grad_s))
            return tuple(new)

        zero = jnp.zeros((128, 2 * rows), f32)
        done = lax.fori_loop(
            start_of(own_at, ends) // STEP, (own_at + rows - 1) // STEP + 1, queries, tuple(zero for _ in range(PAIRS))
        )
        tabs = [own_tabs[0:rows].T, -own_tabs[rows : 2 * rows].T, -own_tabs[2 * rows : 3 * rows].T]
        for p in range(PAIRS):
            grad_t = rope_t(one_pair_t(done[p]) * score_scale, *tabs)
            grad_t_ref[128 * p : 128 * p + 128] = grad_t.astype(bf16)
            grad_ref[:, 128 * p : 128 * p + 128] = grad_t.T.astype(bf16)

    return call(
        kernel,
        [
            *tables,
            own_tables,
            params["attn_gain"],
            params["attn_shift"],
            (params["qkv_sorted"], layer, D),
            params["qkv_bias_sorted"],
            kept["normal_all"],
            Lazy(kept["k_all"]),
            Lazy(kept["v_all"]),
            kept["q_own"],
            kept["dmix"],
            kept["log"],
            kept["delta"],
        ],
        [Out((group, D), bf16), sds((rows, D), bf16), sds((D, rows), bf16)],
        (),
        scalars,
        flops=30 * 10**9,
    )


def key_backward(place, scalars, g_whole, stats, own_tables, params, layer, kept, queries, grad, grad_mlp_in, mixed_below):
    rows, group = place.rows, place.group
    below = layer > 0
    n_stats = len(stats)
    tile = min(1024, group)
    part = place.packed_rows

    def kernel(scal, *refs):
        refs = list(refs)
        ss = [refs.pop(0) for _ in range(n_stats)]
        (g_all, own_tabs, gain, mlp_gain, w, out_w, q_all, gq_ref, gq_t_ref, kv_own, h_ref, g_ref, gmlp_ref, stats_ref) = refs[:14]
        refs = refs[14:]
        if below:
            below_mixed, below_log, below_w, carried = refs[:4]
            refs = refs[4:]
        pieces_out, g_out, payload_ref, dmix_out, delta_out = refs[:5]
        dm_all, log_all, delta_all, packed_t = refs[5:]
        own_at = pl.multiple_of(scal[2] * rows, rows)
        ends = place.ends(scal)
        gain_l = gain[layer : layer + 1]
        for slot in range(place.blocks):
            at = pl.multiple_of(place.position(scal, slot) * rows, rows)
            if below:
                flip = slot % place.n_head
                info = ss[slot // place.n_head][16 * flip : 16 * flip + 16].astype(f32)[:NH]
            else:
                info = ss[slot][rows : rows + 16].astype(f32)[:NH]
            log_all[:, pl.ds(at, rows)] = info[:, 0:128] + info[:, 128:256]
            delta_all[:, pl.ds(at, rows)] = info[:, 256:384] + info[:, 384:512]
        last_end = end_of(own_at + rows - 1, ends, group)

        def project(i, _):
            at = pl.multiple_of(i * tile, tile)
            dm_all[pl.ds(at, tile)] = dot_nt(g_all[pl.ds(at, tile)], out_w[...]).astype(bf16)
            return 0

        low, high = own_at // STEP, (last_end + STEP - 1) // STEP
        lax.fori_loop(low * (STEP // tile), high * (STEP // tile), project, 0)
        q_all = q_all.get()
        s_at = own_at + lax.broadcasted_iota(jnp.int32, (rows, 1), 0)
        k2 = [two_heads(kv_own[0:rows, 128 * p : 128 * p + 128]) for p in range(PAIRS)]
        v2 = [two_heads(kv_own[rows : 2 * rows, 128 * p : 128 * p + 128]) for p in range(PAIRS)]

        def keys(i, carry):
            at = pl.multiple_of(i * STEP, STEP)
            t = at + lax.broadcasted_iota(jnp.int32, (1, STEP), 1)
            start = start_of(t, ends)
            bias = jnp.where((s_at >= start) & (s_at <= t), 0.0, masked_value)
            new = []
            for p in range(PAIRS):
                dk, dv = carry[p]
                qs = q_all[pl.ds(at, STEP), 128 * p : 128 * p + 128]
                dms = dm_all[pl.ds(at, STEP), 128 * p : 128 * p + 128]
                scores = dot_nt(k2[p], qs)
                pulled = dot_nt(v2[p], dms)
                chances, grads = [], []
                for half in range(2):
                    n = 2 * p + half
                    part = slice(half * rows, half * rows + rows)
                    chance = jnp.exp(scores[part] + bias - log_all[n : n + 1, pl.ds(at, STEP)])
                    grads.append(chance * (pulled[part] - delta_all[n : n + 1, pl.ds(at, STEP)]))
                    chances.append(chance)
                chance = jnp.concatenate(chances, axis=0).astype(bf16)
                grad_s = jnp.concatenate(grads, axis=0).astype(bf16)
                new.append((dk + dot(grad_s, qs), dv + dot(chance, dms)))
            return tuple(new)

        zero = jnp.zeros((2 * rows, 128), f32)
        done = lax.fori_loop(low, high, keys, tuple((zero, zero) for _ in range(PAIRS)))
        tabs = [own_tabs[0:rows], -own_tabs[rows : 2 * rows], -own_tabs[2 * rows : 3 * rows]]
        grad_k = [rope(one_pair(done[p][0]), *tabs).astype(bf16) for p in range(PAIRS)]
        grad_v = [one_pair(done[p][1]).astype(bf16) for p in range(PAIRS)]
        w = w.get()
        grad_in = dot_nt(gq_ref.get()[...], w[:, 0:D])
        for j, parts in ((1, grad_k), (2, grad_v)):
            grad_in += dot_nt(jnp.concatenate(parts, axis=1), w[:, j * D : j * D + D])

        normal, inverse = norm_parts(h_ref.get()[...].astype(f32))
        grad_mlp = gmlp_ref.get()[...]
        grad_normal = grad_in * gain_l + grad_mlp * mlp_gain[layer : layer + 1]
        back = inverse * (
            grad_normal
            - jnp.mean(grad_normal, axis=-1, keepdims=True)
            - normal * jnp.mean(grad_normal * normal, axis=-1, keepdims=True)
        )
        g_new = g_ref.get()[...].astype(f32) + back
        g_out[...] = g_new

        sums = [
            jnp.sum(v, axis=0, keepdims=True)
            for v in (grad_in * normal, grad_in, grad_mlp * normal, grad_mlp)
        ]
        for j in range(3):
            for p in range(PAIRS):
                if j == 0:
                    turned = gq_t_ref.get()[128 * p : 128 * p + 128]
                else:
                    turned = (grad_k, grad_v)[j - 1][p].astype(f32).T.astype(bf16)
                for half in range(2):
                    at = (2 * p + half) * 3 * HD + j * HD
                    packed_t[at : at + HD] = turned[half * HD : half * HD + HD]
        layer_sums = jnp.where(lane_of(8) < 4, stats_ref[...], 0.0)
        layer_sums = jnp.broadcast_to(pltpu.roll(layer_sums, scal[2] * 4, 1)[0:1], (16, 128))
        row16 = lax.broadcasted_iota(jnp.int32, (16, 128), 0)
        for p in range(place.n_head):
            extra = jnp.concatenate([x[:, 128 * p : 128 * p + 128] for x in sums] + [jnp.zeros((4, 128), f32)], axis=0)
            extra = jnp.concatenate([extra, extra], axis=0)
            extra = jnp.where((row16 & 7) == 4, layer_sums, extra)
            high, rest = split_low(extra)
            extra = jnp.where(row16 < 8, high, rest)
            for c in range(place.n_ctx):
                at = (p * place.n_ctx + c) * part
                pieces_out[c * place.n_head + p, 0:part] = packed_t[at : at + part]
                pieces_out[c * place.n_head + p, part : part + 16] = extra
        if below:
            pieces_out[:, part + 16 :] = carried[...]

        g_low = g_new.astype(bf16)
        if below:
            payload_ref[0:rows] = g_low
            dmix = dot_nt(below_w.get()[...], g_low).astype(bf16)
            dmix_out[...] = dmix
            deltas = delta_rows(dmix, below_mixed.get()[...])
            delta_out[...] = deltas
            payload_ref[rows : rows + 16] = stat_payload(below_log[...], deltas)
        else:
            payload_ref[...] = jnp.zeros_like(payload_ref)
            dmix_out[...] = jnp.zeros_like(dmix_out)
            delta_out[...] = jnp.zeros_like(delta_out)

    ins = [
        *stats,
        g_whole,
        own_tables,
        params["attn_gain"],
        params["mlp_gain"],
        lazy_layer(params["qkv_sorted"], layer),
        (params["out_weight"], layer),
        *[Lazy(x) for x in queries],
        kept["kv_own"],
        Lazy(kept["hidden"]),
        Lazy(grad),
        Lazy(grad_mlp_in),
        kept["stats"],
    ]
    if below:
        ins += [Lazy(mixed_below["mixed"]), mixed_below["log"], lazy_layer(params["out_weight"], layer - 1)]
        ins.append(kept["mixed_low"])
    outs = [
        sds((place.blocks, part + 16 + (2 * place.mixed_rows if below else 0), rows), bf16),
        sds((rows, D), f32),
        sds((rows + 16, D) if below else (16, D), bf16),
        sds((D, rows) if below else (16, rows), bf16),
        sds((NH, rows), f32),
    ]
    scratch = [VMEM((group, D), bf16), VMEM((NH, group), f32), VMEM((NH, group), f32), VMEM((3 * D, rows), bf16)]
    return call(kernel, ins, outs, scratch, scalars, flops=60 * 10**9)


def mlp_weight_grads(place, scalars, blocks, normal_all, params, layer, mixed=None):
    group, rows, units = place.group, place.rows, place.units
    tile = min(2048, group)
    size = 0 if mixed is None else place.mixed_rows

    def kernel(scal, *refs):
        gs = refs[: place.blocks]
        refs = list(refs[place.blocks :])
        mixed_ref, other_ref = (refs.pop(0), refs.pop(0)) if size else (None, None)
        normal_ref, gain, shift, up, up_b, down, g_out, up_out, down_out = refs[:9]
        g_ref = g_out.ref
        mixed_t = refs[9] if size else None
        gain_l, shift_l = gain[layer : layer + 1], shift[layer : layer + 1]
        for slot in range(place.blocks):
            at = pl.multiple_of(place.position(scal, slot) * rows, rows)
            g_ref[pl.ds(at, rows)] = gs[slot][0:rows]
            if size:
                mixed_t[:, slot * rows : (slot + 1) * rows] = mixed_ref[slot, place.packed_rows + 16 :]

        g_out.send()

        def step(i, carry):
            up_t, down_g, bias, g_sum = carry
            at = pl.multiple_of(i * tile, tile)
            x = (normal_ref[pl.ds(at, tile)].astype(f32) * gain_l + shift_l).astype(bf16)
            g = g_ref[pl.ds(at, tile)]
            gate = dot(x, up[...]) + up_b[...]
            cdf = 0.5 * (1.0 + lax.erf(gate * math.sqrt(0.5)))
            pdf = jnp.exp(-0.5 * gate * gate) * (1.0 / math.sqrt(2.0 * math.pi))
            acted = (gate * cdf).astype(bf16)
            grad_gate = (dot_nt(g, down[...]) * (cdf + gate * pdf)).astype(bf16)
            up_t += dot(grad_gate.T, x)
            down_g += dot(acted.T, g)
            bias += jnp.sum(grad_gate.astype(f32), axis=0, keepdims=True)
            g_sum += jnp.sum(g.astype(f32), axis=0, keepdims=True)
            return up_t, down_g, bias, g_sum

        zero = jnp.zeros((units, D), f32)
        up_t, down_g, bias, g_sum = lax.fori_loop(
            0, group // tile, step, (zero, zero, jnp.zeros((1, units), f32), jnp.zeros((1, D), f32))
        )
        up_out[0:units] = up_t.astype(bf16)
        if units < 128:
            bias = jnp.concatenate([bias, jnp.zeros((1, 128 - units), f32)], axis=1)
        wide = jnp.concatenate([bias, jnp.zeros((1, D - 128), f32)], axis=1)
        row = lax.broadcasted_iota(jnp.int32, (32, D), 0)
        extra = jnp.where((row & 7) == 0, wide, jnp.where((row & 7) == 1, g_sum, 0.0))
        high, rest = split_low(extra)
        up_out[units : units + 32] = jnp.where(row < 8, high, jnp.where(row < 16, rest, jnp.zeros_like(rest)))
        if size:
            out_g = [dot(mixed_t[k * size : (k + 1) * size], g[...]) for k, g in enumerate((g_ref, other_ref))]
        for p in range(place.n_head):
            cols = slice(128 * p, 128 * p + 128)
            down_out[p, 0:units] = down_g[:, cols].astype(bf16)
            for k in range(2 if size else 0):
                down_out[p, units + k * size : units + (k + 1) * size] = out_g[k][:, cols].astype(bf16)

    up, up_b, down = params["units"][layer]
    made = call(
        kernel,
        [*blocks, *([] if mixed is None else mixed), normal_all, params["mlp_gain"], params["mlp_shift"], up, up_b, down],
        [Out((group, D), bf16), sds((units + 32, D), bf16), sds((place.n_head, units + 2 * size, 128), bf16)],
        [VMEM((2 * size, group), bf16)] if size else [],
        scalars,
        flops=4 * 2 * group * D * units,
    )
    return made


def attention_weight_grads(place, scalars, received, normal_all, params, layer):
    group, rows, part = place.group, place.rows, place.packed_rows
    tile = min(2048, group)

    def kernel(received_ref, normal_ref, gain, shift, out_ref, chunk_t):
        gain_l, shift_l = gain[layer : layer + 1], shift[layer : layer + 1]
        extra = jnp.zeros((16, 128), f32)
        for j in range(place.blocks):
            chunk_t[:, j * rows : (j + 1) * rows] = received_ref[j, 0:part]
            extra += received_ref[j, part : part + 16].astype(f32)
        total = jnp.zeros((part, D), f32)
        for at in range(0, group, tile):
            x = (normal_ref[at : at + tile].astype(f32) * gain_l + shift_l).astype(bf16)
            total += dot(chunk_t[:, at : at + tile], x)
        out_ref[0:part] = total.astype(bf16)
        bias = dot_nt(jnp.ones((16, group), bf16), chunk_t[...])
        bias = jnp.concatenate([bias, jnp.zeros((16, 128 - part), f32)], axis=1)
        extra = extra[0:8] + extra[8:16]
        wide = jnp.concatenate([extra[k : k + 1] for k in range(4)], axis=1)
        none = jnp.zeros((1, D - 256), f32)
        second = jnp.concatenate([bias[0:1], extra[4:5], none], axis=1)
        row = lax.broadcasted_iota(jnp.int32, (16, D), 0)
        high, rest = split_low(jnp.where((row & 7) == 0, wide, jnp.where((row & 7) == 1, second, 0.0)))
        out_ref[part : part + 16] = jnp.where(row < 8, high, rest)

    return call(
        kernel,
        [received, normal_all, params["attn_gain"], params["attn_shift"]],
        [sds((part + 16, D), bf16)],
        [VMEM((part, group), bf16)],
        flops=2 * group * D * part,
    )[0]


def pack_mlp(place, scalars, up_share, pieces, halves):
    rows = place.units + 32 + pieces.shape[1]
    half = rows // 2

    def kernel(scal, up_ref, pieces_ref, *refs):
        if halves:
            mine, other, full = refs
        else:
            (full,) = refs
        full[0 : place.units + 32] = up_ref[...]
        for p in range(place.n_head):
            full[place.units + 32 :, 128 * p : 128 * p + 128] = pieces_ref[p]
        if halves:
            at = pl.multiple_of(scal[7] * half, half)
            mine[...] = full[pl.ds(at, half)]
            other[...] = full[pl.ds(pl.multiple_of(half - at, half), half)]

    outs = [sds((half, D), bf16)] * 2 if halves else [sds((rows, D), bf16)]
    scratch = [VMEM((rows, D), bf16)] if halves else []
    return call(kernel, [up_share, pieces], outs, scratch, scalars, flops=10**7)


def along_lanes(rows, width):
    if width == 128:
        return jnp.concatenate(rows, axis=1)
    full = len(rows) * width
    out = jnp.zeros((8, full), f32)
    for k, row in enumerate(rows):
        lane = lax.broadcasted_iota(jnp.int32, (8, full), 1)
        row = jnp.concatenate([row, jnp.zeros((1, full - 128), f32)], axis=1)
        row = jnp.where(lane < width, jnp.broadcast_to(row, (8, full)), 0.0)
        out += pltpu.roll(row, k * width, 1) if k else row
    return out[0:1]


def whole_shares(place, scal, refs, at, size, full, halves):
    if not halves:
        return [x.at[at : at + size] for x in refs]
    half = size // 2
    for s in range(place.n_ctx):
        full[s, pl.ds(pl.multiple_of(scal[7] * half, half), half)] = refs[s][at : at + half]
        start = s * half
        full[s, pl.ds(pl.multiple_of((1 - scal[7]) * half, half), half)] = refs[-1][start : start + half]
    return [full.at[s] for s in range(place.n_ctx)]


def place_mlp(place, scalars, shares, layer, into):
    n_ctx, units = place.n_ctx, place.units
    taken = 0 if into is None else 2
    halves = len(shares) > n_ctx
    size = place.mixed_rows if layer == 0 else 0
    rows = 2 * units + 32 + 2 * size

    def kernel(scal, *refs):
        up_out, down_out, small_out, *out_outs, up_t, bias_rows, full = refs[len(shares) + taken :]
        ordered = len(shares) == 1
        if ordered:
            srcs = [refs[0].at[c * rows : (c + 1) * rows] for c in range(n_ctx)]
        else:
            srcs = whole_shares(place, scal, refs[: len(shares)], 0, rows, full, halves)
        for s in range(n_ctx):
            c = s if ordered else lax.rem(scal[0] - s + n_ctx, n_ctx)
            at = pl.multiple_of(c * units, units)
            up_t[pl.ds(at, units)] = srcs[s][0:units].astype(f32)
            extra = srcs[s][units : units + 16].astype(f32)
            extra = extra[0:8] + extra[8:16]
            bias_rows[c] = jnp.broadcast_to(extra[0:1, :128], (8, 128))
            if s == 0:
                small_out[...] = jnp.zeros_like(small_out)
                for q in range(place.n_head):

                    @pl.when(scal[1] == q)
                    def _():
                        small_out[1:2, 0:128] = extra[1:2, 128 * q : 128 * q + 128]

            for p in range(place.n_head):
                at = pl.multiple_of(p * (FF // place.n_head) + c * units, units)
                base = units + 32
                down_out[pl.ds(at, units)] = srcs[s][base : base + units, 128 * p : 128 * p + 128].astype(f32)
                at = pl.multiple_of(p * 128 + c * place.mixed_rows, place.mixed_rows)
                for k in range(2 if size else 0):
                    start = base + units + k * size
                    out_outs[0][k, pl.ds(at, size)] = srcs[s][start : start + size, 128 * p : 128 * p + 128].astype(f32)
        up_out[...] = up_t[...].T
        small_out[0:1] = along_lanes([bias_rows[c][0:1] for c in range(n_ctx)], units)

    wide = FF // place.n_head
    return call(
        kernel,
        shares,
        [
            (sds((LAYERS, D, wide), f32), layer),
            (sds((LAYERS, FF, 128), f32), layer),
            sds((8, wide), f32),
            *([sds((LAYERS, D, 128), f32)] if size else []),
        ],
        [VMEM((wide, D), f32), VMEM((n_ctx, 8, 128), f32), VMEM((n_ctx, rows, D) if halves else (1, 16, D), bf16)],
        scalars,
        flops=10**7,
        into=into,
    )


def place_attention(place, scalars, shares, layer, into, smalls=None, count=1):
    n_ctx, part = place.n_ctx, place.packed_rows
    taken = 0 if into is None else 1
    wide = 3 * D // place.n_head
    wide_up = FF // place.n_head
    given = [] if smalls is None else smalls

    def kernel(scal, *refs):
        shares_in, given_in = refs[: len(shares)], refs[len(shares) : len(shares) + len(given)]
        qkv_out, *small_outs, qkv_t, info, small = refs[len(shares) + len(given) + taken :]
        small[...] = jnp.zeros_like(small)
        for s in range(n_ctx):
            c = lax.rem(scal[0] - s + n_ctx, n_ctx)
            at = pl.multiple_of(c * part, part)
            qkv_t[pl.ds(at, part)] = shares_in[s][0:part].astype(f32)
            extra = shares_in[s][part : part + 16].astype(f32)
            extra = extra[0:8] + extra[8:16]
            info[c] = extra
            if s == 0:
                for k in range(4):
                    small[k : k + 1, 0:128] = extra[0:1, 128 * k : 128 * k + 128]
                small[4:5, 0:128] = extra[1:2, 128:256]
        qkv_out[...] = qkv_t[...].T
        small[5:6] = along_lanes([info[c, 1:2, 0:128] for c in range(n_ctx)], part)
        if smalls is None:
            small_outs[0][...] = small[...]
            return
        attn_1, mlp_0, mlp_1 = given_in
        lane = lane_of(1)
        for spot, attn, mlp in ((0, small, mlp_0), (1, attn_1, mlp_1)):
            row = slice(spot, spot + 1)
            for k in range(4):
                small_outs[k][row] = attn[k : k + 1, 0:128]
            small_outs[4][row] = attn[5:6]
            small_outs[5][row] = mlp[0:1]
            small_outs[6][row] = mlp[1:2, 0:128]
            small_outs[7][row] = mlp[1:2, 0:128]
            for k in range(3):
                picked = jnp.where((lane & 3) == k, attn[4:5, 0:128], 0.0)
                small_outs[8][row, k : k + 1] = jnp.sqrt(jnp.sum(picked, axis=1, keepdims=True) * (1.0 / count))

    if smalls is None:
        outs = [sds((8, wide), f32)]
    else:
        widths = [128, 128, 128, 128, wide, wide_up, 128, 128, 3]
        outs = [sds((LAYERS, width), f32) for width in widths]
    return call(
        kernel,
        [*shares, *given],
        [(sds((LAYERS, D, wide), f32), layer), *outs],
        [
            VMEM((wide, D), f32),
            VMEM((n_ctx, 8, D), f32),
            VMEM((8, wide), f32),
        ],
        scalars,
        flops=10**7,
        into=into,
    )


def prepare(place, lengths, qkv_weight, qkv_bias):
    group = place.group
    blocks = group // 128
    dim = jnp.arange(128, dtype=jnp.int32)[None, :] % HD
    freq = rope_base ** (-2.0 * (dim % (ROT // 2)).astype(f32) / ROT)
    starts = jnp.concatenate([jnp.zeros((1,), jnp.int32), lengths[0, :3]])
    starts = jnp.stack([starts[0], starts[1], starts[1] + starts[2], starts[1] + starts[2] + starts[3]])
    first = (jnp.arange(blocks, dtype=jnp.int32)[:, None] * 128 - starts[None, :]).reshape(-1, 1)
    whole = jnp.concatenate([first, jnp.arange(128, dtype=jnp.int32)[:, None]], axis=0).astype(f32) * freq
    cosines, sines = jnp.cos(whole), jnp.sin(whole)
    base = 4 * blocks

    def kernel(scal, w_ref, b_ref, cos_ref, sin_ref, w_out, b_out, cos_t, left_t, right_t, own_t):
        def sort(read, write):
            for p in range(PAIRS):
                a, b, c = (read(slice(128 * (3 * p + i), 128 * (3 * p + i) + 128)).astype(f32) for i in range(3))
                first = lane_of(a.shape[0]) < HD
                made = (jnp.where(first, a, b), pltpu.roll(jnp.where(first, c, a), HD, 1), jnp.where(first, b, c))
                for j in range(3):
                    write(slice(j * D + 128 * p, j * D + 128 * p + 128), made[j])

        for layer in range(LAYERS):

            def store(to, x, layer=layer):
                w_out[layer, :, to] = x.astype(bf16)

            sort(lambda at, layer=layer: w_ref[layer, :, at], store)

        def store_bias(to, x):
            b_out[:, to] = x

        sort(lambda at: b_ref[:, at], store_bias)
        ends = place.ends(scal)
        dim = lane_of(128) & (HD - 1)
        cos_b, sin_b = cos_ref[base : base + 128], sin_ref[base : base + 128]

        def table(i, _):
            at = pl.multiple_of(i * 128, 128)
            t = at + lax.broadcasted_iota(jnp.int32, (128, 1), 0)
            cos_a, sin_a = cos_ref[pl.ds(4 * i, 1)], sin_ref[pl.ds(4 * i, 1)]
            for k in range(1, 4):
                later = t >= ends[k - 1]
                cos_a = jnp.where(later, cos_ref[pl.ds(4 * i + k, 1)], cos_a)
                sin_a = jnp.where(later, sin_ref[pl.ds(4 * i + k, 1)], sin_a)
            cosine = cos_a * cos_b - sin_a * sin_b
            sine = sin_a * cos_b + cos_a * sin_b
            cos_t[pl.ds(at, 128)] = jnp.where(dim < ROT, cosine, 1.0)
            left_t[pl.ds(at, 128)] = jnp.where(dim < ROT // 2, -sine, 0.0)
            right_t[pl.ds(at, 128)] = jnp.where((dim >= ROT // 2) & (dim < ROT), sine, 0.0)
            return 0

        lax.fori_loop(0, blocks, table, 0)
        own_at = pl.multiple_of(scal[2] * place.rows, place.rows)
        for k, ref in enumerate((cos_t, left_t, right_t)):
            own_t[k * place.rows : (k + 1) * place.rows] = ref[pl.ds(own_at, place.rows)]

    bias = jnp.concatenate([qkv_bias, jnp.zeros((8 - LAYERS, 3 * D), f32)], axis=0)
    made = call(
        kernel,
        [qkv_weight, bias, cosines, sines],
        [sds(qkv_weight.shape, bf16), sds((8, 3 * D), f32), *[sds((group, 128), f32)] * 3, sds((3 * place.rows, 128), f32)],
        (),
        lengths,
        flops=10**7,
    )
    return made[0], made[1], made[2:5], made[5]


def tie(x, *after):
    return lax.optimization_barrier((x, *after))[0] if after else x


def flip_heads(x, flip):
    return lax.ppermute(x, "head", [(i, i ^ flip) for i in range(lax.axis_size("head"))])


def turn_ctx(x, shift):
    n = lax.axis_size("ctx")
    return lax.ppermute(x, "ctx", [(i, (i + shift) % n) for i in range(n)])


def gather_rings(own):
    return [own] + [turn_ctx(own, s) for s in range(1, lax.axis_size("ctx"))]


def gather_flips(rings, flip, *after):
    return [flip_heads(tie(x, *after), flip) for x in rings]


def by_slot(rings, far, near, far_near):
    return [x for four in zip(rings, near, far, far_near) for x in four]


def with_flip(own, flip):
    return jnp.concatenate([own, flip_heads(own, flip)], axis=0)


def swap_dp(x):
    return lax.ppermute(x, "dp", [(0, 1), (1, 0)])


def per_device(
    hidden_in,
    lengths,
    attn_gain,
    attn_shift,
    mlp_gain,
    mlp_shift,
    qkv_weight,
    qkv_bias,
    out_weight,
    out_bias,
    up_weight,
    up_bias,
    down_weight,
    down_bias,
    cotangent,
):
    rows = hidden_in.shape[0]
    n_dp, n_ctx, n_head = (lax.axis_size(a) for a in ("dp", "ctx", "head"))
    place = Place(n_dp, n_ctx, n_head, rows)
    group = place.group
    scalars = lengths
    qkv_sorted, qkv_bias_sorted, tables, own_tables = prepare(place, lengths, qkv_weight, qkv_bias)
    params = {
        "attn_gain": attn_gain,
        "attn_shift": attn_shift,
        "mlp_gain": mlp_gain,
        "mlp_shift": mlp_shift,
        "qkv_sorted": qkv_sorted,
        "qkv_bias_sorted": qkv_bias_sorted,
        "out_weight": out_weight,
        "out_bias": out_bias,
        "up_weight": up_weight,
        "up_bias": up_bias,
        "down_weight": down_weight,
        "down_bias": down_bias,
    }
    def attention(layer, blocks, hidden, mlp_out, last_grad):
        names = ("normal_all", "k_all", "v_all", "q_own", "kv_own", "mixed", "mixed_low", "log", "delta", "dmix", "h_out", "stats", "low")
        made = attention_forward(place, scalars, blocks, tables, params, layer, hidden, mlp_out, last_grad)
        return dict(zip(names, made), hidden=hidden)

    def backward_queries(layer, kept):
        return query_backward(place, scalars, tables, own_tables, params, layer, kept)

    def backward_keys(layer, g_all, stats, kept, queries, grad, grad_mlp_in, below):
        return key_backward(
            place, scalars, g_all, stats, own_tables, params, layer, kept, queries, grad, grad_mlp_in, below
        )

    def head_swap(pieces):
        return lax.all_to_all(pieces, "head", 0, 0, tiled=True)

    def group_swap(pieces):
        return lax.all_to_all(pieces, ("ctx", "head"), 0, 0, tiled=True)

    def reduce_mlp(up_share, pieces, halves):
        made = pack_mlp(place, scalars, up_share, pieces, halves)
        if n_dp == 2:
            return (made[0].astype(f32) + swap_dp(made[-1]).astype(f32)).astype(bf16)
        return lax.psum(made[0], "dp")

    def sum_dp(x):
        if n_dp == 2:
            return (x.astype(f32) + swap_dp(x).astype(f32)).astype(bf16)
        return lax.psum(x, "dp")

    def finish(rings):
        return [*rings, swap_dp(jnp.concatenate(rings, axis=0))] if n_dp == 2 else rings

    together = lax.optimization_barrier

    mlp_0, factor_0, _ = mlp_forward(hidden_in, params, 0)
    rings, mlp_0, factor_0 = together((gather_rings(hidden_in), mlp_0, factor_0))
    far = gather_flips(rings, 2)
    far, rings, params["qkv_sorted"], tables, own_tables = together((far, rings, qkv_sorted, tables, own_tables))
    near, far_near = together((gather_flips(rings, 1), gather_flips(far, 1)))
    first, cot_rings = together(
        (attention(0, by_slot(rings, far, near, far_near), hidden_in, mlp_0, None), gather_rings(tie(cotangent, near)))
    )
    hidden, low = first["h_out"], first["low"]
    units = place.units
    at = lax.axis_index("head") * (FF // n_head) + lax.axis_index("ctx") * units
    params["units"] = [
        (
            lax.dynamic_slice(tie(up_weight, first["low"]), (layer, 0, at), (1, D, units))[0],
            lax.dynamic_slice(tie(up_bias, first["low"]), (layer, at), (1, units)),
            lax.dynamic_slice(tie(down_weight, first["low"]), (layer, at, 0), (1, units, D))[0],
        )
        for layer in range(LAYERS)
    ]
    mlp_1, back_1 = mlp_both(hidden, cotangent, params, 1)
    rings, mlp_1, back_1 = together((gather_rings(low), mlp_1, back_1))
    far, rings, params["units"] = together((gather_flips(rings, 2), rings, params["units"]))
    near, far_near = together((gather_flips(rings, 1), gather_flips(far, 1)))
    second = attention(1, by_slot(rings, far, near, far_near), hidden, mlp_1, [cotangent, first["mixed_low"]])
    second, cot_far, cot_rings = together((second, gather_flips(cot_rings, 2, near), cot_rings))
    output_rows, low = second["h_out"], second["low"]

    pair, cot_near, cot_far_near = together((with_flip(low, 1), gather_flips(cot_rings, 1), gather_flips(cot_far, 1)))
    made = mlp_weight_grads(
        place, scalars, by_slot(cot_rings, cot_far, cot_near, cot_far_near), second["normal_all"], params, 1
    )
    (cot_all, up_share_1, pieces_1), four = together((made, with_flip(pair, 2)))
    queries_1, stats = together((backward_queries(1, second), gather_rings(four)))
    made = backward_keys(1, cot_all, stats, second, queries_1, cotangent, back_1, first)
    packed_1, grad, payload, dmix, delta = made
    first["dmix"], first["delta"] = dmix, delta
    back_0 = mlp_backward(grad, factor_0, hidden_in, params, 0)
    rings, back_0, pieces_1 = together((gather_rings(payload), back_0, head_swap(tie(pieces_1, payload))))
    received_1 = group_swap(tie(packed_1, back_0))
    far, rings, queries_0 = together(
        (gather_flips(rings, 2), rings, backward_queries(0, dict(first, delta=tie(delta, back_0))))
    )
    half_1 = reduce_mlp(tie(up_share_1, far), pieces_1, n_dp == 2)
    near, far_near = together((gather_flips(rings, 1), gather_flips(far, 1)))
    blocks = by_slot(rings, far, near, far_near)
    mlp_rings_1 = gather_rings(tie(half_1, near))
    g_all, up_share_0, pieces_0 = mlp_weight_grads(
        place, scalars, blocks, first["normal_all"], params, 0, [received_1, cot_all]
    )
    made = backward_keys(0, g_all, blocks, first, queries_0, grad, back_0, None)
    (packed_0, grad, _, _, _), pieces_0, mlp_rings_1, up_share_0, received_1 = together(
        (made, head_swap(pieces_0), mlp_rings_1, up_share_0, received_1)
    )
    half_0 = reduce_mlp(up_share_0, pieces_0, n_dp == 2)
    mlp_rings_0 = gather_rings(half_0)
    share_1 = attention_weight_grads(place, scalars, tie(received_1, half_0), second["normal_all"], params, 1)
    sum_1 = sum_dp(share_1)
    received_0, sum_1, mlp_rings_0, mlp_shares_1 = together(
        (group_swap(packed_0), sum_1, mlp_rings_0, finish([tie(x, half_0) for x in mlp_rings_1]))
    )
    share_0 = attention_weight_grads(place, scalars, received_0, first["normal_all"], params, 0)
    *big, mlp_small_1 = place_mlp(place, scalars, [tie(mlp_shares_1[0], share_0), *mlp_shares_1[1:]], 1, None)
    other_0 = swap_dp(share_0) if n_dp == 2 else lax.psum(share_0, "dp")
    attn_rings_1 = gather_rings(tie(sum_1, share_0))
    mlp_shares_0 = finish([tie(x, other_0) for x in mlp_rings_0])
    other_0, attn_rings_1 = together((other_0, attn_rings_1))
    sum_0 = (share_0.astype(f32) + other_0.astype(f32)).astype(bf16) if n_dp == 2 else other_0
    sum_0, big, mlp_small_1 = together((sum_0, big, mlp_small_1))
    *attn_big, attn_small_1 = place_attention(place, scalars, attn_rings_1, 1, None)
    up_grad, down_grad, mlp_small_0, out_grad = place_mlp(place, scalars, mlp_shares_0, 0, big)
    attn_rings_0, mlp_small_0, attn_big, attn_small_1 = together(
        (gather_rings(sum_0), mlp_small_0, attn_big, attn_small_1)
    )
    qkv_grad, gain, shift, mlp_g, mlp_s, qkv_b, up_b, down_b, out_b, layer_stats = place_attention(
        place, scalars, attn_rings_0, 0, attn_big, [attn_small_1, mlp_small_0, mlp_small_1], group * n_dp * D
    )
    return (
        output_rows, grad, gain, shift, mlp_g, mlp_s, qkv_grad, qkv_b, out_grad, out_b, up_grad, up_b, down_grad, down_b, layer_stats
    )


def solution(mesh):
    rows = P(("dp", "ctx", "head"), None)
    return jax.shard_map(
        per_device,
        mesh=mesh,
        in_specs=(rows, P("dp", None), *([P()] * 12), rows),
        out_specs=(
            rows,
            rows,
            P(None, "head"),
            P(None, "head"),
            P(None, "head"),
            P(None, "head"),
            P(None, None, "head"),
            P(None, "head"),
            P(None, None, "head"),
            P(None, "head"),
            P(None, None, "head"),
            P(None, "head"),
            P(None, None, "head"),
            P(None, "head"),
            P(),
        ),
        check_vma=False,
    )
```
